256 devices in a mesh: gx: 4 (over x), gy: 8 (over y, core), gz: 8 (over z).
Axes of the slice: x: 4, y: 4, z: 8, core: 2. Of those that a mesh axis runs over, the one named last changes fastest.
Arguments:
- right_side: float32 [64, 256, 1024], P('gx', 'gy', 'gz'), may hold values from -8 to 8
- coeff_cells: float32 [64, 256, 1024], P('gx', 'gy', 'gz'), may hold values from 0.5 to 4
Outputs:
- solution: float32 [64, 256, 1024], P('gx', 'gy', 'gz')
The draws below stay inside these ranges and needn't reach their ends.
All inputs are finite; a program needn't handle non-finite values.
Results may differ from the reference program's by a relative error of at most 0.0001.
Values sent between devices are 32-bit elements; how exact they have to be, the bound alone decides.
No kernel may reach another device: no remote copies, remote signals or barrier semaphores. Data moves between devices by JAX's collectives and lax.ppermute only.
A program may use at most 128 MiB of HBM per device.

```python
import math
import jax
import jax.numpy as jnp

LEVELS = 3
SWEEPS = 4
BOTTOM = 8
NX = 64
NY = 256
NZ = 1024


def draw_right_side(key, part):
    key = jax.random.fold_in(key, 7)
    rough_key, mode_key, phase_key = jax.random.split(key, 3)
    pos_first = (jnp.arange(NX, dtype=jnp.float32)[:, None, None] + 0.5) / NX
    pos_second = (jnp.arange(NY, dtype=jnp.float32)[None, :, None] + 0.5) / NY
    pos_third = (jnp.arange(NZ, dtype=jnp.float32)[None, None, :] + 0.5) / NZ
    modes = jax.random.randint(mode_key, (3,), 1, 4).astype(jnp.float32)
    phases = jax.random.uniform(phase_key, (3,), jnp.float32, 0.0, 2.0 * math.pi)
    wave = jnp.sin(math.pi * modes[0] * pos_first + phases[0])
    wave = wave * jnp.sin(math.pi * modes[1] * pos_second + phases[1])
    wave = wave * jnp.sin(math.pi * modes[2] * pos_third + phases[2])
    rough = jax.random.normal(rough_key, (NX, NY, NZ), jnp.float32)
    values = rough + 0.6 * wave
    return jnp.clip(values, -8.0, 8.0).astype(jnp.float32)


def steps_of(own_key, extent, cuts, least, largest):
    loudness, own = 1.0, jax.random.fold_in(own_key, 6)
    for axis_at, shards_of in cuts:
        heights = jnp.exp(jax.random.uniform(jax.random.fold_in(own, axis_at), (shards_of,), jnp.float32, least / len(cuts), largest / len(cuts)))
        loudness = loudness * jnp.repeat(heights, extent[axis_at] // shards_of).reshape([-1 if axis == axis_at else 1 for axis in range(len(extent))])
    return loudness


def setup_inputs(seed: int = 0) -> dict:
    splits = jax.random.split(jax.random.key(seed), 3)
    return {
        "right_side": draw_right_side(jax.random.fold_in(splits[2], 71), 0),
        "coeff_cells": jnp.clip(jnp.exp(math.log(4.0) - 2.0794415 * jax.random.uniform(splits[1], (NX, NY, NZ), jnp.float32) ** steps_of(splits[1], (NX, NY, NZ), ((0, 4), (1, 8), (2, 8)), -0.2, 0.2)), 0.5, 4.0),
    }


cheby_top = 2.0
smooth_low = 0.25
bottom_low = 0.02


def chebyshev_terms(lower_bound, sweeps):
    middle = (cheby_top + lower_bound) / 2.0
    radius = (cheby_top - lower_bound) / 2.0
    sigma_ratio = middle / radius
    rho_old = 1.0 / sigma_ratio
    term_list = []
    for sweep_index in range(1, sweeps):
        rho_new = 1.0 / (2.0 * sigma_ratio - rho_old)
        term_list.append((rho_new * rho_old, 2.0 * rho_new / radius))
        rho_old = rho_new
    return 1.0 / middle, term_list


def face_weights(beta_pad):
    face_first = 0.5 * (beta_pad[:-1, 1:-1, 1:-1] + beta_pad[1:, 1:-1, 1:-1])
    face_second = 0.5 * (beta_pad[1:-1, :-1, 1:-1] + beta_pad[1:-1, 1:, 1:-1])
    face_third = 0.5 * (beta_pad[1:-1, 1:-1, :-1] + beta_pad[1:-1, 1:-1, 1:])
    return face_first, face_second, face_third


def diagonal_sum(face_list):
    face_first, face_second, face_third = face_list
    running = face_first[:-1] + face_first[1:] + face_second[:, :-1] + face_second[:, 1:]
    return running + face_third[:, :, :-1] + face_third[:, :, 1:]


def apply_operator(padded, face_list, level_scale):
    face_first, face_second, face_third = face_list
    centre = padded[1:-1, 1:-1, 1:-1]
    running = face_first[:-1] * (centre - padded[:-2, 1:-1, 1:-1])
    running = running + face_first[1:] * (centre - padded[2:, 1:-1, 1:-1])
    running = running + face_second[:, :-1] * (centre - padded[1:-1, :-2, 1:-1])
    running = running + face_second[:, 1:] * (centre - padded[1:-1, 2:, 1:-1])
    running = running + face_third[:, :, :-1] * (centre - padded[1:-1, 1:-1, :-2])
    running = running + face_third[:, :, 1:] * (centre - padded[1:-1, 1:-1, 2:])
    return level_scale * running


def zero_pad(values):
    return jnp.pad(values, 1)


def smooth(source, face_list, inverse_diag, level_scale, lower_bound, sweeps, pad_field, with_residual):
    initial, term_list = chebyshev_terms(lower_bound, sweeps)
    step_dir = (inverse_diag * source) * initial
    iterate = step_dir
    for carry_part, push_part in term_list:
        remainder = source - apply_operator(pad_field(iterate), face_list, level_scale)
        step_dir = carry_part * step_dir + push_part * (inverse_diag * remainder)
        iterate = iterate + step_dir
    if with_residual:
        return iterate, source - apply_operator(pad_field(iterate), face_list, level_scale)
    return iterate, source


def restrict(values):
    first, second, third = values.shape
    blocks = values.reshape(first // 2, 2, second // 2, 2, third // 2, 2)
    return jnp.mean(blocks, axis=(1, 3, 5))


def prolong(values):
    return jnp.repeat(jnp.repeat(jnp.repeat(values, 2, axis=0), 2, axis=1), 2, axis=2)


def reference(right_side, coeff_cells):
    source = right_side
    beta_cells = coeff_cells
    saved = []
    for depth_level in range(LEVELS):
        level_scale = 0.25 ** depth_level
        face_list = face_weights(zero_pad(beta_cells))
        inverse_diag = 1.0 / (level_scale * diagonal_sum(face_list))
        iterate, remainder = smooth(source, face_list, inverse_diag, level_scale, smooth_low, SWEEPS, zero_pad, True)
        saved.append(iterate)
        source = restrict(remainder)
        beta_cells = restrict(beta_cells)
    level_scale = 0.25 ** LEVELS
    face_list = face_weights(zero_pad(beta_cells))
    inverse_diag = 1.0 / (level_scale * diagonal_sum(face_list))
    correction, unused = smooth(source, face_list, inverse_diag, level_scale, bottom_low, BOTTOM, zero_pad, False)
    for iterate in reversed(saved):
        correction = iterate + prolong(correction)
    return correction
```

```python
import jax
import jax.numpy as jnp
from jax import lax
from jax.experimental import pallas as pl
from jax.experimental.pallas import tpu as pltpu
from jax.sharding import PartitionSpec as P

LEVELS = 3
SWEEPS = 4
BOTTOM = 8

cheby_top = 2.0
smooth_low = 0.25
bottom_low = 0.02

F32 = jnp.float32


def chebyshev_terms(lower_bound, sweeps):
    middle = (cheby_top + lower_bound) / 2.0
    radius = (cheby_top - lower_bound) / 2.0
    sigma_ratio = middle / radius
    rho_old = 1.0 / sigma_ratio
    term_list = []
    for sweep_index in range(1, sweeps):
        rho_new = 1.0 / (2.0 * sigma_ratio - rho_old)
        term_list.append((rho_new * rho_old, 2.0 * rho_new / radius))
        rho_old = rho_new
    return (1.0 / middle, term_list)


def ring(values, axis, step):
    count = lax.axis_size(axis)
    return lax.ppermute(values, axis, [(i, (i + step) % count) for i in range(count)])


def minus(v, axis):
    return pltpu.roll(v, 1, axis)


def plus(v, axis):
    return pltpu.roll(v, v.shape[axis] - 1, axis)


def iota(shape, axis):
    return lax.broadcasted_iota(jnp.int32, shape, axis)


def matrix(shape, hit, value):
    return jnp.where(hit(iota(shape, 0), iota(shape, 1)), F32(value), F32(0.0))


def product(left, right):
    return jnp.dot(left, right, precision=lax.Precision.HIGHEST, preferred_element_type=F32)


def weigh(bm, bc, bp, row_low=None, row_high=None):
    by_m, by_p = minus(bc, 0), plus(bc, 0)
    bz_m, bz_p = minus(bc, 1), plus(bc, 1)
    if row_low is not None:
        by_m, by_p = by_m * row_low, by_p * row_high
    double = 6.0 * bc + ((bm + bp) + (by_m + by_p) + (bz_m + bz_p))
    inverse = jnp.where(bc > 0.0, 1.0 / double, 0.0)
    faces = [(bc + n) * inverse for n in (bm, bp, by_m, by_p, bz_m, bz_p)]
    if row_low is not None:
        faces[2] = faces[2] * row_low
        faces[3] = faces[3] * row_high
    return faces, inverse, double


def scaled_residual(v, i, at, w, gh):
    c = v[i + at]
    z = gh[i] - c
    z = z + w[0, i] * v[i + at - 1] + w[1, i] * v[i + at + 1]
    z = z + w[2, i] * minus(c, 0) + w[3, i] * plus(c, 0)
    z = z + w[4, i] * minus(c, 1) + w[5, i] * plus(c, 1)
    return c, z


def smooth(va, vb, d, w, gh, at, low, high, shrink, terms):
    src, dst = va, vb
    for k, (carry, push) in enumerate(terms):
        low, high = low + shrink, high - shrink

        def body(i, _, src=src, dst=dst, first=k == 0, last=k == len(terms) - 1):
            c, z = scaled_residual(src, i, at, w, gh)
            step = carry * (c if first else d[i]) + push * z
            if not last:
                d[i] = step
            dst[i + at] = c + step
            return 0

        lax.fori_loop(low, high, body, 0)
        src, dst = dst, src
    return src


def plane_of(p, g, b, xl, xh):
    if p < 4:
        return xl[p]
    if p < 20:
        return g[p - 4]
    if p < 24:
        return xh[p - 20]
    if p < 29:
        return xl[p - 20]
    if p < 45:
        return b[p - 29]
    return xh[p - 41]


def rows_of(p, g, b, xl, xh, yl, yh):
    return jnp.concatenate([yl[p], plane_of(p, g, b, xl, xh), yh[p]], axis=0)


def pack_kernel(g, b, xl, xh, yl, yh, high, low):
    slot = iota((64, 128), 1) // 16
    for k in range(7):
        to_high = jnp.zeros((64, 128), F32)
        to_low = jnp.zeros((64, 128), F32)
        for s in range(8):
            p = 8 * k + s
            if p >= 50:
                break
            plane = rows_of(p, g, b, xl, xh, yl, yh)
            to_high = jnp.where(slot == s, pltpu.roll(plane, 16 * (s + 1) % 128, 1), to_high)
            to_low = jnp.where(slot == s, pltpu.roll(plane, 16 * s, 1) if s else plane, to_low)
        high[k] = to_high
        low[k] = to_low


def level0_kernel(g, b, xl, xh, yl, yh, zl, zh, x0, g1, b1, G, B, W, GH, D2, VA, VB, DD, T):
    gx, gy, gz = lax.axis_index("gx"), lax.axis_index("gy"), lax.axis_index("gz")
    rows = iota((64, 128), 0)
    lanes = iota((64, 128), 1)
    row_in = jnp.where(
        ((rows >= 16) | (gy > 0)) & ((rows < 48) | (gy < 7)), F32(1.0), F32(0.0)
    )
    lane_in = jnp.where(
        ((lanes < 16) & (gz < 7)) | ((lanes >= 112) & (gz > 0)), row_in, F32(0.0)
    )
    left_in = jnp.where(gx > 0, F32(1.0), F32(0.0))
    right_in = jnp.where(gx < 3, F32(1.0), F32(0.0))
    for p in range(50):
        k, s = p // 8, p % 8
        near = rows_of(p, g, b, xl, xh, yl, yh)
        from_high = zh[k]
        from_high = pltpu.roll(from_high, 128 - 16 * s, 1) if s else from_high
        from_low = zl[k]
        from_low = pltpu.roll(from_low, 112 - 16 * s, 1) if s < 7 else from_low
        far = jnp.where(lanes < 16, from_high, from_low)
        if p < 24:
            G[p, :, 0:128] = near
            G[p, :, 128:256] = far
        else:
            q = p - 24
            near, far = near * row_in, far * lane_in
            if q < 5:
                near, far = near * left_in, far * left_in
            if q >= 21:
                near, far = near * right_in, far * right_in
            B[q, :, 0:128] = near
            B[q, :, 128:256] = far

    initial, terms = chebyshev_terms(smooth_low, SWEEPS)

    def prepare(i, _):
        faces, inverse, double = weigh(B[i], B[i + 1], B[i + 2])
        for f in range(6):
            W[f, i] = faces[f]
        gh = G[i] * (2.0 * inverse)
        GH[i] = gh
        VA[i] = gh * initial
        D2[i] = double
        return 0

    lax.fori_loop(0, 24, prepare, 0)
    v = smooth(VA, VB, DD, W, GH, 0, 0, 24, 1, terms)
    x0[...] = v[4:20, 16:48, 0:128]

    def restrict(j, _):
        i = 4 + 2 * j
        r = (0.5 * D2[i]) * scaled_residual(v, i, 0, W, GH)[1]
        r = r + (0.5 * D2[i + 1]) * scaled_residual(v, i + 1, 0, W, GH)[1]
        T[0, j] = r[:, 0:128]
        T[1, j] = r[:, 128:256]
        c = B[5 + 2 * j] + B[6 + 2 * j]
        T[2, j] = c[:, 0:128]
        T[3, j] = c[:, 128:256]
        return 0

    lax.fori_loop(0, 8, restrict, 0)
    near_mat = matrix((128, 128), lambda a, c: a // 2 == c, 0.125)
    far_mat = matrix((128, 128), lambda a, c: a // 2 + 64 == c, 0.125)
    for out, at in ((g1, 0), (b1, 2)):
        sums = []
        for half in range(2):
            even = T[at + half, :, pl.ds(0, 32, stride=2), :]
            odd = T[at + half, :, pl.ds(1, 32, stride=2), :]
            sums.append((even + odd).reshape(256, 128))
        total = product(sums[0], near_mat) + product(sums[1], far_mat)
        out[...] = total.reshape(8, 32, 128)


def level1_kernel(g, b, xl, xh, x1, chunk, G, B, W, GH, D2, VA, VB, DD, T):
    gx = lax.axis_index("gx")
    left_in = jnp.where(gx > 0, F32(1.0), F32(0.0))
    right_in = jnp.where(gx < 3, F32(1.0), F32(0.0))
    G[0:4] = xl[0:4]
    G[4:12] = g[...]
    G[12:16] = xh[0:4]
    B[0:5] = xl[4:9] * left_in
    B[5:13] = b[...]
    B[13:18] = xh[4:9] * right_in
    initial, terms = chebyshev_terms(smooth_low, SWEEPS)
    scale = 0.25

    def prepare(i, _):
        faces, inverse, double = weigh(B[i], B[i + 1], B[i + 2])
        for f in range(6):
            W[f, i] = faces[f]
        gh = G[i] * ((2.0 / scale) * inverse)
        GH[i] = gh
        VA[i] = gh * initial
        D2[i] = double
        return 0

    lax.fori_loop(0, 16, prepare, 0)
    v = smooth(VA, VB, DD, W, GH, 0, 0, 16, 1, terms)
    x1[...] = v[4:12, 8:24, :]

    def restrict(j, _):
        i = 4 + 2 * j
        r = (0.5 * scale * D2[i]) * scaled_residual(v, i, 0, W, GH)[1]
        r = r + (0.5 * scale * D2[i + 1]) * scaled_residual(v, i + 1, 0, W, GH)[1]
        T[0, j] = r
        T[1, j] = B[5 + 2 * j] + B[6 + 2 * j]
        return 0

    lax.fori_loop(0, 4, restrict, 0)
    for a in range(2):
        total = jnp.zeros((8, 128), F32)
        for q in range(4):
            mat = matrix(
                (128, 128), lambda i, o, q=q: (i < 64) & (i // 2 + 32 * q == o), 0.125
            )
            even = T[a, q, pl.ds(8, 8, stride=2), :]
            odd = T[a, q, pl.ds(9, 8, stride=2), :]
            total = total + product(even + odd, mat)
        chunk[a] = total


def finish_kernel(
    recv, x0, x1, out, G, B, W, GH, D2, VA, VB, DD, T, G3, B3, W3, VA3, VB3, DD3, GH3, X3, E1, E0
):
    gx, gy, gz = lax.axis_index("gx"), lax.axis_index("gy"), lax.axis_index("gz")
    lanes = iota((8, 128), 1)
    ones = jnp.ones((8, 128), F32)
    zeros = jnp.zeros((8, 128), F32)
    lane_in = jnp.where(
        lanes < 32, ones, jnp.where(lanes < 64, jnp.where(gz < 7, ones, zeros), zeros)
    )
    lane_in = jnp.where(lanes >= 96, jnp.where(gz > 0, ones, zeros), lane_in)

    def turn(v, s):
        s = s % 128
        return pltpu.roll(v, s, 1) if s else v

    B[0] = jnp.zeros((64, 128), F32)
    B[17] = jnp.zeros((64, 128), F32)
    VA[0] = jnp.zeros((64, 128), F32)
    VA[17] = jnp.zeros((64, 128), F32)
    VB[0] = jnp.zeros((64, 128), F32)
    VB[17] = jnp.zeros((64, 128), F32)
    for j in range(32):
        row = slice(8 * (j % 8), 8 * (j % 8) + 8)
        for q in range(4):
            plane = 4 * (j // 8) + q
            for a in range(2):
                own, left, right = recv[j, a], recv[j, 2 + a], recv[j, 4 + a]
                got = jnp.where(
                    lanes < 32,
                    turn(own, -32 * q),
                    jnp.where(lanes < 64, turn(right, 32 - 32 * q), turn(left, 96 - 32 * q)),
                )
                if a == 0:
                    G[plane, row, :] = got
                else:
                    B[plane + 1, row, :] = got * lane_in
    initial, terms = chebyshev_terms(smooth_low, SWEEPS)
    scale = 0.25**2
    rows = iota((64, 128), 0)
    row_low = jnp.where(rows > 0, F32(1.0), F32(0.0))
    row_high = jnp.where(rows < 63, F32(1.0), F32(0.0))

    def prepare(i, _):
        faces, inverse, double = weigh(B[i], B[i + 1], B[i + 2], row_low, row_high)
        for f in range(6):
            W[f, i] = faces[f]
        gh = G[i] * ((2.0 / scale) * inverse)
        GH[i] = gh
        VA[i + 1] = gh * initial
        D2[i] = double
        return 0

    lax.fori_loop(0, 16, prepare, 0)
    v = smooth(VA, VB, DD, W, GH, 1, 0, 16, 0, terms)

    def restrict(j, _):
        i = 2 * j
        r = (0.5 * scale * D2[i]) * scaled_residual(v, i, 1, W, GH)[1]
        r = r + (0.5 * scale * D2[i + 1]) * scaled_residual(v, i + 1, 1, W, GH)[1]
        T[0, j] = r
        T[1, j] = B[1 + 2 * j] + B[2 + 2 * j]
        return 0

    lax.fori_loop(0, 8, restrict, 0)
    mat = matrix((128, 128), lambda i, o: i // 2 == o % 64, 0.125)
    for a in range(2):
        both = T[a, :, pl.ds(0, 32, stride=2), :] + T[a, :, pl.ds(1, 32, stride=2), :]
        got = product(both.reshape(256, 128), mat).reshape(8, 32, 128)
        if a == 0:
            G3[...] = got
        else:
            B3[1:9] = got

    initial, terms = chebyshev_terms(bottom_low, BOTTOM)
    scale = 0.25**3
    rows = iota((32, 128), 0)
    row_low3 = jnp.where(rows > 0, F32(1.0), F32(0.0))
    row_high3 = jnp.where(rows < 31, F32(1.0), F32(0.0))
    for ref in (B3, VA3, VB3):
        ref[0] = jnp.zeros((32, 128), F32)
        ref[9] = jnp.zeros((32, 128), F32)

    def prepare3(i, _):
        faces, inverse, double = weigh(B3[i], B3[i + 1], B3[i + 2], row_low3, row_high3)
        for f in range(6):
            W3[f, i] = faces[f]
        gh = G3[i] * ((2.0 / scale) * inverse)
        GH3[i] = gh
        VA3[i + 1] = gh * initial
        return 0

    lax.fori_loop(0, 8, prepare3, 0)
    e3 = smooth(VA3, VB3, DD3, W3, GH3, 1, 0, 8, 0, terms)

    spread = matrix((128, 128), lambda i, o: i == o // 2, 1.0)
    for i in range(2):
        own = e3[1 + 2 * gx + i]
        X3[i, pl.ds(0, 32, stride=2), :] = own
        X3[i, pl.ds(1, 32, stride=2), :] = own
    row = pl.multiple_of(8 * gy, 8)
    for i in range(4):
        e2 = v[1 + 4 * gx + i, pl.ds(row, 8), :]
        e2 = e2 + product(X3[i // 2, pl.ds(row, 8), :], spread)
        up = product(e2, spread)
        E1[i, pl.ds(0, 8, stride=2), :] = up
        E1[i, pl.ds(1, 8, stride=2), :] = up
    for i in range(8):
        e1 = x1[i] + E1[i // 2]
        up = product(e1, spread)
        E0[i, pl.ds(0, 16, stride=2), :] = up
        E0[i, pl.ds(1, 16, stride=2), :] = up
    for i in range(16):
        out[i] = x0[i] + E0[i // 2]


def call(kernel, outs, scratch, limit):
    many = len(outs) > 1
    shapes = [jax.ShapeDtypeStruct(s, F32) for s in outs]
    return pl.pallas_call(
        kernel,
        out_shape=shapes if many else shapes[0],
        scratch_shapes=[pltpu.VMEM(s, F32) for s in scratch],
        compiler_params=pltpu.CompilerParams(vmem_limit_bytes=limit << 20),
    )


def per_device(g, b):
    xl = ring(jnp.concatenate([g[-4:], b[-5:]]), "gx", 1)
    xh = ring(jnp.concatenate([g[:4], b[:5]]), "gx", -1)

    def rows(at):
        parts = [xl[:4], g, xh[:4], xl[4:], b, xh[4:]]
        return jnp.concatenate([p[:, at : at + 16] for p in parts])

    yl = ring(rows(16), "gy", 1)
    yh = ring(rows(0), "gy", -1)
    high, low = call(pack_kernel, [(7, 64, 128)] * 2, [], 16)(g, b, xl, xh, yl, yh)
    zl = ring(high, "gz", 1)
    zh = ring(low, "gz", -1)

    wide = (64, 256)
    x0, g1, b1 = call(
        level0_kernel,
        [(16, 32, 128), (8, 32, 128), (8, 32, 128)],
        [(24,) + wide, (26,) + wide, (6, 24) + wide]
        + [(24,) + wide] * 5
        + [(4, 8, 64, 128)],
        40,
    )(g, b, xl, xh, yl, yh, zl, zh)

    xl = ring(jnp.concatenate([g1[-4:], b1[-5:]]), "gx", 1)
    xh = ring(jnp.concatenate([g1[:4], b1[:5]]), "gx", -1)
    wide = (32, 128)
    x1, chunk = call(
        level1_kernel,
        [(8, 16, 128), (2, 8, 128)],
        [(16,) + wide, (18,) + wide, (6, 16) + wide]
        + [(16,) + wide] * 5
        + [(2, 4) + wide],
        16,
    )(g1, b1, xl, xh)

    left = ring(chunk, "gz", 1)
    right = ring(chunk, "gz", -1)
    send = jnp.concatenate([chunk, left, right])
    send = jnp.broadcast_to(send[None], (32, 6, 8, 128))
    recv = lax.all_to_all(send, ("gx", "gy"), 0, 0, tiled=False)

    wide, low3 = (64, 128), (32, 128)
    return call(
        finish_kernel,
        [(16, 32, 128)],
        [(16,) + wide, (18,) + wide, (6, 16) + wide]
        + [(16,) + wide] * 2
        + [(18,) + wide] * 2
        + [(16,) + wide, (2, 8) + wide]
        + [(8,) + low3, (10,) + low3, (6, 8) + low3, (10,) + low3, (10,) + low3]
        + [(8,) + low3] * 2
        + [(2, 64, 128), (4, 16, 128), (8, 32, 128)],
        24,
    )(recv, x0, x1)


def solution(mesh):
    placed = (P("gx", "gy", "gz"), P("gx", "gy", "gz"))
    return jax.shard_map(
        per_device, mesh=mesh, in_specs=placed, out_specs=P("gx", "gy", "gz"), check_vma=False
    )
```

```python
import jax
import jax.numpy as jnp
from jax import lax
from jax.experimental import pallas as pl
from jax.experimental.pallas import tpu as pltpu
from jax.sharding import PartitionSpec as P

LEVELS = 3
SWEEPS = 4
BOTTOM = 8

cheby_top = 2.0
smooth_low = 0.25
bottom_low = 0.02

F32 = jnp.float32


def chebyshev_terms(lower_bound, sweeps):
    middle = (cheby_top + lower_bound) / 2.0
    radius = (cheby_top - lower_bound) / 2.0
    sigma_ratio = middle / radius
    rho_old = 1.0 / sigma_ratio
    term_list = []
    for sweep_index in range(1, sweeps):
        rho_new = 1.0 / (2.0 * sigma_ratio - rho_old)
        term_list.append((rho_new * rho_old, 2.0 * rho_new / radius))
        rho_old = rho_new
    return (1.0 / middle, term_list)


def ring(values, axis, step):
    count = lax.axis_size(axis)
    return lax.ppermute(values, axis, [(i, (i + step) % count) for i in range(count)])


def iota(shape, axis):
    return lax.broadcasted_iota(jnp.int32, shape, axis)


def matrix(shape, hit, value):
    return jnp.where(hit(iota(shape, 0), iota(shape, 1)), F32(value), F32(0.0))


def product(left, right):
    return jnp.dot(left, right, precision=lax.Precision.HIGHEST, preferred_element_type=F32)


def beside(cols):
    low = [pltpu.roll(c, 1, 1) for c in cols]
    high = [pltpu.roll(c, 127, 1) for c in cols]
    if len(cols) == 2:
        lanes = iota(cols[0].shape, 1)
        first, last = lanes == 0, lanes == 127
        low = [jnp.where(first, low[1], low[0]), jnp.where(first, low[0], low[1])]
        high = [jnp.where(last, high[1], high[0]), jnp.where(last, high[0], high[1])]
    return low, high


def around(field, plane, row, count):
    cols = range(field.shape[0])
    here = [field[c, plane, pl.ds(8 + row, count), :] for c in cols]
    low, high = beside(here)
    out = []
    for c in cols:
        out.append(
            (
                here[c],
                field[c, plane - 1, pl.ds(8 + row, count), :],
                field[c, plane + 1, pl.ds(8 + row, count), :],
                field[c, plane, pl.ds(7 + row, count), :],
                field[c, plane, pl.ds(9 + row, count), :],
                low[c],
                high[c],
            )
        )
    return out


def sweep_planes(low, high, body, unroll):
    steps = (high - low) // unroll
    if steps > 1:

        def several(j, _):
            for u in range(unroll):
                body(low + j * unroll + u)
            return 0

        lax.fori_loop(0, steps, several, 0)
        low = low + steps * unroll
    for i in range(low, high):
        body(i)


class Level:
    def __init__(self, rows, block, unroll, at, scale, low, sweeps, w, gh, d, va, vb, double):
        self.rows, self.block, self.unroll, self.at, self.scale = rows, block, unroll, at, scale
        self.initial, self.terms = chebyshev_terms(low, sweeps)
        self.w, self.gh, self.d, self.va, self.vb, self.double = w, gh, d, va, vb, double

    def blocks(self, first=0, last=None):
        last = self.rows if last is None else last
        return [(r, min(self.block, last - r)) for r in range(first, last, self.block)]

    def clear(self, planes):
        for ref in (self.va, self.vb):
            shape = ref.shape
            edge = jnp.zeros((shape[0], shape[1], 8, 128), F32)
            ref[:, :, 0:8, :] = edge
            ref[:, :, 8 + self.rows : 16 + self.rows, :] = edge
            for p in planes:
                ref[:, p] = jnp.zeros((shape[0],) + shape[2:], F32)

    def prepare(self, low, high, b, g, shift):
        def body(i):
            for r, n in self.blocks():
                for c, (bc, *near) in enumerate(around(b, i + shift, r, n)):
                    double = 6.0 * bc + (
                        (near[0] + near[1]) + (near[2] + near[3]) + (near[4] + near[5])
                    )
                    inverse = jnp.where(bc > 0.0, 1.0 / double, 0.0)
                    for f in range(6):
                        self.w[f, c, i, pl.ds(r, n), :] = (bc + near[f]) * inverse
                    gh = g(c, i, r, n) * ((2.0 / self.scale) * inverse)
                    self.gh[c, i, pl.ds(r, n), :] = gh
                    self.va[c, i + self.at, pl.ds(8 + r, n), :] = gh * self.initial
                    if self.double is not None:
                        self.double[c, i, pl.ds(r, n), :] = (0.5 * self.scale) * double

        sweep_planes(low, high, body, self.unroll)

    def scaled_residual(self, v, i, r, n):
        out = []
        for c, (vc, *near) in enumerate(around(v, i + self.at, r, n)):
            z = self.gh[c, i, pl.ds(r, n), :] - vc
            for f in range(6):
                z = z + self.w[f, c, i, pl.ds(r, n), :] * near[f]
            out.append((vc, z))
        return out

    def smooth(self, low, high, shrink):
        src, dst = self.va, self.vb
        for k, (carry, push) in enumerate(self.terms):
            low, high = low + shrink, high - shrink

            def body(i, src=src, dst=dst, k=k, carry=carry, push=push):
                for r, n in self.blocks():
                    for c, (vc, z) in enumerate(self.scaled_residual(src, i, r, n)):
                        old = vc if k == 0 else self.d[c, i, pl.ds(r, n), :]
                        step = carry * old + push * z
                        if k < len(self.terms) - 1:
                            self.d[c, i, pl.ds(r, n), :] = step
                        dst[c, i + self.at, pl.ds(8 + r, n), :] = vc + step

            sweep_planes(low, high, body, self.unroll)
            src, dst = dst, src
        return src

    def residual_pairs(self, v, low, high, first, last, put):
        def body(j):
            for r, n in self.blocks(first, last):
                total = None
                for i in (low + 2 * j, low + 2 * j + 1):
                    now = [
                        self.double[c, i, pl.ds(r, n), :] * z
                        for c, (_, z) in enumerate(self.scaled_residual(v, i, r, n))
                    ]
                    total = now if total is None else [a + b for a, b in zip(total, now)]
                for c, t in enumerate(total):
                    put(j, c, r, n, t)

        sweep_planes(0, (high - low) // 2, body, max(1, self.unroll // 2))


def flag(condition):
    return jnp.where(condition, F32(1.0), F32(0.0))


def plane_of(p, g, b, xl, xh):
    if p < 4:
        return xl[p]
    if p < 20:
        return g[p - 4]
    if p < 24:
        return xh[p - 20]
    if p < 29:
        return xl[p - 20]
    if p < 45:
        return b[p - 29]
    return xh[p - 41]


def pack_kernel(g, b, xl, xh, high, low):
    slot = iota((32, 128), 1) // 16
    for k in range(7):
        to_high = jnp.zeros((32, 128), F32)
        to_low = jnp.zeros((32, 128), F32)
        for s in range(8):
            p = 8 * k + s
            if p >= 50:
                break
            plane = plane_of(p, g, b, xl, xh)
            to_high = jnp.where(slot == s, pltpu.roll(plane, 16 * (s + 1) % 128, 1), to_high)
            to_low = jnp.where(slot == s, pltpu.roll(plane, 16 * s, 1) if s else plane, to_low)
        high[k] = to_high
        low[k] = to_low


def level0_kernel(g, b, xl, xh, yl, yh, zl, zh, x0, g1, b1, G, B, W, GH, D2, VA, VB, DD, T):
    gx, gy, gz = lax.axis_index("gx"), lax.axis_index("gy"), lax.axis_index("gz")
    lanes = iota((64, 128), 1)
    rows = iota((64, 128), 0)
    y_low, y_high, x_low, x_high = flag(gy > 0), flag(gy < 7), flag(gx > 0), flag(gx < 3)
    lane_in = jnp.where(lanes < 16, flag(gz < 7), jnp.where(lanes >= 112, flag(gz > 0), F32(0.0)))
    lane_in = jnp.where(rows < 16, y_low, jnp.where(rows < 48, F32(1.0), y_high)) * lane_in
    for p in range(50):
        k, s = p // 8, p % 8
        from_high = jnp.concatenate([yl[57 + k], zh[k], yh[57 + k]], axis=0)
        from_high = pltpu.roll(from_high, 128 - 16 * s, 1) if s else from_high
        from_low = jnp.concatenate([yl[50 + k], zl[k], yh[50 + k]], axis=0)
        from_low = pltpu.roll(from_low, 112 - 16 * s, 1) if s < 7 else from_low
        far = jnp.where(lanes < 16, from_high, from_low)
        own, below, above = plane_of(p, g, b, xl, xh), yl[p], yh[p]
        if p < 24:
            G[0, p, 4:20, :] = below
            G[0, p, 20:52, :] = own
            G[0, p, 52:68, :] = above
            G[1, p, 4:68, :] = far
        else:
            q = p - 24
            far = far * lane_in
            below, above = below * y_low, above * y_high
            if q < 5:
                own, below, above, far = (x_low * t for t in (own, below, above, far))
            if q >= 21:
                own, below, above, far = (x_high * t for t in (own, below, above, far))
            B[0, q, 4:20, :] = below
            B[0, q, 20:52, :] = own
            B[0, q, 52:68, :] = above
            B[1, q, 4:68, :] = far

    level = Level(56, BLOCK0, UNROLL0, 0, 1.0, smooth_low, SWEEPS, W, GH, DD, VA, VB, D2)
    level.clear([])
    level.prepare(0, 24, B, lambda c, i, r, n: G[c, i, pl.ds(8 + r, n), :], 1)
    v = level.smooth(0, 24, 1)
    x0[...] = v[0, 4:20, 20:52, :]

    def put(j, c, r, n, total):
        T[c, j, pl.ds(r, n), :] = total

    level.residual_pairs(v, 4, 20, 0, 56, put)
    near_mat = matrix((128, 128), lambda a, c: a // 2 == c, 0.125)
    far_mat = matrix((128, 128), lambda a, c: a // 2 + 64 == c, 0.125)

    def halved(start, count):
        sums = []
        for c in range(2):
            even = T[c, :, pl.ds(start, count, stride=2), :]
            odd = T[c, :, pl.ds(start + 1, count, stride=2), :]
            sums.append((even + odd).reshape(8 * count, 128))
        total = product(sums[0], near_mat) + product(sums[1], far_mat)
        return total.reshape(8, count, 128)

    g1[...] = halved(4, 24)
    for c in range(2):
        for j in range(8):
            T[c, j, 0:64, :] = B[c, 5 + 2 * j, 4:68, :] + B[c, 6 + 2 * j, 4:68, :]
    b1[...] = halved(0, 32)


def level1_kernel(g, b, xl, xh, x1, chunk, B, W, GH, D2, VA, VB, DD, T):
    gx = lax.axis_index("gx")
    for q in range(5):
        B[0, q, 4:36, :] = xl[96 + 32 * q : 128 + 32 * q, :] * flag(gx > 0)
        B[0, 13 + q, 4:36, :] = xh[96 + 32 * q : 128 + 32 * q, :] * flag(gx < 3)
    for q in range(8):
        B[0, 5 + q, 4:36, :] = b[q]

    def source(c, i, r, n):
        if i < 4:
            return xl[24 * i + r : 24 * i + r + n, :]
        if i < 12:
            return g[i - 4, r : r + n, :]
        return xh[24 * (i - 12) + r : 24 * (i - 12) + r + n, :]

    level = Level(24, 24, 16, 0, 0.25, smooth_low, SWEEPS, W, GH, DD, VA, VB, D2)
    level.clear([])
    level.prepare(0, 16, B, source, 1)
    v = level.smooth(0, 16, 1)
    x1[...] = v[0, 4:12, 12:28, :]

    def put(j, c, r, n, total):
        T[0, j, pl.ds(r, n), :] = total

    level.residual_pairs(v, 4, 12, 0, 24, put)
    for q in range(4):
        T[1, q] = B[0, 5 + 2 * q, 8:32, :] + B[0, 6 + 2 * q, 8:32, :]
    both = T[:, :, pl.ds(4, 8, stride=2), :] + T[:, :, pl.ds(5, 8, stride=2), :]
    mat = matrix((128, 128), lambda a, c: (a < 64) & (a // 2 == c), 0.125)
    total = product(both.reshape(64, 128), mat).reshape(2, 4, 8, 128)
    for a in range(2):
        out = total[a, 0]
        for q in range(1, 4):
            out = out + pltpu.roll(total[a, q], 32 * q, 1)
        chunk[a] = out


def finish_kernel(
    slab, zl, zh, x0, x1, out, G, B, W, GH, D2, VA, VB, DD, T, B3, W3, VA3, VB3, DD3, GH3, X3, E1, E0
):
    gx, gy, gz = lax.axis_index("gx"), lax.axis_index("gy"), lax.axis_index("gz")
    lanes = iota((8, 128), 1)
    zeros = jnp.zeros((8, 128), F32)
    lane_in = jnp.where(lanes < 32, F32(1.0), jnp.where(lanes < 64, flag(gz < 7), zeros))
    lane_in = jnp.where(lanes >= 96, flag(gz > 0), lane_in)

    def turn(v, s):
        s = s % 128
        return pltpu.roll(v, s, 1) if s else v

    for p in (0, 17):
        B[0, p] = jnp.zeros((80, 128), F32)
    B[0, :, 0:8, :] = jnp.zeros((18, 8, 128), F32)
    B[0, :, 72:80, :] = jnp.zeros((18, 8, 128), F32)
    for j in range(32):
        row = 8 * (j % 8)
        for q in range(4):
            plane = 4 * (j // 8) + q
            for a in range(2):
                own, left, right = slab[j, a], zl[j, a], zh[j, a]
                got = jnp.where(
                    lanes < 32,
                    turn(own, -32 * q),
                    jnp.where(lanes < 64, turn(right, 32 - 32 * q), turn(left, 96 - 32 * q)),
                )
                if a == 0:
                    G[plane, row : row + 8, :] = got
                else:
                    B[0, plane + 1, 8 + row : 16 + row, :] = got * lane_in

    level = Level(64, BLOCK2, UNROLL2, 1, 0.25**2, smooth_low, SWEEPS, W, GH, DD, VA, VB, D2)
    level.clear([0, 17])
    level.prepare(0, 16, B, lambda c, i, r, n: G[i, pl.ds(r, n), :], 1)
    v = level.smooth(0, 16, 0)

    def put(j, c, r, n, total):
        T[0, j, pl.ds(r, n), :] = total

    level.residual_pairs(v, 0, 16, 0, 64, put)
    for j in range(8):
        T[1, j] = B[0, 1 + 2 * j, 8:72, :] + B[0, 2 + 2 * j, 8:72, :]
    both = T[:, :, pl.ds(0, 32, stride=2), :] + T[:, :, pl.ds(1, 32, stride=2), :]
    mat = matrix((128, 128), lambda a, c: a // 2 == c % 64, 0.125)
    coarse = product(both.reshape(512, 128), mat).reshape(2, 8, 32, 128)
    for p in (0, 9):
        B3[0, p] = jnp.zeros((48, 128), F32)
    B3[0, :, 0:8, :] = jnp.zeros((10, 8, 128), F32)
    B3[0, :, 40:48, :] = jnp.zeros((10, 8, 128), F32)
    B3[0, 1:9, 8:40, :] = coarse[1]

    base = Level(32, 32, 8, 1, 0.25**3, bottom_low, BOTTOM, W3, GH3, DD3, VA3, VB3, None)
    base.clear([0, 9])
    base.prepare(0, 8, B3, lambda c, i, r, n: coarse[0, i, r : r + n, :], 1)
    e3 = base.smooth(0, 8, 0)

    spread = matrix((128, 128), lambda a, c: a == c // 2, 1.0)
    for i in range(2):
        own = e3[0, 1 + 2 * gx + i, 8:40, :]
        X3[i, pl.ds(0, 32, stride=2), :] = own
        X3[i, pl.ds(1, 32, stride=2), :] = own
    row = pl.multiple_of(8 * gy, 8)
    up = product(X3[:, pl.ds(row, 8), :].reshape(16, 128), spread).reshape(2, 8, 128)
    e2 = [v[0, 1 + 4 * gx + i, pl.ds(8 + row, 8), :] + up[i // 2] for i in range(4)]
    up = product(jnp.concatenate(e2, axis=0), spread).reshape(4, 8, 128)
    for i in range(4):
        E1[i, pl.ds(0, 8, stride=2), :] = up[i]
        E1[i, pl.ds(1, 8, stride=2), :] = up[i]
    e1 = [x1[i] + E1[i // 2] for i in range(8)]
    up = product(jnp.concatenate(e1, axis=0), spread).reshape(8, 16, 128)
    for i in range(8):
        E0[i, pl.ds(0, 16, stride=2), :] = up[i]
        E0[i, pl.ds(1, 16, stride=2), :] = up[i]
        out[2 * i] = x0[2 * i] + E0[i]
        out[2 * i + 1] = x0[2 * i + 1] + E0[i]


BLOCK0, UNROLL0, BLOCK2, UNROLL2 = 56, 8, 64, 16


def call(kernel, outs, scratch, limit):
    many = len(outs) > 1
    shapes = [jax.ShapeDtypeStruct(s, F32) for s in outs]
    return pl.pallas_call(
        kernel,
        out_shape=shapes if many else shapes[0],
        scratch_shapes=[pltpu.VMEM(s, F32) for s in scratch],
        compiler_params=pltpu.CompilerParams(vmem_limit_bytes=limit << 20),
    )


def stage0(*args):
    wide, tall = (56, 128), (72, 128)
    scratch = [(2, 24) + tall, (2, 26) + tall, (6, 2, 24) + wide, (2, 24) + wide, (2, 24) + wide]
    scratch += [(2, 24) + tall, (2, 24) + tall, (2, 24) + wide, (2, 8, 64, 128)]
    return call(level0_kernel, [(16, 32, 128), (8, 24, 128), (8, 32, 128)], scratch, 36)(*args)


def stage1(*args):
    wide, tall = (24, 128), (40, 128)
    scratch = [(1, 18) + tall, (6, 1, 16) + wide, (1, 16) + wide, (1, 16) + wide]
    scratch += [(1, 16) + tall, (1, 16) + tall, (1, 16) + wide, (2, 4) + wide]
    return call(level1_kernel, [(8, 16, 128), (2, 8, 128)], scratch, 16)(*args)


def stage2(*args):
    wide, tall, wide3, tall3 = (64, 128), (80, 128), (32, 128), (48, 128)
    scratch = [(16,) + wide, (1, 18) + tall, (6, 1, 16) + wide, (1, 16) + wide, (1, 16) + wide]
    scratch += [(1, 18) + tall, (1, 18) + tall, (1, 16) + wide, (2, 8) + wide]
    scratch += [(1, 10) + tall3, (6, 1, 8) + wide3, (1, 10) + tall3, (1, 10) + tall3]
    scratch += [(1, 8) + wide3, (1, 8) + wide3, (2, 64, 128), (4, 16, 128), (8, 32, 128)]
    return call(finish_kernel, [(16, 32, 128)], scratch, 24)(*args)


def per_device(g, b):
    xl = ring(jnp.concatenate([g[-4:], b[-5:]]), "gx", 1)
    xh = ring(jnp.concatenate([g[:4], b[:5]]), "gx", -1)

    high, low = call(pack_kernel, [(7, 32, 128)] * 2, [], 16)(g, b, xl, xh)
    zl = ring(high, "gz", 1)
    zh = ring(low, "gz", -1)

    def rows(at):
        parts = [xl[:4], g, xh[:4], xl[4:], b, xh[4:], zl, zh]
        return jnp.concatenate([p[:, at : at + 16] for p in parts])

    yl = ring(rows(16), "gy", 1)
    yh = ring(rows(0), "gy", -1)
    x0, g1, b1 = stage0(g, b, xl, xh, yl, yh, zl, zh)

    def both(at4, at5):
        return jnp.concatenate([g1[at4].reshape(96, 128), b1[at5].reshape(160, 128)])

    xl = ring(both(slice(4, 8), slice(3, 8)), "gx", 1)
    xh = ring(both(slice(0, 4), slice(0, 5)), "gx", -1)
    x1, chunk = stage1(g1, b1, xl, xh)

    send = jnp.broadcast_to(chunk[None], (32, 2, 8, 128))
    slab = lax.all_to_all(send, ("gx", "gy"), 0, 0, tiled=False)
    return stage2(slab, ring(slab, "gz", 1), ring(slab, "gz", -1), x0, x1)


def solution(mesh):
    placed = (P("gx", "gy", "gz"), P("gx", "gy", "gz"))
    return jax.shard_map(
        per_device, mesh=mesh, in_specs=placed, out_specs=P("gx", "gy", "gz"), check_vma=False
    )
```

```python
import jax
import jax.numpy as jnp
from jax import lax
from jax.experimental import pallas as pl
from jax.experimental.pallas import tpu as pltpu
from jax.sharding import PartitionSpec as P

LEVELS = 3
SWEEPS = 4
BOTTOM = 8

cheby_top = 2.0
smooth_low = 0.25
bottom_low = 0.02

F32 = jnp.float32


def chebyshev_terms(lower_bound, sweeps):
    middle = (cheby_top + lower_bound) / 2.0
    radius = (cheby_top - lower_bound) / 2.0
    sigma_ratio = middle / radius
    rho_old = 1.0 / sigma_ratio
    term_list = []
    for sweep_index in range(1, sweeps):
        rho_new = 1.0 / (2.0 * sigma_ratio - rho_old)
        term_list.append((rho_new * rho_old, 2.0 * rho_new / radius))
        rho_old = rho_new
    return (1.0 / middle, term_list)


def ring(values, axis, step):
    count = lax.axis_size(axis)
    return lax.ppermute(values, axis, [(i, (i + step) % count) for i in range(count)])


def iota(shape, axis):
    return lax.broadcasted_iota(jnp.int32, shape, axis)


def matrix(shape, hit, value):
    return jnp.where(hit(iota(shape, 0), iota(shape, 1)), F32(value), F32(0.0))


def product(left, right):
    return jnp.dot(left, right, precision=lax.Precision.HIGHEST, preferred_element_type=F32)


def beside(cols):
    low = [pltpu.roll(c, 1, 1) for c in cols]
    high = [pltpu.roll(c, 127, 1) for c in cols]
    if len(cols) == 2:
        lanes = iota(cols[0].shape, 1)
        first, last = lanes == 0, lanes == 127
        low = [jnp.where(first, low[1], low[0]), jnp.where(first, low[0], low[1])]
        high = [jnp.where(last, high[1], high[0]), jnp.where(last, high[0], high[1])]
    return low, high


def around(field, plane, row, count):
    cols = range(field.shape[0])
    here = [field[c, plane, pl.ds(8 + row, count), :] for c in cols]
    low, high = beside(here)
    out = []
    for c in cols:
        out.append(
            (
                here[c],
                field[c, plane - 1, pl.ds(8 + row, count), :],
                field[c, plane + 1, pl.ds(8 + row, count), :],
                field[c, plane, pl.ds(7 + row, count), :],
                field[c, plane, pl.ds(9 + row, count), :],
                low[c],
                high[c],
            )
        )
    return out


def sweep_planes(low, high, body, unroll):
    steps = (high - low) // unroll
    if steps > 1:

        def several(j, _):
            for u in range(unroll):
                body(low + j * unroll + u)
            return 0

        lax.fori_loop(0, steps, several, 0)
        low = low + steps * unroll
    for i in range(low, high):
        body(i)


class Level:
    def __init__(self, rows, block, unroll, at, scale, low, sweeps, w, gh, d, va, vb, double):
        self.rows, self.block, self.unroll, self.at, self.scale = rows, block, unroll, at, scale
        self.initial, self.terms = chebyshev_terms(low, sweeps)
        self.w, self.gh, self.d, self.va, self.vb, self.double = w, gh, d, va, vb, double

    def blocks(self, first=0, last=None):
        last = self.rows if last is None else last
        return [(r, min(self.block, last - r)) for r in range(first, last, self.block)]

    def clear(self, planes):
        for ref in (self.va, self.vb):
            shape = ref.shape
            edge = jnp.zeros((shape[0], shape[1], 8, 128), F32)
            ref[:, :, 0:8, :] = edge
            ref[:, :, 8 + self.rows : 16 + self.rows, :] = edge
            for p in planes:
                ref[:, p] = jnp.zeros((shape[0],) + shape[2:], F32)

    def prepare(self, low, high, b, g, shift):
        def body(i):
            for r, n in self.blocks():
                for c, (bc, *near) in enumerate(around(b, i + shift, r, n)):
                    double = 6.0 * bc + (
                        (near[0] + near[1]) + (near[2] + near[3]) + (near[4] + near[5])
                    )
                    inverse = jnp.where(bc > 0.0, 1.0 / double, 0.0)
                    for f in range(6):
                        self.w[f, c, i, pl.ds(r, n), :] = (bc + near[f]) * inverse
                    gh = g(c, i, r, n) * ((2.0 / self.scale) * inverse)
                    self.gh[c, i, pl.ds(r, n), :] = gh
                    self.va[c, i + self.at, pl.ds(8 + r, n), :] = gh * self.initial
                    if self.double is not None:
                        self.double[c, i, pl.ds(r, n), :] = (0.5 * self.scale) * double

        sweep_planes(low, high, body, self.unroll)

    def scaled_residual(self, v, i, r, n):
        out = []
        for c, (vc, *near) in enumerate(around(v, i + self.at, r, n)):
            z = self.gh[c, i, pl.ds(r, n), :] - vc
            for f in range(6):
                z = z + self.w[f, c, i, pl.ds(r, n), :] * near[f]
            out.append((vc, z))
        return out

    def smooth(self, low, high, shrink):
        src, dst = self.va, self.vb
        for k, (carry, push) in enumerate(self.terms):
            low, high = low + shrink, high - shrink

            def body(i, src=src, dst=dst, k=k, carry=carry, push=push):
                for r, n in self.blocks():
                    for c, (vc, z) in enumerate(self.scaled_residual(src, i, r, n)):
                        old = vc if k == 0 else self.d[c, i, pl.ds(r, n), :]
                        step = carry * old + push * z
                        if k < len(self.terms) - 1:
                            self.d[c, i, pl.ds(r, n), :] = step
                        dst[c, i + self.at, pl.ds(8 + r, n), :] = vc + step

            sweep_planes(low, high, body, self.unroll)
            src, dst = dst, src
        return src

    def residual_pairs(self, v, low, high, first, last, put):
        def body(j):
            for r, n in self.blocks(first, last):
                total = None
                for i in (low + 2 * j, low + 2 * j + 1):
                    now = [
                        self.double[c, i, pl.ds(r, n), :] * z
                        for c, (_, z) in enumerate(self.scaled_residual(v, i, r, n))
                    ]
                    total = now if total is None else [a + b for a, b in zip(total, now)]
                for c, t in enumerate(total):
                    put(j, c, r, n, t)

        sweep_planes(0, (high - low) // 2, body, max(1, self.unroll // 2))


def flag(condition):
    return jnp.where(condition, F32(1.0), F32(0.0))


def plane_of(p, g, b, xl, xh):
    if p < 4:
        return xl[p]
    if p < 20:
        return g[p - 4]
    if p < 24:
        return xh[p - 20]
    if p < 29:
        return xl[p - 20]
    if p < 45:
        return b[p - 29]
    return xh[p - 41]


def pack_kernel(g, b, xl, xh, high, low):
    slot = iota((32, 128), 1) // 16
    for k in range(7):
        to_high = jnp.zeros((32, 128), F32)
        to_low = jnp.zeros((32, 128), F32)
        for s in range(8):
            p = 8 * k + s
            if p >= 50:
                break
            plane = plane_of(p, g, b, xl, xh)
            to_high = jnp.where(slot == s, pltpu.roll(plane, 16 * (s + 1) % 128, 1), to_high)
            to_low = jnp.where(slot == s, pltpu.roll(plane, 16 * s, 1) if s else plane, to_low)
        high[k] = to_high
        low[k] = to_low


INNER = 64
OUTER = list(range(1, 23)) + list(range(25, 49)) + list(range(50, 64))
LAST = list(range(29, 45))
OUTER_AT = 8 * INNER
LAST_AT = OUTER_AT + 4 * len(OUTER)
Y_ROWS = LAST_AT + len(LAST)


def pack_y_kernel(g, b, xl, xh, zl, zh, high, low):
    def plane(p):
        if p < 50:
            return plane_of(p, g, b, xl, xh)
        return zl[p - 50] if p < 57 else zh[p - 57]

    for p in range(INNER):
        here = plane(p)
        high[8 * p : 8 * p + 8, :] = here[24:32]
        low[8 * p : 8 * p + 8, :] = here[0:8]
    for i, p in enumerate(OUTER):
        here, at = plane(p), OUTER_AT + 4 * i
        high[at : at + 4, :] = here[20:24]
        low[at : at + 4, :] = here[8:12]
    for i, p in enumerate(LAST):
        here, at = plane(p), LAST_AT + i
        high[at : at + 1, :] = here[19:20]
        low[at : at + 1, :] = here[12:13]


def level0_kernel(g, b, xl, xh, yl, yh, zl, zh, x0, g1, b1, G, B, Z, W, GH, D2, VA, VB, DD, T):
    gx, gy, gz = lax.axis_index("gx"), lax.axis_index("gy"), lax.axis_index("gz")
    lanes = iota((56, 128), 1)
    rows = iota((56, 128), 0)
    y_low, y_high, x_low, x_high = flag(gy > 0), flag(gy < 7), flag(gx > 0), flag(gx < 3)
    lane_in = jnp.where(lanes < 16, flag(gz < 7), jnp.where(lanes >= 112, flag(gz > 0), F32(0.0)))
    lane_in = jnp.where(rows < 12, y_low, jnp.where(rows < 44, F32(1.0), y_high)) * lane_in
    blank4, blank8 = jnp.zeros((4, 128), F32), jnp.zeros((8, 128), F32)
    order = {p: i for i, p in enumerate(OUTER)}

    def outer(side, p):
        if p not in order:
            return blank4
        at = OUTER_AT + 4 * order[p]
        return side[at : at + 4, :]

    for side, source in ((0, zl), (1, zh)):
        for k in range(7):
            p = 50 + 7 * side + k
            Z[side, k, 0:4, :] = outer(yl, p)
            Z[side, k, 4:12, :] = yl[8 * p : 8 * p + 8, :]
            Z[side, k, 12:44, :] = source[k]
            Z[side, k, 44:52, :] = yh[8 * p : 8 * p + 8, :]
            Z[side, k, 52:56, :] = outer(yh, p)
    for p in range(50):
        k, s = p // 8, p % 8
        from_high = Z[1, k]
        from_high = pltpu.roll(from_high, 128 - 16 * s, 1) if s else from_high
        from_low = Z[0, k]
        from_low = pltpu.roll(from_low, 112 - 16 * s, 1) if s < 7 else from_low
        far = jnp.where(lanes < 16, from_high, from_low)
        own = plane_of(p, g, b, xl, xh)
        below, above = yl[8 * p : 8 * p + 8, :], yh[8 * p : 8 * p + 8, :]
        below4, above4 = outer(yl, p), outer(yh, p)
        field, q = (G, p) if p < 24 else (B, p - 24)
        if p >= 24:
            far = far * lane_in
            side = x_low if q < 5 else x_high if q >= 21 else None
            if side is not None:
                own, far = own * side, far * side
                below, below4 = below * (y_low * side), below4 * (y_low * side)
                above, above4 = above * (y_high * side), above4 * (y_high * side)
            else:
                below, below4 = below * y_low, below4 * y_low
                above, above4 = above * y_high, above4 * y_high
            field[0, q, 0:8, :] = blank8
            field[0, q, 64:72, :] = blank8
            field[1, q, 0:8, :] = blank8
            field[1, q, 64:72, :] = blank8
            if p in LAST:
                at = LAST_AT + LAST.index(p)
                field[0, q, 7:8, :] = yl[at : at + 1, :] * y_low
                field[0, q, 64:65, :] = yh[at : at + 1, :] * y_high
        field[0, q, 8:12, :] = below4
        field[0, q, 12:20, :] = below
        field[0, q, 20:52, :] = own
        field[0, q, 52:60, :] = above
        field[0, q, 60:64, :] = above4
        field[1, q, 8:64, :] = far

    level = Level(56, BLOCK0, UNROLL0, 0, 1.0, smooth_low, SWEEPS, W, GH, DD, VA, VB, D2)
    level.clear([])
    level.prepare(0, 24, B, lambda c, i, r, n: G[c, i, pl.ds(8 + r, n), :], 1)
    v = level.smooth(0, 24, 1)
    x0[...] = v[0, 4:20, 20:52, :]

    def put(j, c, r, n, total):
        T[c, j, pl.ds(r, n), :] = total

    level.residual_pairs(v, 4, 20, 4, 52, put)
    near_mat = matrix((128, 128), lambda a, c: a // 2 == c, 0.125)
    far_mat = matrix((128, 128), lambda a, c: a // 2 + 64 == c, 0.125)

    def halved(start, count):
        sums = []
        for c in range(2):
            even = T[c, :, pl.ds(start, count, stride=2), :]
            odd = T[c, :, pl.ds(start + 1, count, stride=2), :]
            sums.append((even + odd).reshape(8 * count, 128))
        total = product(sums[0], near_mat) + product(sums[1], far_mat)
        return total.reshape(8, count, 128)

    g1[...] = halved(4, 24)
    for c in range(2):
        for j in range(8):
            T[c, j, 4:60, :] = B[c, 5 + 2 * j, 8:64, :] + B[c, 6 + 2 * j, 8:64, :]
            T[c, j, 0:4, :] = blank4
            T[c, j, 60:64, :] = blank4
    b1[...] = halved(0, 32)


def level1_kernel(g, b, xl, xh, x1, chunk, B, W, GH, D2, VA, VB, DD, T):
    gx = lax.axis_index("gx")
    for q in range(5):
        B[0, q, 4:36, :] = xl[96 + 32 * q : 128 + 32 * q, :] * flag(gx > 0)
        B[0, 13 + q, 4:36, :] = xh[96 + 32 * q : 128 + 32 * q, :] * flag(gx < 3)
    for q in range(8):
        B[0, 5 + q, 4:36, :] = b[q]

    def source(c, i, r, n):
        if i < 4:
            return xl[24 * i + r : 24 * i + r + n, :]
        if i < 12:
            return g[i - 4, r : r + n, :]
        return xh[24 * (i - 12) + r : 24 * (i - 12) + r + n, :]

    level = Level(24, 24, 16, 0, 0.25, smooth_low, SWEEPS, W, GH, DD, VA, VB, D2)
    level.clear([])
    level.prepare(0, 16, B, source, 1)
    v = level.smooth(0, 16, 1)
    x1[...] = v[0, 4:12, 12:28, :]

    def put(j, c, r, n, total):
        T[0, j, pl.ds(r, n), :] = total

    level.residual_pairs(v, 4, 12, 0, 24, put)
    for q in range(4):
        T[1, q] = B[0, 5 + 2 * q, 8:32, :] + B[0, 6 + 2 * q, 8:32, :]
    both = T[:, :, pl.ds(4, 8, stride=2), :] + T[:, :, pl.ds(5, 8, stride=2), :]
    mat = matrix((128, 128), lambda a, c: (a < 64) & (a // 2 == c), 0.125)
    total = product(both.reshape(64, 128), mat).reshape(2, 4, 8, 128)
    for a in range(2):
        out = total[a, 0]
        for q in range(1, 4):
            out = out + pltpu.roll(total[a, q], 32 * q, 1)
        chunk[a] = out


def turn(v, shift):
    shift = shift % 128
    return pltpu.roll(v, shift, 1) if shift else v


def pack_z_kernel(slab, high, low):
    lanes = iota((8, 128), 1)
    first = lanes % 32 < 16
    for j in range(32):
        g, b = slab[j, 0], slab[j, 1]
        high[j] = jnp.where(first, turn(g, -16), b)
        low[j] = jnp.where(first, g, turn(b, 16))
    gy = lax.axis_index("gy")
    for d in range(3):
        by = jnp.clip(gy + d - 1, 0, 7)
        to_high = jnp.zeros((8, 128), F32)
        to_low = jnp.zeros((8, 128), F32)
        for n in range(8):
            here = slab[8 * (n // 2) + by, n % 2]
            mine = lanes % 32 // 4 == n
            to_high = jnp.where(mine, turn(here, 4 * n - 12), to_high)
            to_low = jnp.where(mine, turn(here, 4 * n - 16), to_low)
        high[32 + d] = to_high
        low[32 + d] = to_low


def finish_kernel(
    slab, zl, zh, x0, x1, out, G, B, W, GH, D2, VA, VB, DD, T, B3, W3, VA3, VB3, DD3, GH3, X3, E1, E0
):
    gx, gy, gz = lax.axis_index("gx"), lax.axis_index("gy"), lax.axis_index("gz")
    lanes = iota((8, 128), 1)
    zeros = jnp.zeros((8, 128), F32)
    lane_in = jnp.where(lanes < 32, F32(1.0), jnp.where(lanes < 64, flag(gz < 7), zeros))
    lane_in = jnp.where(lanes >= 96, flag(gz > 0), lane_in)

    for p in (0, 17):
        B[0, p] = jnp.zeros((80, 128), F32)
    B[0, :, 0:8, :] = jnp.zeros((18, 8, 128), F32)
    B[0, :, 72:80, :] = jnp.zeros((18, 8, 128), F32)
    for j in range(32):
        row = 8 * (j % 8)
        for q in range(4):
            plane = 4 * (j // 8) + q
            for a in range(2):
                own, left, right = slab[j, a], zl[j], zh[j]
                far = jnp.where(lanes < 48, turn(right, 32 - 16 * a - 32 * q), 0.0)
                far = jnp.where(lanes >= 112, turn(left, 112 - 16 * a - 32 * q), far)
                got = jnp.where(lanes < 32, turn(own, -32 * q), far)
                if a == 0:
                    G[plane, row : row + 8, :] = got
                else:
                    B[0, plane + 1, 8 + row : 16 + row, :] = got * lane_in
    low4, high4 = (lanes >= 108) & (lanes < 112), (lanes >= 48) & (lanes < 52)
    for d in range(3):
        row = pl.multiple_of(8 * jnp.clip(gy + d - 1, 0, 7), 8)
        left, right = zl[32 + d], zh[32 + d]
        for n in range(8):
            for q in range(4):
                plane = 4 * (n // 2) + q
                far = jnp.where(low4, turn(left, 108 - 32 * q - 4 * n), 0.0)
                far = jnp.where(high4, turn(right, 48 - 32 * q - 4 * n), far)
                if n % 2 == 0:
                    here = G[plane, pl.ds(row, 8), :]
                    G[plane, pl.ds(row, 8), :] = jnp.where(low4 | high4, far, here)
                else:
                    here = B[0, plane + 1, pl.ds(8 + row, 8), :]
                    far = jnp.where(low4 | high4, far * lane_in, here)
                    B[0, plane + 1, pl.ds(8 + row, 8), :] = far

    level = Level(64, BLOCK2, UNROLL2, 1, 0.25**2, smooth_low, SWEEPS, W, GH, DD, VA, VB, D2)
    level.clear([0, 17])
    level.prepare(0, 16, B, lambda c, i, r, n: G[i, pl.ds(r, n), :], 1)
    v = level.smooth(0, 16, 0)

    def put(j, c, r, n, total):
        T[0, j, pl.ds(r, n), :] = total

    level.residual_pairs(v, 0, 16, 0, 64, put)
    for j in range(8):
        T[1, j] = B[0, 1 + 2 * j, 8:72, :] + B[0, 2 + 2 * j, 8:72, :]
    both = T[:, :, pl.ds(0, 32, stride=2), :] + T[:, :, pl.ds(1, 32, stride=2), :]
    mat = matrix((128, 128), lambda a, c: a // 2 == c % 64, 0.125)
    coarse = product(both.reshape(512, 128), mat).reshape(2, 8, 32, 128)
    for p in (0, 9):
        B3[0, p] = jnp.zeros((48, 128), F32)
    B3[0, :, 0:8, :] = jnp.zeros((10, 8, 128), F32)
    B3[0, :, 40:48, :] = jnp.zeros((10, 8, 128), F32)
    B3[0, 1:9, 8:40, :] = coarse[1]

    base = Level(32, 32, 8, 1, 0.25**3, bottom_low, BOTTOM, W3, GH3, DD3, VA3, VB3, None)
    base.clear([0, 9])
    base.prepare(0, 8, B3, lambda c, i, r, n: coarse[0, i, r : r + n, :], 1)
    e3 = base.smooth(0, 8, 0)

    spread = matrix((128, 128), lambda a, c: a == c // 2, 1.0)
    for i in range(2):
        own = e3[0, 1 + 2 * gx + i, 8:40, :]
        X3[i, pl.ds(0, 32, stride=2), :] = own
        X3[i, pl.ds(1, 32, stride=2), :] = own
    row = pl.multiple_of(8 * gy, 8)
    up = product(X3[:, pl.ds(row, 8), :].reshape(16, 128), spread).reshape(2, 8, 128)
    e2 = [v[0, 1 + 4 * gx + i, pl.ds(8 + row, 8), :] + up[i // 2] for i in range(4)]
    up = product(jnp.concatenate(e2, axis=0), spread).reshape(4, 8, 128)
    for i in range(4):
        E1[i, pl.ds(0, 8, stride=2), :] = up[i]
        E1[i, pl.ds(1, 8, stride=2), :] = up[i]
    e1 = [x1[i] + E1[i // 2] for i in range(8)]
    up = product(jnp.concatenate(e1, axis=0), spread).reshape(8, 16, 128)
    for i in range(8):
        E0[i, pl.ds(0, 16, stride=2), :] = up[i]
        E0[i, pl.ds(1, 16, stride=2), :] = up[i]
        out[2 * i] = x0[2 * i] + E0[i]
        out[2 * i + 1] = x0[2 * i + 1] + E0[i]


BLOCK0, UNROLL0, BLOCK2, UNROLL2 = 56, 8, 64, 16


def call(kernel, outs, scratch, limit):
    many = len(outs) > 1
    shapes = [jax.ShapeDtypeStruct(s, F32) for s in outs]
    return pl.pallas_call(
        kernel,
        out_shape=shapes if many else shapes[0],
        scratch_shapes=[pltpu.VMEM(s, F32) for s in scratch],
        compiler_params=pltpu.CompilerParams(vmem_limit_bytes=limit << 20),
    )


def stage0(*args):
    wide, tall = (56, 128), (72, 128)
    scratch = [(2, 24) + tall, (2, 26) + tall, (2, 7) + wide, (6, 2, 24) + wide, (2, 24) + wide, (2, 24) + wide]
    scratch += [(2, 24) + tall, (2, 24) + tall, (2, 24) + wide, (2, 8, 64, 128)]
    return call(level0_kernel, [(16, 32, 128), (8, 24, 128), (8, 32, 128)], scratch, 36)(*args)


def stage1(*args):
    wide, tall = (24, 128), (40, 128)
    scratch = [(1, 18) + tall, (6, 1, 16) + wide, (1, 16) + wide, (1, 16) + wide]
    scratch += [(1, 16) + tall, (1, 16) + tall, (1, 16) + wide, (2, 4) + wide]
    return call(level1_kernel, [(8, 16, 128), (2, 8, 128)], scratch, 16)(*args)


def stage2(*args):
    wide, tall, wide3, tall3 = (64, 128), (80, 128), (32, 128), (48, 128)
    scratch = [(16,) + wide, (1, 18) + tall, (6, 1, 16) + wide, (1, 16) + wide, (1, 16) + wide]
    scratch += [(1, 18) + tall, (1, 18) + tall, (1, 16) + wide, (2, 8) + wide]
    scratch += [(1, 10) + tall3, (6, 1, 8) + wide3, (1, 10) + tall3, (1, 10) + tall3]
    scratch += [(1, 8) + wide3, (1, 8) + wide3, (2, 64, 128), (4, 16, 128), (8, 32, 128)]
    return call(finish_kernel, [(16, 32, 128)], scratch, 24)(*args)


def per_device(g, b):
    xl = ring(jnp.concatenate([g[-4:], b[-5:]]), "gx", 1)
    xh = ring(jnp.concatenate([g[:4], b[:5]]), "gx", -1)

    high, low = call(pack_kernel, [(7, 32, 128)] * 2, [], 16)(g, b, xl, xh)
    zl = ring(high, "gz", 1)
    zh = ring(low, "gz", -1)

    high, low = call(pack_y_kernel, [(Y_ROWS, 128)] * 2, [], 16)(g, b, xl, xh, zl, zh)
    yl = ring(high, "gy", 1)
    yh = ring(low, "gy", -1)
    x0, g1, b1 = stage0(g, b, xl, xh, yl, yh, zl, zh)

    def both(at4, at5):
        return jnp.concatenate([g1[at4].reshape(96, 128), b1[at5].reshape(160, 128)])

    xl = ring(both(slice(4, 8), slice(3, 8)), "gx", 1)
    xh = ring(both(slice(0, 4), slice(0, 5)), "gx", -1)
    x1, chunk = stage1(g1, b1, xl, xh)

    send = jnp.broadcast_to(chunk[None], (32, 2, 8, 128))
    slab = lax.all_to_all(send, ("gx", "gy"), 0, 0, tiled=False)
    high, low = call(pack_z_kernel, [(35, 8, 128)] * 2, [], 16)(slab)
    return stage2(slab, ring(high, "gz", 1), ring(low, "gz", -1), x0, x1)


def solution(mesh):
    placed = (P("gx", "gy", "gz"), P("gx", "gy", "gz"))
    return jax.shard_map(
        per_device, mesh=mesh, in_specs=placed, out_specs=P("gx", "gy", "gz"), check_vma=False
    )
```

```python
import jax
import jax.numpy as jnp
from jax import lax
from jax.experimental import pallas as pl
from jax.experimental.pallas import tpu as pltpu
from jax.sharding import PartitionSpec as P

LEVELS = 3
SWEEPS = 4
BOTTOM = 8

cheby_top = 2.0
smooth_low = 0.25
bottom_low = 0.02

F32 = jnp.float32


def chebyshev_terms(lower_bound, sweeps):
    middle = (cheby_top + lower_bound) / 2.0
    radius = (cheby_top - lower_bound) / 2.0
    sigma_ratio = middle / radius
    rho_old = 1.0 / sigma_ratio
    term_list = []
    for sweep_index in range(1, sweeps):
        rho_new = 1.0 / (2.0 * sigma_ratio - rho_old)
        term_list.append((rho_new * rho_old, 2.0 * rho_new / radius))
        rho_old = rho_new
    return (1.0 / middle, term_list)


def ring(values, axis, step):
    count = lax.axis_size(axis)
    return lax.ppermute(values, axis, [(i, (i + step) % count) for i in range(count)])


def iota(shape, axis):
    return lax.broadcasted_iota(jnp.int32, shape, axis)


def matrix(shape, hit, value):
    return jnp.where(hit(iota(shape, 0), iota(shape, 1)), F32(value), F32(0.0))


def product(left, right):
    parts, rest = [], left
    for _ in range(3):
        part = rest.astype(jnp.bfloat16)
        parts.append(part)
        rest = rest - part.astype(F32)
    right = right.astype(jnp.bfloat16)
    high, middle, low = (jnp.dot(p, right, preferred_element_type=F32) for p in parts)
    return high + (middle + low)


def beside(cols):
    low = [pltpu.roll(c, 1, 1) for c in cols]
    high = [pltpu.roll(c, 127, 1) for c in cols]
    if len(cols) == 2:
        lanes = iota(cols[0].shape, 1)
        first, last = lanes == 0, lanes == 127
        low = [jnp.where(first, low[1], low[0]), jnp.where(first, low[0], low[1])]
        high = [jnp.where(last, high[1], high[0]), jnp.where(last, high[0], high[1])]
    return low, high


def around(field, first, planes, row, count):
    cols = range(field.shape[0])
    here = [
        [field[c, first + p, pl.ds(8 + row, count), :] for c in cols] for p in range(-1, planes + 1)
    ]
    out = []
    for p in range(planes):
        low, high = beside(here[p + 1])
        out.append(
            [
                (
                    here[p + 1][c],
                    here[p][c],
                    here[p + 2][c],
                    field[c, first + p, pl.ds(7 + row, count), :],
                    field[c, first + p, pl.ds(9 + row, count), :],
                    low[c],
                    high[c],
                )
                for c in cols
            ]
        )
    return out


def sweep_planes(low, high, body, unroll):
    steps = (high - low) // unroll
    if steps > 1:

        def several(j, _):
            body(low + j * unroll, unroll)
            return 0

        lax.fori_loop(0, steps, several, 0)
        low = low + steps * unroll
    if high > low:
        body(low, high - low)


class Level:
    def __init__(self, rows, block, unroll, at, scale, low, sweeps, w, gh, d, va, vb, double):
        self.rows, self.block, self.unroll, self.at, self.scale = rows, block, unroll, at, scale
        self.initial, self.terms = chebyshev_terms(low, sweeps)
        self.w, self.gh, self.d, self.va, self.vb, self.double = w, gh, d, va, vb, double

    def blocks(self, first=0, last=None):
        last = self.rows if last is None else last
        return [(r, min(self.block, last - r)) for r in range(first, last, self.block)]

    def clear(self, planes):
        for ref in (self.va, self.vb):
            shape = ref.shape
            edge = jnp.zeros((shape[0], shape[1], 8, 128), F32)
            ref[:, :, 0:8, :] = edge
            ref[:, :, 8 + self.rows : 16 + self.rows, :] = edge
            for p in planes:
                ref[:, p] = jnp.zeros((shape[0],) + shape[2:], F32)

    def prepare(self, low, high, b, g, shift):
        def body(first, planes):
            for r, n in self.blocks():
                for p, fields in enumerate(around(b, first + shift, planes, r, n)):
                    i = first + p
                    for c, (bc, *near) in enumerate(fields):
                        double = 6.0 * bc + (
                            (near[0] + near[1]) + (near[2] + near[3]) + (near[4] + near[5])
                        )
                        inverse = jnp.where(bc > 0.0, 1.0 / double, 0.0)
                        for f in range(6):
                            self.w[f, c, i, pl.ds(r, n), :] = (bc + near[f]) * inverse
                        gh = g(c, i, r, n) * ((2.0 / self.scale) * inverse)
                        self.gh[c, i, pl.ds(r, n), :] = gh
                        self.va[c, i + self.at, pl.ds(8 + r, n), :] = gh * self.initial
                        if self.double is not None:
                            self.double[c, i, pl.ds(r, n), :] = (0.5 * self.scale) * double

        sweep_planes(low, high, body, self.unroll)

    def scaled_residual(self, v, first, planes, r, n):
        out = []
        for p, fields in enumerate(around(v, first + self.at, planes, r, n)):
            out.append([])
            for c, (vc, *near) in enumerate(fields):
                z = self.gh[c, first + p, pl.ds(r, n), :] - vc
                for f in range(6):
                    z = z + self.w[f, c, first + p, pl.ds(r, n), :] * near[f]
                out[-1].append((vc, z))
        return out

    def smooth(self, low, high, shrink):
        src, dst = self.va, self.vb
        for k, (carry, push) in enumerate(self.terms):
            low, high = low + shrink, high - shrink

            def body(first, planes, src=src, dst=dst, k=k, carry=carry, push=push):
                for r, n in self.blocks():
                    for p, got in enumerate(self.scaled_residual(src, first, planes, r, n)):
                        i = first + p
                        for c, (vc, z) in enumerate(got):
                            old = vc if k == 0 else self.d[c, i, pl.ds(r, n), :]
                            step = carry * old + push * z
                            if k < len(self.terms) - 1:
                                self.d[c, i, pl.ds(r, n), :] = step
                            dst[c, i + self.at, pl.ds(8 + r, n), :] = vc + step

            sweep_planes(low, high, body, self.unroll)
            src, dst = dst, src
        return src

    def residual_pairs(self, v, low, high, first, last, put):
        def body(j, pairs):
            i = low + 2 * j
            for r, n in self.blocks(first, last):
                got = self.scaled_residual(v, i, 2 * pairs, r, n)
                for p in range(pairs):
                    for c in range(len(got[0])):
                        total = None
                        for q in (2 * p, 2 * p + 1):
                            now = self.double[c, i + q, pl.ds(r, n), :] * got[q][c][1]
                            total = now if total is None else total + now
                        put(j + p, c, r, n, total)

        sweep_planes(0, (high - low) // 2, body, max(1, self.unroll // 2))


def flag(condition):
    return jnp.where(condition, F32(1.0), F32(0.0))


def plane_of(p, g, b, xl, xh):
    if p < 4:
        return xl[p]
    if p < 20:
        return g[p - 4]
    if p < 24:
        return xh[p - 20]
    if p < 29:
        return xl[p - 20]
    if p < 45:
        return b[p - 29]
    return xh[p - 41]


def pack_kernel(g, b, xl, xh, high, low):
    slot = iota((32, 128), 1) // 16
    for k in range(7):
        to_high = jnp.zeros((32, 128), F32)
        to_low = jnp.zeros((32, 128), F32)
        for s in range(8):
            p = 8 * k + s
            if p >= 50:
                break
            plane = plane_of(p, g, b, xl, xh)
            to_high = jnp.where(slot == s, pltpu.roll(plane, 16 * (s + 1) % 128, 1), to_high)
            to_low = jnp.where(slot == s, pltpu.roll(plane, 16 * s, 1) if s else plane, to_low)
        high[k] = to_high
        low[k] = to_low


INNER = 64
OUTER = list(range(1, 23)) + list(range(25, 49)) + list(range(50, 64))
LAST = list(range(29, 45))
OUTER_AT = 8 * INNER
LAST_AT = OUTER_AT + 4 * len(OUTER)
Y_ROWS = LAST_AT + len(LAST)


def pack_y_kernel(g, b, xl, xh, zl, zh, high, low):
    def plane(p):
        if p < 50:
            return plane_of(p, g, b, xl, xh)
        return zl[p - 50] if p < 57 else zh[p - 57]

    for p in range(INNER):
        here = plane(p)
        high[8 * p : 8 * p + 8, :] = here[24:32]
        low[8 * p : 8 * p + 8, :] = here[0:8]
    for i, p in enumerate(OUTER):
        here, at = plane(p), OUTER_AT + 4 * i
        high[at : at + 4, :] = here[20:24]
        low[at : at + 4, :] = here[8:12]
    for i, p in enumerate(LAST):
        here, at = plane(p), LAST_AT + i
        high[at : at + 1, :] = here[19:20]
        low[at : at + 1, :] = here[12:13]


def level0_kernel(g, b, xl, xh, yl, yh, zl, zh, x0, g1, b1, G, B, Z, W, GH, D2, VA, VB, DD, T):
    gx, gy, gz = lax.axis_index("gx"), lax.axis_index("gy"), lax.axis_index("gz")
    lanes = iota((56, 128), 1)
    rows = iota((56, 128), 0)
    y_low, y_high, x_low, x_high = flag(gy > 0), flag(gy < 7), flag(gx > 0), flag(gx < 3)
    lane_in = jnp.where(lanes < 16, flag(gz < 7), jnp.where(lanes >= 112, flag(gz > 0), F32(0.0)))
    lane_in = jnp.where(rows < 12, y_low, jnp.where(rows < 44, F32(1.0), y_high)) * lane_in
    blank4, blank8 = jnp.zeros((4, 128), F32), jnp.zeros((8, 128), F32)
    order = {p: i for i, p in enumerate(OUTER)}

    def outer(side, p):
        if p not in order:
            return blank4
        at = OUTER_AT + 4 * order[p]
        return side[at : at + 4, :]

    for side, source in ((0, zl), (1, zh)):
        for k in range(7):
            p = 50 + 7 * side + k
            Z[side, k, 0:4, :] = outer(yl, p)
            Z[side, k, 4:12, :] = yl[8 * p : 8 * p + 8, :]
            Z[side, k, 12:44, :] = source[k]
            Z[side, k, 44:52, :] = yh[8 * p : 8 * p + 8, :]
            Z[side, k, 52:56, :] = outer(yh, p)
    for p in range(50):
        k, s = p // 8, p % 8
        from_high = Z[1, k]
        from_high = pltpu.roll(from_high, 128 - 16 * s, 1) if s else from_high
        from_low = Z[0, k]
        from_low = pltpu.roll(from_low, 112 - 16 * s, 1) if s < 7 else from_low
        far = jnp.where(lanes < 16, from_high, from_low)
        own = plane_of(p, g, b, xl, xh)
        below, above = yl[8 * p : 8 * p + 8, :], yh[8 * p : 8 * p + 8, :]
        below4, above4 = outer(yl, p), outer(yh, p)
        field, q = (G, p) if p < 24 else (B, p - 24)
        if p >= 24:
            far = far * lane_in
            side = x_low if q < 5 else x_high if q >= 21 else None
            if side is not None:
                own, far = own * side, far * side
                below, below4 = below * (y_low * side), below4 * (y_low * side)
                above, above4 = above * (y_high * side), above4 * (y_high * side)
            else:
                below, below4 = below * y_low, below4 * y_low
                above, above4 = above * y_high, above4 * y_high
            field[0, q, 0:8, :] = blank8
            field[0, q, 64:72, :] = blank8
            field[1, q, 0:8, :] = blank8
            field[1, q, 64:72, :] = blank8
            if p in LAST:
                at = LAST_AT + LAST.index(p)
                field[0, q, 7:8, :] = yl[at : at + 1, :] * y_low
                field[0, q, 64:65, :] = yh[at : at + 1, :] * y_high
        field[0, q, 8:12, :] = below4
        field[0, q, 12:20, :] = below
        field[0, q, 20:52, :] = own
        field[0, q, 52:60, :] = above
        field[0, q, 60:64, :] = above4
        field[1, q, 8:64, :] = far

    level = Level(56, BLOCK0, UNROLL0, 0, 1.0, smooth_low, SWEEPS, W, GH, DD, VA, VB, D2)
    level.clear([])
    level.prepare(0, 24, B, lambda c, i, r, n: G[c, i, pl.ds(8 + r, n), :], 1)
    v = level.smooth(0, 24, 1)
    x0[...] = v[0, 4:20, 20:52, :]

    def put(j, c, r, n, total):
        T[c, j, pl.ds(r, n), :] = total

    level.residual_pairs(v, 4, 20, 4, 52, put)
    near_mat = matrix((128, 128), lambda a, c: a // 2 == c, 0.125)
    far_mat = matrix((128, 128), lambda a, c: a // 2 + 64 == c, 0.125)

    def halved(start, count):
        sums = []
        for c in range(2):
            even = T[c, :, pl.ds(start, count, stride=2), :]
            odd = T[c, :, pl.ds(start + 1, count, stride=2), :]
            sums.append((even + odd).reshape(8 * count, 128))
        total = product(sums[0], near_mat) + product(sums[1], far_mat)
        return total.reshape(8, count, 128)

    g1[...] = halved(4, 24)
    for c in range(2):
        for j in range(8):
            T[c, j, 4:60, :] = B[c, 5 + 2 * j, 8:64, :] + B[c, 6 + 2 * j, 8:64, :]
            T[c, j, 0:4, :] = blank4
            T[c, j, 60:64, :] = blank4
    b1[...] = halved(0, 32)


def level1_kernel(g, b, xl, xh, x1, chunk, B, W, GH, D2, VA, VB, DD, T):
    gx = lax.axis_index("gx")
    for q in range(5):
        B[0, q, 4:36, :] = xl[96 + 32 * q : 128 + 32 * q, :] * flag(gx > 0)
        B[0, 13 + q, 4:36, :] = xh[96 + 32 * q : 128 + 32 * q, :] * flag(gx < 3)
    for q in range(8):
        B[0, 5 + q, 4:36, :] = b[q]

    def source(c, i, r, n):
        if i < 4:
            return xl[24 * i + r : 24 * i + r + n, :]
        if i < 12:
            return g[i - 4, r : r + n, :]
        return xh[24 * (i - 12) + r : 24 * (i - 12) + r + n, :]

    level = Level(24, 24, 16, 0, 0.25, smooth_low, SWEEPS, W, GH, DD, VA, VB, D2)
    level.clear([])
    level.prepare(0, 16, B, source, 1)
    v = level.smooth(0, 16, 1)
    x1[...] = v[0, 4:12, 12:28, :]

    def put(j, c, r, n, total):
        T[0, j, pl.ds(r, n), :] = total

    level.residual_pairs(v, 4, 12, 0, 24, put)
    for q in range(4):
        T[1, q] = B[0, 5 + 2 * q, 8:32, :] + B[0, 6 + 2 * q, 8:32, :]
    both = T[:, :, pl.ds(4, 8, stride=2), :] + T[:, :, pl.ds(5, 8, stride=2), :]
    mat = matrix((128, 128), lambda a, c: (a < 64) & (a // 2 == c), 0.125)
    total = product(both.reshape(64, 128), mat).reshape(2, 4, 8, 128)
    for a in range(2):
        out = total[a, 0]
        for q in range(1, 4):
            out = out + pltpu.roll(total[a, q], 32 * q, 1)
        chunk[a] = out


def turn(v, shift):
    shift = shift % 128
    return pltpu.roll(v, shift, 1) if shift else v


def pack_z_kernel(slab, high, low):
    lanes = iota((8, 128), 1)
    first = lanes % 32 < 16
    for j in range(32):
        g, b = slab[j, 0], slab[j, 1]
        high[j] = jnp.where(first, turn(g, -16), b)
        low[j] = jnp.where(first, g, turn(b, 16))
    gy = lax.axis_index("gy")
    for d in range(3):
        by = jnp.clip(gy + d - 1, 0, 7)
        to_high = jnp.zeros((8, 128), F32)
        to_low = jnp.zeros((8, 128), F32)
        for n in range(8):
            here = slab[8 * (n // 2) + by, n % 2]
            mine = lanes % 32 // 4 == n
            to_high = jnp.where(mine, turn(here, 4 * n - 12), to_high)
            to_low = jnp.where(mine, turn(here, 4 * n - 16), to_low)
        high[32 + d] = to_high
        low[32 + d] = to_low


def finish_kernel(
    slab, zl, zh, x0, x1, out, G, B, W, GH, D2, VA, VB, DD, T, B3, W3, VA3, VB3, DD3, GH3, X3, E1, E0
):
    gx, gy, gz = lax.axis_index("gx"), lax.axis_index("gy"), lax.axis_index("gz")
    lanes = iota((8, 128), 1)
    zeros = jnp.zeros((8, 128), F32)
    lane_in = jnp.where(lanes < 32, F32(1.0), jnp.where(lanes < 64, flag(gz < 7), zeros))
    lane_in = jnp.where(lanes >= 96, flag(gz > 0), lane_in)

    for p in (0, 17):
        B[0, p] = jnp.zeros((80, 128), F32)
    B[0, :, 0:8, :] = jnp.zeros((18, 8, 128), F32)
    B[0, :, 72:80, :] = jnp.zeros((18, 8, 128), F32)
    for j in range(32):
        row = 8 * (j % 8)
        for q in range(4):
            plane = 4 * (j // 8) + q
            for a in range(2):
                own, left, right = slab[j, a], zl[j], zh[j]
                far = jnp.where(lanes < 48, turn(right, 32 - 16 * a - 32 * q), 0.0)
                far = jnp.where(lanes >= 112, turn(left, 112 - 16 * a - 32 * q), far)
                got = jnp.where(lanes < 32, turn(own, -32 * q), far)
                if a == 0:
                    G[plane, row : row + 8, :] = got
                else:
                    B[0, plane + 1, 8 + row : 16 + row, :] = got * lane_in
    low4, high4 = (lanes >= 108) & (lanes < 112), (lanes >= 48) & (lanes < 52)
    for d in range(3):
        row = pl.multiple_of(8 * jnp.clip(gy + d - 1, 0, 7), 8)
        left, right = zl[32 + d], zh[32 + d]
        for n in range(8):
            for q in range(4):
                plane = 4 * (n // 2) + q
                far = jnp.where(low4, turn(left, 108 - 32 * q - 4 * n), 0.0)
                far = jnp.where(high4, turn(right, 48 - 32 * q - 4 * n), far)
                if n % 2 == 0:
                    here = G[plane, pl.ds(row, 8), :]
                    G[plane, pl.ds(row, 8), :] = jnp.where(low4 | high4, far, here)
                else:
                    here = B[0, plane + 1, pl.ds(8 + row, 8), :]
                    far = jnp.where(low4 | high4, far * lane_in, here)
                    B[0, plane + 1, pl.ds(8 + row, 8), :] = far

    level = Level(64, BLOCK2, UNROLL2, 1, 0.25**2, smooth_low, SWEEPS, W, GH, DD, VA, VB, D2)
    level.clear([0, 17])
    level.prepare(0, 16, B, lambda c, i, r, n: G[i, pl.ds(r, n), :], 1)
    v = level.smooth(0, 16, 0)

    def put(j, c, r, n, total):
        T[0, j, pl.ds(r, n), :] = total

    level.residual_pairs(v, 0, 16, 0, 64, put)
    for j in range(8):
        T[1, j] = B[0, 1 + 2 * j, 8:72, :] + B[0, 2 + 2 * j, 8:72, :]
    both = T[:, :, pl.ds(0, 32, stride=2), :] + T[:, :, pl.ds(1, 32, stride=2), :]
    mat = matrix((128, 128), lambda a, c: a // 2 == c % 64, 0.125)
    coarse = product(both.reshape(512, 128), mat).reshape(2, 8, 32, 128)
    for p in (0, 9):
        B3[0, p] = jnp.zeros((48, 128), F32)
    B3[0, :, 0:8, :] = jnp.zeros((10, 8, 128), F32)
    B3[0, :, 40:48, :] = jnp.zeros((10, 8, 128), F32)
    B3[0, 1:9, 8:40, :] = coarse[1]

    base = Level(32, 32, 8, 1, 0.25**3, bottom_low, BOTTOM, W3, GH3, DD3, VA3, VB3, None)
    base.clear([0, 9])
    base.prepare(0, 8, B3, lambda c, i, r, n: coarse[0, i, r : r + n, :], 1)
    e3 = base.smooth(0, 8, 0)

    spread = matrix((128, 128), lambda a, c: a == c // 2, 1.0)
    for i in range(2):
        own = e3[0, 1 + 2 * gx + i, 8:40, :]
        X3[i, pl.ds(0, 32, stride=2), :] = own
        X3[i, pl.ds(1, 32, stride=2), :] = own
    row = pl.multiple_of(8 * gy, 8)
    up = product(X3[:, pl.ds(row, 8), :].reshape(16, 128), spread).reshape(2, 8, 128)
    e2 = [v[0, 1 + 4 * gx + i, pl.ds(8 + row, 8), :] + up[i // 2] for i in range(4)]
    up = product(jnp.concatenate(e2, axis=0), spread).reshape(4, 8, 128)
    for i in range(4):
        E1[i, pl.ds(0, 8, stride=2), :] = up[i]
        E1[i, pl.ds(1, 8, stride=2), :] = up[i]
    e1 = [x1[i] + E1[i // 2] for i in range(8)]
    up = product(jnp.concatenate(e1, axis=0), spread).reshape(8, 16, 128)
    for i in range(8):
        E0[i, pl.ds(0, 16, stride=2), :] = up[i]
        E0[i, pl.ds(1, 16, stride=2), :] = up[i]
        out[2 * i] = x0[2 * i] + E0[i]
        out[2 * i + 1] = x0[2 * i + 1] + E0[i]


BLOCK0, UNROLL0, BLOCK2, UNROLL2 = 8, 8, 64, 16


def call(kernel, outs, scratch, limit):
    many = len(outs) > 1
    shapes = [jax.ShapeDtypeStruct(s, F32) for s in outs]
    return pl.pallas_call(
        kernel,
        out_shape=shapes if many else shapes[0],
        scratch_shapes=[pltpu.VMEM(s, F32) for s in scratch],
        compiler_params=pltpu.CompilerParams(vmem_limit_bytes=limit << 20),
    )


def stage0(*args):
    wide, tall = (56, 128), (72, 128)
    scratch = [(2, 24) + tall, (2, 26) + tall, (2, 7) + wide, (6, 2, 24) + wide, (2, 24) + wide, (2, 24) + wide]
    scratch += [(2, 24) + tall, (2, 24) + tall, (2, 24) + wide, (2, 8, 64, 128)]
    return call(level0_kernel, [(16, 32, 128), (8, 24, 128), (8, 32, 128)], scratch, 36)(*args)


def stage1(*args):
    wide, tall = (24, 128), (40, 128)
    scratch = [(1, 18) + tall, (6, 1, 16) + wide, (1, 16) + wide, (1, 16) + wide]
    scratch += [(1, 16) + tall, (1, 16) + tall, (1, 16) + wide, (2, 4) + wide]
    return call(level1_kernel, [(8, 16, 128), (2, 8, 128)], scratch, 16)(*args)


def stage2(*args):
    wide, tall, wide3, tall3 = (64, 128), (80, 128), (32, 128), (48, 128)
    scratch = [(16,) + wide, (1, 18) + tall, (6, 1, 16) + wide, (1, 16) + wide, (1, 16) + wide]
    scratch += [(1, 18) + tall, (1, 18) + tall, (1, 16) + wide, (2, 8) + wide]
    scratch += [(1, 10) + tall3, (6, 1, 8) + wide3, (1, 10) + tall3, (1, 10) + tall3]
    scratch += [(1, 8) + wide3, (1, 8) + wide3, (2, 64, 128), (4, 16, 128), (8, 32, 128)]
    return call(finish_kernel, [(16, 32, 128)], scratch, 24)(*args)


def per_device(g, b):
    xl = ring(jnp.concatenate([g[-4:], b[-5:]]), "gx", 1)
    xh = ring(jnp.concatenate([g[:4], b[:5]]), "gx", -1)

    high, low = call(pack_kernel, [(7, 32, 128)] * 2, [], 16)(g, b, xl, xh)
    zl = ring(high, "gz", 1)
    zh = ring(low, "gz", -1)

    high, low = call(pack_y_kernel, [(Y_ROWS, 128)] * 2, [], 16)(g, b, xl, xh, zl, zh)
    yl = ring(high, "gy", 1)
    yh = ring(low, "gy", -1)
    x0, g1, b1 = stage0(g, b, xl, xh, yl, yh, zl, zh)

    def both(at4, at5):
        return jnp.concatenate([g1[at4].reshape(96, 128), b1[at5].reshape(160, 128)])

    xl = ring(both(slice(4, 8), slice(3, 8)), "gx", 1)
    xh = ring(both(slice(0, 4), slice(0, 5)), "gx", -1)
    x1, chunk = stage1(g1, b1, xl, xh)

    send = jnp.broadcast_to(chunk[None], (32, 2, 8, 128))
    slab = lax.all_to_all(send, ("gx", "gy"), 0, 0, tiled=False)
    high, low = call(pack_z_kernel, [(35, 8, 128)] * 2, [], 16)(slab)
    return stage2(slab, ring(high, "gz", 1), ring(low, "gz", -1), x0, x1)


def solution(mesh):
    placed = (P("gx", "gy", "gz"), P("gx", "gy", "gz"))
    return jax.shard_map(
        per_device, mesh=mesh, in_specs=placed, out_specs=P("gx", "gy", "gz"), check_vma=False
    )
```

```python
import jax
import jax.numpy as jnp
from jax import lax
from jax.experimental import pallas as pl
from jax.experimental.pallas import tpu as pltpu
from jax.sharding import PartitionSpec as P

LEVELS = 3
SWEEPS = 4
BOTTOM = 8

cheby_top = 2.0
smooth_low = 0.25
bottom_low = 0.02

F32 = jnp.float32


def chebyshev_terms(lower_bound, sweeps):
    middle = (cheby_top + lower_bound) / 2.0
    radius = (cheby_top - lower_bound) / 2.0
    sigma_ratio = middle / radius
    rho_old = 1.0 / sigma_ratio
    term_list = []
    for sweep_index in range(1, sweeps):
        rho_new = 1.0 / (2.0 * sigma_ratio - rho_old)
        term_list.append((rho_new * rho_old, 2.0 * rho_new / radius))
        rho_old = rho_new
    return (1.0 / middle, term_list)


def ring(values, axis, step):
    count = lax.axis_size(axis)
    return lax.ppermute(values, axis, [(i, (i + step) % count) for i in range(count)])


def iota(shape, axis):
    return lax.broadcasted_iota(jnp.int32, shape, axis)


def matrix(shape, hit, value):
    return jnp.where(hit(iota(shape, 0), iota(shape, 1)), F32(value), F32(0.0))


def product(left, right):
    parts, rest = [], left
    for _ in range(3):
        part = rest.astype(jnp.bfloat16)
        parts.append(part)
        rest = rest - part.astype(F32)
    right = right.astype(jnp.bfloat16)
    high, middle, low = (jnp.dot(p, right, preferred_element_type=F32) for p in parts)
    return high + (middle + low)


def beside(cols):
    low = [pltpu.roll(c, 1, 1) for c in cols]
    high = [pltpu.roll(c, 127, 1) for c in cols]
    if len(cols) == 2:
        lanes = iota(cols[0].shape, 1)
        first, last = lanes == 0, lanes == 127
        low = [jnp.where(first, low[1], low[0]), jnp.where(first, low[0], low[1])]
        high = [jnp.where(last, high[1], high[0]), jnp.where(last, high[0], high[1])]
    return low, high


def around(field, first, planes, row, count):
    cols = range(field.shape[0])
    here = [
        [field[c, first + p, pl.ds(8 + row, count), :] for c in cols] for p in range(-1, planes + 1)
    ]
    out = []
    for p in range(planes):
        low, high = beside(here[p + 1])
        out.append(
            [
                (
                    here[p + 1][c],
                    here[p][c],
                    here[p + 2][c],
                    field[c, first + p, pl.ds(7 + row, count), :],
                    field[c, first + p, pl.ds(9 + row, count), :],
                    low[c],
                    high[c],
                )
                for c in cols
            ]
        )
    return out


def sweep_planes(low, high, body, unroll):
    steps = (high - low) // unroll
    if steps > 1:

        def several(j, _):
            body(low + j * unroll, unroll)
            return 0

        lax.fori_loop(0, steps, several, 0)
        low = low + steps * unroll
    if high > low:
        body(low, high - low)


class Level:
    def __init__(self, rows, block, unroll, at, scale, low, sweeps, w, gh, d, va, vb, double):
        self.rows, self.block, self.unroll, self.at, self.scale = rows, block, unroll, at, scale
        self.initial, self.terms = chebyshev_terms(low, sweeps)
        self.w, self.gh, self.d, self.va, self.vb, self.double = w, gh, d, va, vb, double
        self.spans = [(0, rows)]

    def blocks(self, spans=None):
        return [at for span in spans or self.spans for at in self.cut(*span)]

    def cut(self, first, last):
        return [(r, min(self.block, last - r)) for r in range(first, last, self.block)]

    def clear(self, planes):
        for ref in (self.va, self.vb):
            shape = ref.shape
            edge = jnp.zeros((shape[0], shape[1], 8, 128), F32)
            ref[:, :, 0:8, :] = edge
            ref[:, :, 8 + self.rows : 16 + self.rows, :] = edge
            for p in planes:
                ref[:, p] = jnp.zeros((shape[0],) + shape[2:], F32)

    def prepare(self, low, high, b, g, shift):
        def body(first, planes):
            for r, n in self.blocks():
                for p, fields in enumerate(around(b, first + shift, planes, r, n)):
                    i = first + p
                    for c, (bc, *near) in enumerate(fields):
                        double = 6.0 * bc + (
                            (near[0] + near[1]) + (near[2] + near[3]) + (near[4] + near[5])
                        )
                        inverse = jnp.where(bc > 0.0, 1.0 / double, 0.0)
                        for f in range(6):
                            self.w[f, c, i, pl.ds(r, n), :] = (bc + near[f]) * inverse
                        gh = g(c, i, r, n) * ((2.0 / self.scale) * inverse)
                        self.gh[c, i, pl.ds(r, n), :] = gh
                        self.va[c, i + self.at, pl.ds(8 + r, n), :] = gh * self.initial
                        if self.double is not None:
                            self.double[c, i, pl.ds(r, n), :] = (0.5 * self.scale) * double

        sweep_planes(low, high, body, self.unroll)

    def scaled_residual(self, v, first, planes, r, n):
        out = []
        for p, fields in enumerate(around(v, first + self.at, planes, r, n)):
            out.append([])
            for c, (vc, *near) in enumerate(fields):
                z = self.gh[c, first + p, pl.ds(r, n), :] - vc
                for f in range(6):
                    z = z + self.w[f, c, first + p, pl.ds(r, n), :] * near[f]
                out[-1].append((vc, z))
        return out

    def smooth(self, low, high, shrink, meet=None):
        src, dst = self.va, self.vb
        for k, (carry, push) in enumerate(self.terms):
            if meet is not None:
                meet(k, src)
            low, high = low + shrink, high - shrink

            def body(first, planes, src=src, dst=dst, k=k, carry=carry, push=push):
                for r, n in self.blocks():
                    for p, got in enumerate(self.scaled_residual(src, first, planes, r, n)):
                        i = first + p
                        for c, (vc, z) in enumerate(got):
                            old = vc if k == 0 else self.d[c, i, pl.ds(r, n), :]
                            step = carry * old + push * z
                            if k < len(self.terms) - 1:
                                self.d[c, i, pl.ds(r, n), :] = step
                            dst[c, i + self.at, pl.ds(8 + r, n), :] = vc + step

            sweep_planes(low, high, body, self.unroll)
            src, dst = dst, src
        if meet is not None:
            meet(len(self.terms), src)
        return src

    def residual_pairs(self, v, low, high, spans, put):
        def body(j, pairs):
            i = low + 2 * j
            for r, n in self.blocks(spans):
                got = self.scaled_residual(v, i, 2 * pairs, r, n)
                for p in range(pairs):
                    for c in range(len(got[0])):
                        total = None
                        for q in (2 * p, 2 * p + 1):
                            now = self.double[c, i + q, pl.ds(r, n), :] * got[q][c][1]
                            total = now if total is None else total + now
                        put(j + p, c, r, n, total)

        sweep_planes(0, (high - low) // 2, body, max(1, self.unroll // 2))


def flag(condition):
    return jnp.where(condition, F32(1.0), F32(0.0))


def plane_of(p, g, b, xl, xh):
    if p < 4:
        return xl[p]
    if p < 20:
        return g[p - 4]
    if p < 24:
        return xh[p - 20]
    if p < 29:
        return xl[p - 20]
    if p < 45:
        return b[p - 29]
    return xh[p - 41]


def pack_kernel(g, b, xl, xh, high, low):
    slot = iota((32, 128), 1) // 16
    for k in range(7):
        to_high = jnp.zeros((32, 128), F32)
        to_low = jnp.zeros((32, 128), F32)
        for s in range(8):
            p = 8 * k + s
            if p >= 50:
                break
            plane = plane_of(p, g, b, xl, xh)
            to_high = jnp.where(slot == s, pltpu.roll(plane, 16 * (s + 1) % 128, 1), to_high)
            to_low = jnp.where(slot == s, pltpu.roll(plane, 16 * s, 1) if s else plane, to_low)
        high[k] = to_high
        low[k] = to_low


INNER = 64
OUTER = list(range(1, 23)) + list(range(25, 49)) + list(range(50, 64))
LAST = list(range(29, 45))
OUTER_AT = 8 * INNER
LAST_AT = OUTER_AT + 4 * len(OUTER)
Y_ROWS = LAST_AT + len(LAST)


def pack_y_kernel(g, b, xl, xh, zl, zh, high, low):
    def plane(p):
        if p < 50:
            return plane_of(p, g, b, xl, xh)
        return zl[p - 50] if p < 57 else zh[p - 57]

    for p in range(INNER):
        here = plane(p)
        high[8 * p : 8 * p + 8, :] = here[24:32]
        low[8 * p : 8 * p + 8, :] = here[0:8]
    for i, p in enumerate(OUTER):
        here, at = plane(p), OUTER_AT + 4 * i
        high[at : at + 4, :] = here[20:24]
        low[at : at + 4, :] = here[8:12]
    for i, p in enumerate(LAST):
        here, at = plane(p), LAST_AT + i
        high[at : at + 1, :] = here[19:20]
        low[at : at + 1, :] = here[12:13]


def side_of(p, x_low, x_high):
    return x_low if p < 29 else x_high if p >= 45 else None


def times(factor, *values):
    return values if factor is None else tuple(factor * v for v in values)


def unpack(low, high, p, lanes):
    s = p % 8
    from_high = pltpu.roll(high, 128 - 16 * s, 1) if s else high
    from_low = pltpu.roll(low, 112 - 16 * s, 1) if s < 7 else low
    return jnp.where(lanes < 16, from_high, from_low)


def halved(pairs, count):
    near_mat = matrix((128, 128), lambda a, c: a // 2 == c, 0.125)
    far_mat = matrix((128, 128), lambda a, c: a // 2 + 64 == c, 0.125)
    sums = []
    for c in range(2):
        even = pairs[c, :, pl.ds(0, count, stride=2), :]
        odd = pairs[c, :, pl.ds(1, count, stride=2), :]
        sums.append((even + odd).reshape(8 * count, 128))
    total = product(sums[0], near_mat) + product(sums[1], far_mat)
    return total.reshape(8, count, 128)


def middle_kernel(g, b, xl, xh, zl, zh, x4, rm, b1, VE, WE, GE, DE, G, B, W, GH, D2, VA, VB, DD, T):
    gx, gz = lax.axis_index("gx"), lax.axis_index("gz")
    lanes = iota((32, 128), 1)
    lane_in = jnp.where(lanes < 16, flag(gz < 7), jnp.where(lanes >= 112, flag(gz > 0), F32(0.0)))
    x_low, x_high = flag(gx > 0), flag(gx < 3)
    spare = jnp.zeros((2, 26, 8, 128), F32)
    B[:, :, 0:8, :] = spare
    B[:, :, 40:48, :] = spare
    for p in range(50):
        far = unpack(zl[p // 8], zh[p // 8], p, lanes)
        own = plane_of(p, g, b, xl, xh)
        if p < 24:
            G[0, p] = own
            G[1, p] = far
        else:
            own, far = times(side_of(p, x_low, x_high), own, far * lane_in)
            B[0, p - 24, 8:40, :] = own
            B[1, p - 24, 8:40, :] = far

    level = Level(32, BLOCK0, UNROLL0, 0, 1.0, smooth_low, SWEEPS, W, GH, DD, VA, VB, D2)
    level.clear([])
    level.prepare(0, 24, B, lambda c, i, r, n: G[c, i, pl.ds(r, n), :], 1)

    def keep(k, v):
        VE[k, :, :, 0:8, :] = v[:, :, 12:20, :]
        VE[k, :, :, 8:16, :] = v[:, :, 28:36, :]

    v = level.smooth(0, 24, 1, keep)
    x4[...] = v[0, 4:20, 12:36, :]

    def put(j, c, r, n, total):
        rm[c, j, pl.ds(r - 8, n), :] = total

    level.residual_pairs(v, 4, 20, [(8, 24)], put)
    for to, ref in ((WE, W), (GE, GH), (DE, D2)):
        to[..., 0:8, :] = ref[..., 4:20, 4:12, :]
        to[..., 8:16, :] = ref[..., 4:20, 20:28, :]
    for c in range(2):
        for j in range(8):
            T[c, j] = B[c, 5 + 2 * j, 8:40, :] + B[c, 6 + 2 * j, 8:40, :]
    b1[...] = halved(T, 16)


def ends_kernel(
    g, b, xl, xh, yl, yh, zl, zh, x4, rm, bm, VE, WE, GE, DE, x0, g1, b1,
    G, B, Z, W, GH, D2, VA, VB, DD, T,
):
    gx, gy, gz = lax.axis_index("gx"), lax.axis_index("gy"), lax.axis_index("gz")
    lanes = iota((48, 128), 1)
    rows = iota((48, 128), 0)
    y_low, y_high, x_low, x_high = flag(gy > 0), flag(gy < 7), flag(gx > 0), flag(gx < 3)
    lane_in = jnp.where(lanes < 16, flag(gz < 7), jnp.where(lanes >= 112, flag(gz > 0), F32(0.0)))
    lane_in = jnp.where(rows < 12, y_low, jnp.where(rows < 36, F32(1.0), y_high)) * lane_in
    blank4, blank8 = jnp.zeros((4, 128), F32), jnp.zeros((8, 128), F32)
    order = {p: i for i, p in enumerate(OUTER)}

    def outer(side, p):
        if p not in order:
            return blank4
        at = OUTER_AT + 4 * order[p]
        return side[at : at + 4, :]

    for side, source in ((0, zl), (1, zh)):
        for k in range(7):
            p = 50 + 7 * side + k
            Z[side, k, 0:4, :] = outer(yl, p)
            Z[side, k, 4:12, :] = yl[8 * p : 8 * p + 8, :]
            Z[side, k, 12:20, :] = source[k, 0:8]
            Z[side, k, 20:28, :] = blank8
            Z[side, k, 28:36, :] = source[k, 24:32]
            Z[side, k, 36:44, :] = yh[8 * p : 8 * p + 8, :]
            Z[side, k, 44:48, :] = outer(yh, p)
    for p in range(50):
        far = unpack(Z[0, p // 8], Z[1, p // 8], p, lanes)
        own = plane_of(p, g, b, xl, xh)
        first, last = own[0:8], own[24:32]
        below, above = yl[8 * p : 8 * p + 8, :], yh[8 * p : 8 * p + 8, :]
        below4, above4 = outer(yl, p), outer(yh, p)
        field, q = (G, p) if p < 24 else (B, p - 24)
        if p >= 24:
            side = side_of(p, x_low, x_high)
            first, last, far = times(side, first, last, far * lane_in)
            below, below4 = times(side, below * y_low, below4 * y_low)
            above, above4 = times(side, above * y_high, above4 * y_high)
            for c in range(2):
                field[c, q, 0:8, :] = blank8
                field[c, q, 56:64, :] = blank8
            if p in LAST:
                at = LAST_AT + LAST.index(p)
                field[0, q, 7:8, :] = yl[at : at + 1, :] * y_low
                field[0, q, 56:57, :] = yh[at : at + 1, :] * y_high
        field[0, q, 8:12, :] = below4
        field[0, q, 12:20, :] = below
        field[0, q, 20:28, :] = first
        field[0, q, 36:44, :] = last
        field[0, q, 44:52, :] = above
        field[0, q, 52:56, :] = above4
        field[1, q, 8:56, :] = far

    level = Level(48, BLOCK0, UNROLL0, 0, 1.0, smooth_low, SWEEPS, W, GH, DD, VA, VB, D2)
    level.spans = [(0, 16), (32, 48)]
    level.clear([])
    level.prepare(0, 24, B, lambda c, i, r, n: G[c, i, pl.ds(8 + r, n), :], 1)
    for to, ref in ((W, WE), (GH, GE), (D2, DE)):
        to[..., 4:20, 16:32, :] = ref[...]

    def join(k, v):
        v[:, :, 24:40, :] = VE[k]

    v = level.smooth(0, 24, 1, join)
    x0[:, 0:4, :] = v[0, 4:20, 20:24, :]
    x0[:, 4:28, :] = x4[...]
    x0[:, 28:32, :] = v[0, 4:20, 40:44, :]

    def put(j, c, r, n, total):
        T[c, j, pl.ds(r - 4 if r < 24 else r + 4, n), :] = total

    level.residual_pairs(v, 4, 20, [(4, 20), (28, 44)], put)
    T[:, :, 16:32, :] = rm[...]
    g1[...] = halved(T, 24)
    for c in range(2):
        for j in range(8):
            low, high = 5 + 2 * j, 6 + 2 * j
            T[c, j, 0:4, :] = blank4
            T[c, j, 4:16, :] = B[c, low, 8:20, :] + B[c, high, 8:20, :]
            T[c, j, 16:28, :] = B[c, low, 44:56, :] + B[c, high, 44:56, :]
            T[c, j, 28:32, :] = blank4
    both = halved(T, 16)
    b1[:, 0:8, :] = both[:, 0:8]
    b1[:, 8:24, :] = bm[...]
    b1[:, 24:32, :] = both[:, 8:16]


def level1_kernel(g, b, xl, xh, x1, chunk, B, W, GH, D2, VA, VB, DD, T):
    gx = lax.axis_index("gx")
    for q in range(5):
        B[0, q, 4:36, :] = xl[96 + 32 * q : 128 + 32 * q, :] * flag(gx > 0)
        B[0, 13 + q, 4:36, :] = xh[96 + 32 * q : 128 + 32 * q, :] * flag(gx < 3)
    for q in range(8):
        B[0, 5 + q, 4:36, :] = b[q]

    def source(c, i, r, n):
        if i < 4:
            return xl[24 * i + r : 24 * i + r + n, :]
        if i < 12:
            return g[i - 4, r : r + n, :]
        return xh[24 * (i - 12) + r : 24 * (i - 12) + r + n, :]

    level = Level(24, 24, 16, 0, 0.25, smooth_low, SWEEPS, W, GH, DD, VA, VB, D2)
    level.clear([])
    level.prepare(0, 16, B, source, 1)
    v = level.smooth(0, 16, 1)
    x1[...] = v[0, 4:12, 12:28, :]

    def put(j, c, r, n, total):
        T[0, j, pl.ds(r, n), :] = total

    level.residual_pairs(v, 4, 12, None, put)
    for q in range(4):
        T[1, q] = B[0, 5 + 2 * q, 8:32, :] + B[0, 6 + 2 * q, 8:32, :]
    both = T[:, :, pl.ds(4, 8, stride=2), :] + T[:, :, pl.ds(5, 8, stride=2), :]
    mat = matrix((128, 128), lambda a, c: (a < 64) & (a // 2 == c), 0.125)
    total = product(both.reshape(64, 128), mat).reshape(2, 4, 8, 128)
    for a in range(2):
        out = total[a, 0]
        for q in range(1, 4):
            out = out + pltpu.roll(total[a, q], 32 * q, 1)
        chunk[a] = out


def turn(v, shift):
    shift = shift % 128
    return pltpu.roll(v, shift, 1) if shift else v


def pack_z_kernel(slab, high, low):
    lanes = iota((8, 128), 1)
    first = lanes % 32 < 16
    for j in range(32):
        g, b = slab[j, 0], slab[j, 1]
        high[j] = jnp.where(first, turn(g, -16), b)
        low[j] = jnp.where(first, g, turn(b, 16))
    gy = lax.axis_index("gy")
    for d in range(3):
        by = jnp.clip(gy + d - 1, 0, 7)
        to_high = jnp.zeros((8, 128), F32)
        to_low = jnp.zeros((8, 128), F32)
        for n in range(8):
            here = slab[8 * (n // 2) + by, n % 2]
            mine = lanes % 32 // 4 == n
            to_high = jnp.where(mine, turn(here, 4 * n - 12), to_high)
            to_low = jnp.where(mine, turn(here, 4 * n - 16), to_low)
        high[32 + d] = to_high
        low[32 + d] = to_low


def finish_kernel(
    slab, zl, zh, x0, x1, out, G, B, W, GH, D2, VA, VB, DD, T, B3, W3, VA3, VB3, DD3, GH3, X3, E1, E0
):
    gx, gy, gz = lax.axis_index("gx"), lax.axis_index("gy"), lax.axis_index("gz")
    lanes = iota((8, 128), 1)
    zeros = jnp.zeros((8, 128), F32)
    lane_in = jnp.where(lanes < 32, F32(1.0), jnp.where(lanes < 64, flag(gz < 7), zeros))
    lane_in = jnp.where(lanes >= 96, flag(gz > 0), lane_in)

    for p in (0, 17):
        B[0, p] = jnp.zeros((80, 128), F32)
    B[0, :, 0:8, :] = jnp.zeros((18, 8, 128), F32)
    B[0, :, 72:80, :] = jnp.zeros((18, 8, 128), F32)
    for j in range(32):
        row = 8 * (j % 8)
        for q in range(4):
            plane = 4 * (j // 8) + q
            for a in range(2):
                own, left, right = slab[j, a], zl[j], zh[j]
                far = jnp.where(lanes < 48, turn(right, 32 - 16 * a - 32 * q), 0.0)
                far = jnp.where(lanes >= 112, turn(left, 112 - 16 * a - 32 * q), far)
                got = jnp.where(lanes < 32, turn(own, -32 * q), far)
                if a == 0:
                    G[plane, row : row + 8, :] = got
                else:
                    B[0, plane + 1, 8 + row : 16 + row, :] = got * lane_in
    low4, high4 = (lanes >= 108) & (lanes < 112), (lanes >= 48) & (lanes < 52)
    for d in range(3):
        row = pl.multiple_of(8 * jnp.clip(gy + d - 1, 0, 7), 8)
        left, right = zl[32 + d], zh[32 + d]
        for n in range(8):
            for q in range(4):
                plane = 4 * (n // 2) + q
                far = jnp.where(low4, turn(left, 108 - 32 * q - 4 * n), 0.0)
                far = jnp.where(high4, turn(right, 48 - 32 * q - 4 * n), far)
                if n % 2 == 0:
                    here = G[plane, pl.ds(row, 8), :]
                    G[plane, pl.ds(row, 8), :] = jnp.where(low4 | high4, far, here)
                else:
                    here = B[0, plane + 1, pl.ds(8 + row, 8), :]
                    far = jnp.where(low4 | high4, far * lane_in, here)
                    B[0, plane + 1, pl.ds(8 + row, 8), :] = far

    level = Level(64, BLOCK2, UNROLL2, 1, 0.25**2, smooth_low, SWEEPS, W, GH, DD, VA, VB, D2)
    level.clear([0, 17])
    level.prepare(0, 16, B, lambda c, i, r, n: G[i, pl.ds(r, n), :], 1)
    v = level.smooth(0, 16, 0)

    def put(j, c, r, n, total):
        T[0, j, pl.ds(r, n), :] = total

    level.residual_pairs(v, 0, 16, None, put)
    for j in range(8):
        T[1, j] = B[0, 1 + 2 * j, 8:72, :] + B[0, 2 + 2 * j, 8:72, :]
    both = T[:, :, pl.ds(0, 32, stride=2), :] + T[:, :, pl.ds(1, 32, stride=2), :]
    mat = matrix((128, 128), lambda a, c: a // 2 == c % 64, 0.125)
    coarse = product(both.reshape(512, 128), mat).reshape(2, 8, 32, 128)
    for p in (0, 9):
        B3[0, p] = jnp.zeros((48, 128), F32)
    B3[0, :, 0:8, :] = jnp.zeros((10, 8, 128), F32)
    B3[0, :, 40:48, :] = jnp.zeros((10, 8, 128), F32)
    B3[0, 1:9, 8:40, :] = coarse[1]

    base = Level(32, 32, 8, 1, 0.25**3, bottom_low, BOTTOM, W3, GH3, DD3, VA3, VB3, None)
    base.clear([0, 9])
    base.prepare(0, 8, B3, lambda c, i, r, n: coarse[0, i, r : r + n, :], 1)
    e3 = base.smooth(0, 8, 0)

    spread = matrix((128, 128), lambda a, c: a == c // 2, 1.0)
    for i in range(2):
        own = e3[0, 1 + 2 * gx + i, 8:40, :]
        X3[i, pl.ds(0, 32, stride=2), :] = own
        X3[i, pl.ds(1, 32, stride=2), :] = own
    row = pl.multiple_of(8 * gy, 8)
    up = product(X3[:, pl.ds(row, 8), :].reshape(16, 128), spread).reshape(2, 8, 128)
    e2 = [v[0, 1 + 4 * gx + i, pl.ds(8 + row, 8), :] + up[i // 2] for i in range(4)]
    up = product(jnp.concatenate(e2, axis=0), spread).reshape(4, 8, 128)
    for i in range(4):
        E1[i, pl.ds(0, 8, stride=2), :] = up[i]
        E1[i, pl.ds(1, 8, stride=2), :] = up[i]
    e1 = [x1[i] + E1[i // 2] for i in range(8)]
    up = product(jnp.concatenate(e1, axis=0), spread).reshape(8, 16, 128)
    for i in range(8):
        E0[i, pl.ds(0, 16, stride=2), :] = up[i]
        E0[i, pl.ds(1, 16, stride=2), :] = up[i]
        out[2 * i] = x0[2 * i] + E0[i]
        out[2 * i + 1] = x0[2 * i + 1] + E0[i]


BLOCK0, UNROLL0, BLOCK2, UNROLL2 = 8, 8, 64, 16


def call(kernel, outs, scratch, limit, us=1):
    many = len(outs) > 1
    shapes = [jax.ShapeDtypeStruct(s, F32) for s in outs]
    return pl.pallas_call(
        kernel,
        out_shape=shapes if many else shapes[0],
        scratch_shapes=[pltpu.VMEM(s, F32) for s in scratch],
        compiler_params=pltpu.CompilerParams(vmem_limit_bytes=limit << 20),
        cost_estimate=pl.CostEstimate(
            flops=us * 1000000, bytes_accessed=us * 3600000, transcendentals=0
        ),
    )


def stage0a(*args):
    wide, tall = (32, 128), (48, 128)
    outs = [(16, 24, 128), (2, 8, 16, 128), (8, 16, 128), (4, 2, 24, 16, 128)]
    outs += [(6, 2, 16, 16, 128), (2, 16, 16, 128), (2, 16, 16, 128)]
    scratch = [(2, 24) + wide, (2, 26) + tall, (6, 2, 24) + wide, (2, 24) + wide, (2, 24) + wide]
    scratch += [(2, 24) + tall, (2, 24) + tall, (2, 24) + wide, (2, 8) + wide]
    return call(middle_kernel, outs, scratch, 20, 4)(*args)


def stage0b(*args):
    wide, tall = (48, 128), (64, 128)
    scratch = [(2, 24) + tall, (2, 26) + tall, (2, 7) + wide, (6, 2, 24) + wide]
    scratch += [(2, 24) + wide, (2, 24) + wide]
    scratch += [(2, 24) + tall, (2, 24) + tall, (2, 24) + wide, (2, 8) + wide]
    outs = [(16, 32, 128), (8, 24, 128), (8, 32, 128)]
    return call(ends_kernel, outs, scratch, 28)(*args)


def stage1(*args):
    wide, tall = (24, 128), (40, 128)
    scratch = [(1, 18) + tall, (6, 1, 16) + wide, (1, 16) + wide, (1, 16) + wide]
    scratch += [(1, 16) + tall, (1, 16) + tall, (1, 16) + wide, (2, 4) + wide]
    return call(level1_kernel, [(8, 16, 128), (2, 8, 128)], scratch, 16)(*args)


def stage2(*args):
    wide, tall, wide3, tall3 = (64, 128), (80, 128), (32, 128), (48, 128)
    scratch = [(16,) + wide, (1, 18) + tall, (6, 1, 16) + wide, (1, 16) + wide, (1, 16) + wide]
    scratch += [(1, 18) + tall, (1, 18) + tall, (1, 16) + wide, (2, 8) + wide]
    scratch += [(1, 10) + tall3, (6, 1, 8) + wide3, (1, 10) + tall3, (1, 10) + tall3]
    scratch += [(1, 8) + wide3, (1, 8) + wide3, (2, 64, 128), (4, 16, 128), (8, 32, 128)]
    return call(finish_kernel, [(16, 32, 128)], scratch, 24)(*args)


def load_kernel(g, b, gv, bv, high, low, sems):
    moves = [
        (g.at[12:16], high.at[0:4]),
        (b.at[11:16], high.at[4:9]),
        (g.at[0:4], low.at[0:4]),
        (b.at[0:5], low.at[4:9]),
        (g, gv),
        (b, bv),
    ]
    copies = [pltpu.make_async_copy(a, c, sems.at[i]) for i, (a, c) in enumerate(moves)]
    for copy in copies:
        copy.start()
    for copy in copies:
        copy.wait()


def load(g, b):
    whole, ends = pltpu.VMEM((16, 32, 128), F32), pltpu.VMEM((9, 32, 128), F32)
    return pl.pallas_call(
        load_kernel,
        out_shape=[whole, whole, ends, ends],
        in_specs=[pl.BlockSpec(memory_space=pltpu.HBM)] * 2,
        scratch_shapes=[pltpu.SemaphoreType.DMA((6,))],
        compiler_params=pltpu.CompilerParams(vmem_limit_bytes=60 << 20),
    )(g, b)


def per_device(g, b):
    g, b, high, low = load(g, b)
    xl = ring(high, "gx", 1)
    xh = ring(low, "gx", -1)

    high, low = call(pack_kernel, [(7, 32, 128)] * 2, [], 16)(g, b, xl, xh)
    zl = ring(high, "gz", 1)
    zh = ring(low, "gz", -1)

    high, low = call(pack_y_kernel, [(Y_ROWS, 128)] * 2, [], 16)(g, b, xl, xh, zl, zh)
    yl = ring(high, "gy", 1)
    yh = ring(low, "gy", -1)
    middle = stage0a(g, b, xl, xh, zl, zh)
    x0, g1, b1 = stage0b(g, b, xl, xh, yl, yh, zl, zh, *middle)

    def both(at4, at5):
        return jnp.concatenate([g1[at4].reshape(96, 128), b1[at5].reshape(160, 128)])

    xl = ring(both(slice(4, 8), slice(3, 8)), "gx", 1)
    xh = ring(both(slice(0, 4), slice(0, 5)), "gx", -1)
    x1, chunk = stage1(g1, b1, xl, xh)

    send = jnp.broadcast_to(chunk[None], (32, 2, 8, 128))
    slab = lax.all_to_all(send, ("gx", "gy"), 0, 0, tiled=False)
    high, low = call(pack_z_kernel, [(35, 8, 128)] * 2, [], 16)(slab)
    return stage2(slab, ring(high, "gz", 1), ring(low, "gz", -1), x0, x1)


def solution(mesh):
    placed = (P("gx", "gy", "gz"), P("gx", "gy", "gz"))
    return jax.shard_map(
        per_device, mesh=mesh, in_specs=placed, out_specs=P("gx", "gy", "gz"), check_vma=False
    )
```

```python
import jax
import jax.numpy as jnp
from jax import lax
from jax.experimental import pallas as pl
from jax.experimental.pallas import tpu as pltpu
from jax.sharding import PartitionSpec as P

LEVELS = 3
SWEEPS = 4
BOTTOM = 8

cheby_top = 2.0
smooth_low = 0.25
bottom_low = 0.02

F32 = jnp.float32


def chebyshev_terms(lower_bound, sweeps):
    middle = (cheby_top + lower_bound) / 2.0
    radius = (cheby_top - lower_bound) / 2.0
    sigma_ratio = middle / radius
    rho_old = 1.0 / sigma_ratio
    term_list = []
    for sweep_index in range(1, sweeps):
        rho_new = 1.0 / (2.0 * sigma_ratio - rho_old)
        term_list.append((rho_new * rho_old, 2.0 * rho_new / radius))
        rho_old = rho_new
    return (1.0 / middle, term_list)


def ring(values, axis, step):
    count = lax.axis_size(axis)
    return lax.ppermute(values, axis, [(i, (i + step) % count) for i in range(count)])


def iota(shape, axis):
    return lax.broadcasted_iota(jnp.int32, shape, axis)


def matrix(shape, hit, value):
    return jnp.where(hit(iota(shape, 0), iota(shape, 1)), F32(value), F32(0.0))


def product(left, right):
    parts, rest = [], left
    for _ in range(3):
        part = rest.astype(jnp.bfloat16)
        parts.append(part)
        rest = rest - part.astype(F32)
    right = right.astype(jnp.bfloat16)
    high, middle, low = (jnp.dot(p, right, preferred_element_type=F32) for p in parts)
    return high + (middle + low)


def turn(v, shift):
    shift = shift % 128
    return pltpu.roll(v, shift, 1) if shift else v


def beside(cols):
    low = [pltpu.roll(c, 1, 1) for c in cols]
    high = [pltpu.roll(c, 127, 1) for c in cols]
    if len(cols) == 2:
        lanes = iota(cols[0].shape, 1)
        first, last = lanes == 0, lanes == 127
        low = [jnp.where(first, low[1], low[0]), jnp.where(first, low[0], low[1])]
        high = [jnp.where(last, high[1], high[0]), jnp.where(last, high[0], high[1])]
    return low, high


def around(field, first, planes, row, count):
    cols = range(field.shape[0])
    here = [
        [field[c, first + p, pl.ds(8 + row, count), :] for c in cols] for p in range(-1, planes + 1)
    ]
    out = []
    for p in range(planes):
        low, high = beside(here[p + 1])
        out.append(
            [
                (
                    here[p + 1][c],
                    here[p][c],
                    here[p + 2][c],
                    field[c, first + p, pl.ds(7 + row, count), :],
                    field[c, first + p, pl.ds(9 + row, count), :],
                    low[c],
                    high[c],
                )
                for c in cols
            ]
        )
    return out


def sweep_planes(low, high, body, unroll):
    steps = (high - low) // unroll
    if steps > 1:

        def several(j, _):
            body(low + j * unroll, unroll)
            return 0

        lax.fori_loop(0, steps, several, 0)
        low = low + steps * unroll
    if high > low:
        body(low, high - low)


class Level:
    def __init__(self, rows, block, unroll, at, scale, low, sweeps, w, gh, d, va, vb, double):
        self.rows, self.block, self.unroll, self.at, self.scale = rows, block, unroll, at, scale
        self.initial, self.terms = chebyshev_terms(low, sweeps)
        self.w, self.gh, self.d, self.va, self.vb, self.double = w, gh, d, va, vb, double
        self.spans = [(0, rows)]

    def blocks(self, spans=None):
        return [at for span in spans or self.spans for at in self.cut(*span)]

    def cut(self, first, last):
        return [(r, min(self.block, last - r)) for r in range(first, last, self.block)]

    def clear(self, planes):
        for ref in (self.va, self.vb):
            shape = ref.shape
            edge = jnp.zeros((shape[0], shape[1], 8, 128), F32)
            ref[:, :, 0:8, :] = edge
            ref[:, :, 8 + self.rows : 16 + self.rows, :] = edge
            for p in planes:
                ref[:, p] = jnp.zeros((shape[0],) + shape[2:], F32)

    def prepare(self, low, high, b, g, shift):
        def body(first, planes):
            for r, n in self.blocks():
                for p, fields in enumerate(around(b, first + shift, planes, r, n)):
                    i = first + p
                    for c, (bc, *near) in enumerate(fields):
                        double = 6.0 * bc + (
                            (near[0] + near[1]) + (near[2] + near[3]) + (near[4] + near[5])
                        )
                        inverse = jnp.where(bc > 0.0, 1.0 / double, 0.0)
                        for f in range(6):
                            self.w[f, c, i, pl.ds(r, n), :] = (bc + near[f]) * inverse
                        gh = g(c, i, r, n) * ((2.0 / self.scale) * inverse)
                        self.gh[c, i, pl.ds(r, n), :] = gh
                        self.va[c, i + self.at, pl.ds(8 + r, n), :] = gh * self.initial
                        if self.double is not None:
                            self.double[c, i, pl.ds(r, n), :] = (0.5 * self.scale) * double

        sweep_planes(low, high, body, self.unroll)

    def scaled_residual(self, v, first, planes, r, n):
        out = []
        for p, fields in enumerate(around(v, first + self.at, planes, r, n)):
            out.append([])
            for c, (vc, *near) in enumerate(fields):
                z = self.gh[c, first + p, pl.ds(r, n), :] - vc
                for f in range(6):
                    z = z + self.w[f, c, first + p, pl.ds(r, n), :] * near[f]
                out[-1].append((vc, z))
        return out

    def smooth(self, low, high, shrink, meet=None):
        src, dst = self.va, self.vb
        for k, (carry, push) in enumerate(self.terms):
            if meet is not None:
                meet(k, src)
            low, high = low + shrink, high - shrink

            def body(first, planes, src=src, dst=dst, k=k, carry=carry, push=push):
                for r, n in self.blocks():
                    for p, got in enumerate(self.scaled_residual(src, first, planes, r, n)):
                        i = first + p
                        for c, (vc, z) in enumerate(got):
                            old = vc if k == 0 else self.d[c, i, pl.ds(r, n), :]
                            step = carry * old + push * z
                            if k < len(self.terms) - 1:
                                self.d[c, i, pl.ds(r, n), :] = step
                            dst[c, i + self.at, pl.ds(8 + r, n), :] = vc + step

            sweep_planes(low, high, body, self.unroll)
            src, dst = dst, src
        if meet is not None:
            meet(len(self.terms), src)
        return src

    def residual_pairs(self, v, low, high, spans, put):
        def body(j, pairs):
            i = low + 2 * j
            for r, n in self.blocks(spans):
                got = self.scaled_residual(v, i, 2 * pairs, r, n)
                for p in range(pairs):
                    for c in range(len(got[0])):
                        total = None
                        for q in (2 * p, 2 * p + 1):
                            now = self.double[c, i + q, pl.ds(r, n), :] * got[q][c][1]
                            total = now if total is None else total + now
                        put(j + p, c, r, n, total)

        sweep_planes(0, (high - low) // 2, body, max(1, self.unroll // 2))


def flag(condition):
    return jnp.where(condition, F32(1.0), F32(0.0))


def plane_of(p, g, b, xl, xh):
    if p < 4:
        return xl[p]
    if p < 20:
        return g[p - 4]
    if p < 24:
        return xh[p - 20]
    if p < 29:
        return xl[p - 20]
    if p < 45:
        return b[p - 29]
    return xh[p - 41]


def pack_kernel(g, b, xl, xh, high, low):
    slot = iota((32, 128), 1) // 16
    for k in range(7):
        to_high = jnp.zeros((32, 128), F32)
        to_low = jnp.zeros((32, 128), F32)
        for s in range(8):
            p = 8 * k + s
            if p >= 50:
                break
            plane = plane_of(p, g, b, xl, xh)
            to_high = jnp.where(slot == s, pltpu.roll(plane, 16 * (s + 1) % 128, 1), to_high)
            to_low = jnp.where(slot == s, pltpu.roll(plane, 16 * s, 1) if s else plane, to_low)
        high[k] = to_high
        low[k] = to_low


INNER = 64
OUTER = list(range(1, 23)) + list(range(25, 49)) + list(range(50, 64))
LAST = list(range(29, 45))
OUTER_AT = 8 * INNER
LAST_AT = OUTER_AT + 4 * len(OUTER)
Y_ROWS = LAST_AT + len(LAST)


def pack_y_kernel(g, b, xl, xh, zl, zh, high, low):
    def plane(p):
        if p < 50:
            return plane_of(p, g, b, xl, xh)
        return zl[p - 50] if p < 57 else zh[p - 57]

    for p in range(INNER):
        here = plane(p)
        high[8 * p : 8 * p + 8, :] = here[24:32]
        low[8 * p : 8 * p + 8, :] = here[0:8]
    for i, p in enumerate(OUTER):
        here, at = plane(p), OUTER_AT + 4 * i
        high[at : at + 4, :] = here[20:24]
        low[at : at + 4, :] = here[8:12]
    for i, p in enumerate(LAST):
        here, at = plane(p), LAST_AT + i
        high[at : at + 1, :] = here[19:20]
        low[at : at + 1, :] = here[12:13]


def side_of(p, x_low, x_high):
    return x_low if p < 29 else x_high if p >= 45 else None


def times(factor, *values):
    return values if factor is None else tuple(factor * v for v in values)


def unpack(low, high, p, lanes):
    s = p % 8
    from_high = pltpu.roll(high, 128 - 16 * s, 1) if s else high
    from_low = pltpu.roll(low, 112 - 16 * s, 1) if s < 7 else low
    return jnp.where(lanes < 16, from_high, from_low)


def halved(pairs, count):
    near_mat = matrix((128, 128), lambda a, c: a // 2 == c, 0.125)
    far_mat = matrix((128, 128), lambda a, c: a // 2 + 64 == c, 0.125)
    sums = []
    for c in range(2):
        even = pairs[c, :, pl.ds(0, count, stride=2), :]
        odd = pairs[c, :, pl.ds(1, count, stride=2), :]
        sums.append((even + odd).reshape(8 * count, 128))
    total = product(sums[0], near_mat) + product(sums[1], far_mat)
    return total.reshape(8, count, 128)


def pack_x(out, planes):
    lanes = iota((24, 128), 1)
    for m in range(5):
        here = planes[2 * m]
        if m < 4:
            here = jnp.where(lanes < 64, here, pltpu.roll(planes[2 * m + 1], 64, 1))
        out[24 * m : 24 * m + 24, :] = here
    ends = jnp.zeros((24, 128), F32)
    for n in range(8):
        near = jnp.where(lanes % 16 < 8, turn(planes[n], 16 * n + 64), turn(planes[n], 16 * n + 16))
        ends = jnp.where(lanes // 16 == n, near, ends)
    out[120:144, :] = ends


def unpack_x(side, n):
    lanes = iota((24, 128), 1)
    at = 24 * (n // 2)
    own = turn(side[at : at + 24, :], 64 * (n % 2))
    far = jnp.zeros((24, 128), F32)
    if n < 8:
        ends = side[120:144, :]
        far = jnp.where(lanes < 72, turn(ends, 64 - 16 * n), far)
        far = jnp.where(lanes >= 120, turn(ends, 112 - 16 * n), far)
    return jnp.where(lanes < 64, own, far)


def middle_kernel(g, b, xl, xh, zl, zh, x4, rm, b1, VE, WE, GE, DE, G, B, W, GH, D2, VA, VB, DD, T):
    gx, gz = lax.axis_index("gx"), lax.axis_index("gz")
    lanes = iota((32, 128), 1)
    lane_in = jnp.where(lanes < 16, flag(gz < 7), jnp.where(lanes >= 112, flag(gz > 0), F32(0.0)))
    x_low, x_high = flag(gx > 0), flag(gx < 3)
    spare = jnp.zeros((2, 26, 8, 128), F32)
    B[:, :, 0:8, :] = spare
    B[:, :, 40:48, :] = spare
    for p in range(50):
        far = unpack(zl[p // 8], zh[p // 8], p, lanes)
        own = plane_of(p, g, b, xl, xh)
        if p < 24:
            G[0, p] = own
            G[1, p] = far
        else:
            own, far = times(side_of(p, x_low, x_high), own, far * lane_in)
            B[0, p - 24, 8:40, :] = own
            B[1, p - 24, 8:40, :] = far

    level = Level(32, BLOCK0, UNROLL0, 0, 1.0, smooth_low, SWEEPS, W, GH, DD, VA, VB, D2)
    level.clear([])
    level.prepare(0, 24, B, lambda c, i, r, n: G[c, i, pl.ds(r, n), :], 1)

    def keep(k, v):
        VE[k, :, :, 0:8, :] = v[:, :, 12:20, :]
        VE[k, :, :, 8:16, :] = v[:, :, 28:36, :]

    v = level.smooth(0, 24, 1, keep)
    x4[...] = v[0, 4:20, 12:36, :]

    def put(j, c, r, n, total):
        rm[c, j, pl.ds(r - 8, n), :] = total

    level.residual_pairs(v, 4, 20, [(8, 24)], put)
    for to, ref in ((WE, W), (GE, GH), (DE, D2)):
        to[..., 0:8, :] = ref[..., 4:20, 4:12, :]
        to[..., 8:16, :] = ref[..., 4:20, 20:28, :]
    for c in range(2):
        for j in range(8):
            T[c, j] = B[c, 5 + 2 * j, 8:40, :] + B[c, 6 + 2 * j, 8:40, :]
    b1[...] = halved(T, 16)


def ends_kernel(
    g, b, xl, xh, yl, yh, zl, zh, x4, rm, bm, VE, WE, GE, DE, x0, g1, b1, high, low,
    G, B, Z, W, GH, D2, VA, VB, DD, T,
):
    gx, gy, gz = lax.axis_index("gx"), lax.axis_index("gy"), lax.axis_index("gz")
    lanes = iota((48, 128), 1)
    rows = iota((48, 128), 0)
    y_low, y_high, x_low, x_high = flag(gy > 0), flag(gy < 7), flag(gx > 0), flag(gx < 3)
    lane_in = jnp.where(lanes < 16, flag(gz < 7), jnp.where(lanes >= 112, flag(gz > 0), F32(0.0)))
    lane_in = jnp.where(rows < 12, y_low, jnp.where(rows < 36, F32(1.0), y_high)) * lane_in
    blank4, blank8 = jnp.zeros((4, 128), F32), jnp.zeros((8, 128), F32)
    order = {p: i for i, p in enumerate(OUTER)}

    def outer(side, p):
        if p not in order:
            return blank4
        at = OUTER_AT + 4 * order[p]
        return side[at : at + 4, :]

    for side, source in ((0, zl), (1, zh)):
        for k in range(7):
            p = 50 + 7 * side + k
            Z[side, k, 0:4, :] = outer(yl, p)
            Z[side, k, 4:12, :] = yl[8 * p : 8 * p + 8, :]
            Z[side, k, 12:20, :] = source[k, 0:8]
            Z[side, k, 20:28, :] = blank8
            Z[side, k, 28:36, :] = source[k, 24:32]
            Z[side, k, 36:44, :] = yh[8 * p : 8 * p + 8, :]
            Z[side, k, 44:48, :] = outer(yh, p)
    for p in range(50):
        far = unpack(Z[0, p // 8], Z[1, p // 8], p, lanes)
        own = plane_of(p, g, b, xl, xh)
        first, last = own[0:8], own[24:32]
        below, above = yl[8 * p : 8 * p + 8, :], yh[8 * p : 8 * p + 8, :]
        below4, above4 = outer(yl, p), outer(yh, p)
        field, q = (G, p) if p < 24 else (B, p - 24)
        if p >= 24:
            side = side_of(p, x_low, x_high)
            first, last, far = times(side, first, last, far * lane_in)
            below, below4 = times(side, below * y_low, below4 * y_low)
            above, above4 = times(side, above * y_high, above4 * y_high)
            for c in range(2):
                field[c, q, 0:8, :] = blank8
                field[c, q, 56:64, :] = blank8
            if p in LAST:
                at = LAST_AT + LAST.index(p)
                field[0, q, 7:8, :] = yl[at : at + 1, :] * y_low
                field[0, q, 56:57, :] = yh[at : at + 1, :] * y_high
        field[0, q, 8:12, :] = below4
        field[0, q, 12:20, :] = below
        field[0, q, 20:28, :] = first
        field[0, q, 36:44, :] = last
        field[0, q, 44:52, :] = above
        field[0, q, 52:56, :] = above4
        field[1, q, 8:56, :] = far

    level = Level(48, BLOCK0, UNROLL0, 0, 1.0, smooth_low, SWEEPS, W, GH, DD, VA, VB, D2)
    level.spans = [(0, 16), (32, 48)]
    level.clear([])
    level.prepare(0, 24, B, lambda c, i, r, n: G[c, i, pl.ds(8 + r, n), :], 1)
    for to, ref in ((W, WE), (GH, GE), (D2, DE)):
        to[..., 4:20, 16:32, :] = ref[...]

    def join(k, v):
        v[:, :, 24:40, :] = VE[k]

    v = level.smooth(0, 24, 1, join)
    x0[:, 0:4, :] = v[0, 4:20, 20:24, :]
    x0[:, 4:28, :] = x4[...]
    x0[:, 28:32, :] = v[0, 4:20, 40:44, :]

    def put(j, c, r, n, total):
        T[c, j, pl.ds(r - 4 if r < 24 else r + 4, n), :] = total

    level.residual_pairs(v, 4, 20, [(4, 20), (28, 44)], put)
    T[:, :, 16:32, :] = rm[...]
    g1[...] = halved(T, 24)
    for c in range(2):
        for j in range(8):
            p, q = 5 + 2 * j, 6 + 2 * j
            T[c, j, 0:4, :] = blank4
            T[c, j, 4:16, :] = B[c, p, 8:20, :] + B[c, q, 8:20, :]
            T[c, j, 16:28, :] = B[c, p, 44:56, :] + B[c, q, 44:56, :]
            T[c, j, 28:32, :] = blank4
    both = halved(T, 16)
    b1[:, 0:8, :] = both[:, 0:8]
    b1[:, 8:24, :] = bm[...]
    b1[:, 24:32, :] = both[:, 8:16]
    pack_x(high, [g1[q] for q in range(4, 8)] + [b1[q, 4:28, :] for q in (4, 5, 6, 7, 3)])
    pack_x(low, [g1[q] for q in range(4)] + [b1[q, 4:28, :] for q in range(5)])


def level1_kernel(g, b, xl, xh, x1, chunk, G, B, W, GH, D2, VA, VB, DD, T):
    gx = lax.axis_index("gx")
    blank = jnp.zeros((8, 128), F32)
    for side, inside, at, planes in ((xl, gx > 0, 0, (1, 2, 3, 4, 0)), (xh, gx < 3, 4, range(13, 18))):
        for n in range(4):
            G[at + n] = unpack_x(side, n)
        for n, q in enumerate(planes):
            B[0, q, 0:8, :] = blank
            B[0, q, 8:32, :] = unpack_x(side, 4 + n) * flag(inside)
            B[0, q, 32:40, :] = blank
    for q in range(8):
        B[0, 5 + q, 4:36, :] = b[q]

    def source(c, i, r, n):
        if i < 4:
            return G[i, r : r + n, :]
        if i < 12:
            return g[i - 4, r : r + n, :]
        return G[i - 8, r : r + n, :]

    level = Level(24, 24, 16, 0, 0.25, smooth_low, SWEEPS, W, GH, DD, VA, VB, D2)
    level.clear([])
    level.prepare(0, 16, B, source, 1)
    v = level.smooth(0, 16, 1)
    x1[...] = v[0, 4:12, 12:28, :]

    def put(j, c, r, n, total):
        T[0, j, pl.ds(r, n), :] = total

    level.residual_pairs(v, 4, 12, None, put)
    for q in range(4):
        T[1, q] = B[0, 5 + 2 * q, 8:32, :] + B[0, 6 + 2 * q, 8:32, :]
    both = T[:, :, pl.ds(4, 8, stride=2), :] + T[:, :, pl.ds(5, 8, stride=2), :]
    mat = matrix((128, 128), lambda a, c: (a < 64) & (a // 2 == c), 0.125)
    total = product(both.reshape(64, 128), mat).reshape(2, 4, 8, 128)
    for a in range(2):
        out = total[a, 0]
        for q in range(1, 4):
            out = out + pltpu.roll(total[a, q], 32 * q, 1)
        chunk[a] = out


def pack_z_kernel(slab, high, low):
    lanes = iota((8, 128), 1)
    first = lanes % 32 < 16
    for j in range(32):
        g, b = slab[j, 0], slab[j, 1]
        high[j] = jnp.where(first, turn(g, -16), b)
        low[j] = jnp.where(first, g, turn(b, 16))
    gy = lax.axis_index("gy")
    for d in range(3):
        by = jnp.clip(gy + d - 1, 0, 7)
        to_high = jnp.zeros((8, 128), F32)
        to_low = jnp.zeros((8, 128), F32)
        for n in range(8):
            here = slab[8 * (n // 2) + by, n % 2]
            mine = lanes % 32 // 4 == n
            to_high = jnp.where(mine, turn(here, 4 * n - 12), to_high)
            to_low = jnp.where(mine, turn(here, 4 * n - 16), to_low)
        high[32 + d] = to_high
        low[32 + d] = to_low


def finish_kernel(
    slab, zl, zh, x0, x1, out, G, B, W, GH, D2, VA, VB, DD, T, B3, W3, VA3, VB3, DD3, GH3, X3, E1, E0
):
    gx, gy, gz = lax.axis_index("gx"), lax.axis_index("gy"), lax.axis_index("gz")
    lanes = iota((8, 128), 1)
    zeros = jnp.zeros((8, 128), F32)
    lane_in = jnp.where(lanes < 32, F32(1.0), jnp.where(lanes < 64, flag(gz < 7), zeros))
    lane_in = jnp.where(lanes >= 96, flag(gz > 0), lane_in)

    for p in (0, 17):
        B[0, p] = jnp.zeros((80, 128), F32)
    B[0, :, 0:8, :] = jnp.zeros((18, 8, 128), F32)
    B[0, :, 72:80, :] = jnp.zeros((18, 8, 128), F32)
    for j in range(32):
        row = 8 * (j % 8)
        for q in range(4):
            plane = 4 * (j // 8) + q
            for a in range(2):
                own, left, right = slab[j, a], zl[j], zh[j]
                far = jnp.where(lanes < 48, turn(right, 32 - 16 * a - 32 * q), 0.0)
                far = jnp.where(lanes >= 112, turn(left, 112 - 16 * a - 32 * q), far)
                got = jnp.where(lanes < 32, turn(own, -32 * q), far)
                if a == 0:
                    G[plane, row : row + 8, :] = got
                else:
                    B[0, plane + 1, 8 + row : 16 + row, :] = got * lane_in
    low4, high4 = (lanes >= 108) & (lanes < 112), (lanes >= 48) & (lanes < 52)
    for d in range(3):
        row = pl.multiple_of(8 * jnp.clip(gy + d - 1, 0, 7), 8)
        left, right = zl[32 + d], zh[32 + d]
        for n in range(8):
            for q in range(4):
                plane = 4 * (n // 2) + q
                far = jnp.where(low4, turn(left, 108 - 32 * q - 4 * n), 0.0)
                far = jnp.where(high4, turn(right, 48 - 32 * q - 4 * n), far)
                if n % 2 == 0:
                    here = G[plane, pl.ds(row, 8), :]
                    G[plane, pl.ds(row, 8), :] = jnp.where(low4 | high4, far, here)
                else:
                    here = B[0, plane + 1, pl.ds(8 + row, 8), :]
                    far = jnp.where(low4 | high4, far * lane_in, here)
                    B[0, plane + 1, pl.ds(8 + row, 8), :] = far

    level = Level(64, BLOCK2, UNROLL2, 1, 0.25**2, smooth_low, SWEEPS, W, GH, DD, VA, VB, D2)
    level.clear([0, 17])
    level.prepare(0, 16, B, lambda c, i, r, n: G[i, pl.ds(r, n), :], 1)
    v = level.smooth(0, 16, 0)

    def put(j, c, r, n, total):
        T[0, j, pl.ds(r, n), :] = total

    level.residual_pairs(v, 0, 16, None, put)
    for j in range(8):
        T[1, j] = B[0, 1 + 2 * j, 8:72, :] + B[0, 2 + 2 * j, 8:72, :]
    both = T[:, :, pl.ds(0, 32, stride=2), :] + T[:, :, pl.ds(1, 32, stride=2), :]
    mat = matrix((128, 128), lambda a, c: a // 2 == c % 64, 0.125)
    coarse = product(both.reshape(512, 128), mat).reshape(2, 8, 32, 128)
    for p in (0, 9):
        B3[0, p] = jnp.zeros((48, 128), F32)
    B3[0, :, 0:8, :] = jnp.zeros((10, 8, 128), F32)
    B3[0, :, 40:48, :] = jnp.zeros((10, 8, 128), F32)
    B3[0, 1:9, 8:40, :] = coarse[1]

    base = Level(32, 32, 8, 1, 0.25**3, bottom_low, BOTTOM, W3, GH3, DD3, VA3, VB3, None)
    base.clear([0, 9])
    base.prepare(0, 8, B3, lambda c, i, r, n: coarse[0, i, r : r + n, :], 1)
    e3 = base.smooth(0, 8, 0)

    spread = matrix((128, 128), lambda a, c: a == c // 2, 1.0)
    for i in range(2):
        own = e3[0, 1 + 2 * gx + i, 8:40, :]
        X3[i, pl.ds(0, 32, stride=2), :] = own
        X3[i, pl.ds(1, 32, stride=2), :] = own
    row = pl.multiple_of(8 * gy, 8)
    up = product(X3[:, pl.ds(row, 8), :].reshape(16, 128), spread).reshape(2, 8, 128)
    e2 = [v[0, 1 + 4 * gx + i, pl.ds(8 + row, 8), :] + up[i // 2] for i in range(4)]
    up = product(jnp.concatenate(e2, axis=0), spread).reshape(4, 8, 128)
    for i in range(4):
        E1[i, pl.ds(0, 8, stride=2), :] = up[i]
        E1[i, pl.ds(1, 8, stride=2), :] = up[i]
    e1 = [x1[i] + E1[i // 2] for i in range(8)]
    up = product(jnp.concatenate(e1, axis=0), spread).reshape(8, 16, 128)
    for i in range(8):
        E0[i, pl.ds(0, 16, stride=2), :] = up[i]
        E0[i, pl.ds(1, 16, stride=2), :] = up[i]
        out[2 * i] = x0[2 * i] + E0[i]
        out[2 * i + 1] = x0[2 * i + 1] + E0[i]


BLOCK0, UNROLL0, BLOCK2, UNROLL2 = 8, 8, 64, 16


def call(kernel, outs, scratch, limit, us=1):
    many = len(outs) > 1
    shapes = [jax.ShapeDtypeStruct(s, F32) for s in outs]
    return pl.pallas_call(
        kernel,
        out_shape=shapes if many else shapes[0],
        scratch_shapes=[pltpu.VMEM(s, F32) for s in scratch],
        compiler_params=pltpu.CompilerParams(vmem_limit_bytes=limit << 20),
        cost_estimate=pl.CostEstimate(
            flops=us * 1000000, bytes_accessed=us * 3600000, transcendentals=0
        ),
    )


def stage0a(*args):
    wide, tall = (32, 128), (48, 128)
    outs = [(16, 24, 128), (2, 8, 16, 128), (8, 16, 128), (4, 2, 24, 16, 128)]
    outs += [(6, 2, 16, 16, 128), (2, 16, 16, 128), (2, 16, 16, 128)]
    scratch = [(2, 24) + wide, (2, 26) + tall, (6, 2, 24) + wide, (2, 24) + wide, (2, 24) + wide]
    scratch += [(2, 24) + tall, (2, 24) + tall, (2, 24) + wide, (2, 8) + wide]
    return call(middle_kernel, outs, scratch, 20, 4)(*args)


def stage0b(*args):
    wide, tall = (48, 128), (64, 128)
    scratch = [(2, 24) + tall, (2, 26) + tall, (2, 7) + wide, (6, 2, 24) + wide]
    scratch += [(2, 24) + wide, (2, 24) + wide]
    scratch += [(2, 24) + tall, (2, 24) + tall, (2, 24) + wide, (2, 8) + wide]
    outs = [(16, 32, 128), (8, 24, 128), (8, 32, 128), (144, 128), (144, 128)]
    return call(ends_kernel, outs, scratch, 28)(*args)


def stage1(*args):
    wide, tall = (24, 128), (40, 128)
    scratch = [(8,) + wide, (1, 18) + tall, (6, 1, 16) + wide, (1, 16) + wide, (1, 16) + wide]
    scratch += [(1, 16) + tall, (1, 16) + tall, (1, 16) + wide, (2, 4) + wide]
    return call(level1_kernel, [(8, 16, 128), (2, 8, 128)], scratch, 16)(*args)


def stage2(*args):
    wide, tall, wide3, tall3 = (64, 128), (80, 128), (32, 128), (48, 128)
    scratch = [(16,) + wide, (1, 18) + tall, (6, 1, 16) + wide, (1, 16) + wide, (1, 16) + wide]
    scratch += [(1, 18) + tall, (1, 18) + tall, (1, 16) + wide, (2, 8) + wide]
    scratch += [(1, 10) + tall3, (6, 1, 8) + wide3, (1, 10) + tall3, (1, 10) + tall3]
    scratch += [(1, 8) + wide3, (1, 8) + wide3, (2, 64, 128), (4, 16, 128), (8, 32, 128)]
    return call(finish_kernel, [(16, 32, 128)], scratch, 24)(*args)


def load_kernel(g, b, gv, bv, high, low, sems):
    moves = [
        (g.at[12:16], high.at[0:4]),
        (b.at[11:16], high.at[4:9]),
        (g.at[0:4], low.at[0:4]),
        (b.at[0:5], low.at[4:9]),
    ]
    moves += [(g, gv), (b, bv)]
    copies = [pltpu.make_async_copy(a, c, sems.at[i]) for i, (a, c) in enumerate(moves)]
    for copy in copies:
        copy.start()
    for copy in copies:
        copy.wait()


def load(g, b):
    whole, ends = pltpu.VMEM((16, 32, 128), F32), pltpu.VMEM((9, 32, 128), F32)
    return pl.pallas_call(
        load_kernel,
        out_shape=[whole, whole, ends, ends],
        in_specs=[pl.BlockSpec(memory_space=pltpu.HBM)] * 2,
        scratch_shapes=[pltpu.SemaphoreType.DMA((6,))],
        compiler_params=pltpu.CompilerParams(vmem_limit_bytes=60 << 20),
    )(g, b)


def per_device(g, b):
    g, b, high, low = load(g, b)
    xl = ring(high, "gx", 1)
    xh = ring(low, "gx", -1)

    high, low = call(pack_kernel, [(7, 32, 128)] * 2, [], 16)(g, b, xl, xh)
    zl = ring(high, "gz", 1)
    zh = ring(low, "gz", -1)

    high, low = call(pack_y_kernel, [(Y_ROWS, 128)] * 2, [], 16)(g, b, xl, xh, zl, zh)
    yl = ring(high, "gy", 1)
    yh = ring(low, "gy", -1)
    middle = stage0a(g, b, xl, xh, zl, zh)
    x0, g1, b1, high, low = stage0b(g, b, xl, xh, yl, yh, zl, zh, *middle)

    xl = ring(high, "gx", 1)
    xh = ring(low, "gx", -1)
    x1, chunk = stage1(g1, b1, xl, xh)

    send = jnp.broadcast_to(chunk[None], (32, 2, 8, 128))
    slab = lax.all_to_all(send, ("gx", "gy"), 0, 0, tiled=False)
    high, low = call(pack_z_kernel, [(35, 8, 128)] * 2, [], 16)(slab)
    return stage2(slab, ring(high, "gz", 1), ring(low, "gz", -1), x0, x1)


def solution(mesh):
    placed = (P("gx", "gy", "gz"), P("gx", "gy", "gz"))
    return jax.shard_map(
        per_device, mesh=mesh, in_specs=placed, out_specs=P("gx", "gy", "gz"), check_vma=False
    )
```

```python
import jax
import jax.numpy as jnp
from jax import lax
from jax.experimental import pallas as pl
from jax.experimental.pallas import tpu as pltpu
from jax.sharding import PartitionSpec as P

LEVELS = 3
SWEEPS = 4
BOTTOM = 8

cheby_top = 2.0
smooth_low = 0.25
bottom_low = 0.02

F32 = jnp.float32


def chebyshev_terms(lower_bound, sweeps):
    middle = (cheby_top + lower_bound) / 2.0
    radius = (cheby_top - lower_bound) / 2.0
    sigma_ratio = middle / radius
    rho_old = 1.0 / sigma_ratio
    term_list = []
    for sweep_index in range(1, sweeps):
        rho_new = 1.0 / (2.0 * sigma_ratio - rho_old)
        term_list.append((rho_new * rho_old, 2.0 * rho_new / radius))
        rho_old = rho_new
    return (1.0 / middle, term_list)


def ring(values, axis, step):
    count = lax.axis_size(axis)
    return lax.ppermute(values, axis, [(i, (i + step) % count) for i in range(count)])


def iota(shape, axis):
    return lax.broadcasted_iota(jnp.int32, shape, axis)


def matrix(shape, hit, value):
    return jnp.where(hit(iota(shape, 0), iota(shape, 1)), F32(value), F32(0.0))


def product(left, right):
    parts, rest = [], left
    for _ in range(3):
        part = rest.astype(jnp.bfloat16)
        parts.append(part)
        rest = rest - part.astype(F32)
    right = right.astype(jnp.bfloat16)
    high, middle, low = (jnp.dot(p, right, preferred_element_type=F32) for p in parts)
    return high + (middle + low)


def turn(v, shift):
    shift = shift % 128
    return pltpu.roll(v, shift, 1) if shift else v


def beside(cols):
    low = [pltpu.roll(c, 1, 1) for c in cols]
    high = [pltpu.roll(c, 127, 1) for c in cols]
    if len(cols) == 2:
        lanes = iota(cols[0].shape, 1)
        first, last = lanes == 0, lanes == 127
        low = [jnp.where(first, low[1], low[0]), jnp.where(first, low[0], low[1])]
        high = [jnp.where(last, high[1], high[0]), jnp.where(last, high[0], high[1])]
    return low, high


def around(field, first, planes, row, count):
    cols = range(field.shape[0])
    here = [
        [field[c, first + p, pl.ds(8 + row, count), :] for c in cols] for p in range(-1, planes + 1)
    ]
    out = []
    for p in range(planes):
        low, high = beside(here[p + 1])
        out.append(
            [
                (
                    here[p + 1][c],
                    here[p][c],
                    here[p + 2][c],
                    field[c, first + p, pl.ds(7 + row, count), :],
                    field[c, first + p, pl.ds(9 + row, count), :],
                    low[c],
                    high[c],
                )
                for c in cols
            ]
        )
    return out


def sweep_planes(low, high, body, unroll):
    steps = (high - low) // unroll
    if steps > 1:

        def several(j, _):
            body(low + j * unroll, unroll)
            return 0

        lax.fori_loop(0, steps, several, 0)
        low = low + steps * unroll
    if high > low:
        body(low, high - low)


class Level:
    def __init__(self, rows, block, unroll, at, scale, low, sweeps, w, gh, d, va, vb, double):
        self.rows, self.block, self.unroll, self.at, self.scale = rows, block, unroll, at, scale
        self.initial, self.terms = chebyshev_terms(low, sweeps)
        self.w, self.gh, self.d, self.va, self.vb, self.double = w, gh, d, va, vb, double
        self.spans = [(0, rows)]

    def blocks(self, spans=None):
        return [at for span in spans or self.spans for at in self.cut(*span)]

    def cut(self, first, last):
        return [(r, min(self.block, last - r)) for r in range(first, last, self.block)]

    def clear(self, planes):
        for ref in (self.va, self.vb):
            shape = ref.shape
            edge = jnp.zeros((shape[0], shape[1], 8, 128), F32)
            ref[:, :, 0:8, :] = edge
            ref[:, :, 8 + self.rows : 16 + self.rows, :] = edge
            for p in planes:
                ref[:, p] = jnp.zeros((shape[0],) + shape[2:], F32)

    def prepare(self, low, high, b, g, shift):
        def body(first, planes):
            for r, n in self.blocks():
                for p, fields in enumerate(around(b, first + shift, planes, r, n)):
                    i = first + p
                    for c, (bc, *near) in enumerate(fields):
                        double = 6.0 * bc + (
                            (near[0] + near[1]) + (near[2] + near[3]) + (near[4] + near[5])
                        )
                        inverse = jnp.where(bc > 0.0, 1.0 / double, 0.0)
                        for f in range(6):
                            self.w[f, c, i, pl.ds(r, n), :] = (bc + near[f]) * inverse
                        gh = g(c, i, r, n) * ((2.0 / self.scale) * inverse)
                        self.gh[c, i, pl.ds(r, n), :] = gh
                        self.va[c, i + self.at, pl.ds(8 + r, n), :] = gh * self.initial
                        if self.double is not None:
                            self.double[c, i, pl.ds(r, n), :] = (0.5 * self.scale) * double

        sweep_planes(low, high, body, self.unroll)

    def scaled_residual(self, v, first, planes, r, n):
        out = []
        for p, fields in enumerate(around(v, first + self.at, planes, r, n)):
            out.append([])
            for c, (vc, *near) in enumerate(fields):
                z = self.gh[c, first + p, pl.ds(r, n), :] - vc
                for f in range(6):
                    z = z + self.w[f, c, first + p, pl.ds(r, n), :] * near[f]
                out[-1].append((vc, z))
        return out

    def smooth(self, low, high, shrink, meet=None):
        src, dst = self.va, self.vb
        for k, (carry, push) in enumerate(self.terms):
            if meet is not None:
                meet(k, src)
            low, high = low + shrink, high - shrink

            def body(first, planes, src=src, dst=dst, k=k, carry=carry, push=push):
                for r, n in self.blocks():
                    for p, got in enumerate(self.scaled_residual(src, first, planes, r, n)):
                        i = first + p
                        for c, (vc, z) in enumerate(got):
                            old = vc if k == 0 else self.d[c, i, pl.ds(r, n), :]
                            step = carry * old + push * z
                            if k < len(self.terms) - 1:
                                self.d[c, i, pl.ds(r, n), :] = step
                            dst[c, i + self.at, pl.ds(8 + r, n), :] = vc + step

            sweep_planes(low, high, body, self.unroll)
            src, dst = dst, src
        if meet is not None:
            meet(len(self.terms), src)
        return src

    def residual_pairs(self, v, low, high, spans, put):
        def body(j, pairs):
            i = low + 2 * j
            for r, n in self.blocks(spans):
                got = self.scaled_residual(v, i, 2 * pairs, r, n)
                for p in range(pairs):
                    for c in range(len(got[0])):
                        total = None
                        for q in (2 * p, 2 * p + 1):
                            now = self.double[c, i + q, pl.ds(r, n), :] * got[q][c][1]
                            total = now if total is None else total + now
                        put(j + p, c, r, n, total)

        sweep_planes(0, (high - low) // 2, body, max(1, self.unroll // 2))


def flag(condition):
    return jnp.where(condition, F32(1.0), F32(0.0))


def plane_of(p, g, b, xl, xh):
    if p < 4:
        return xl[p]
    if p < 20:
        return g[p - 4]
    if p < 24:
        return xh[p - 20]
    if p < 29:
        return xl[p - 20]
    if p < 45:
        return b[p - 29]
    return xh[p - 41]


def pack_kernel(g, b, xl, xh, high, low):
    slot = iota((32, 128), 1) // 16
    for k in range(7):
        to_high = jnp.zeros((32, 128), F32)
        to_low = jnp.zeros((32, 128), F32)
        for s in range(8):
            p = 8 * k + s
            if p >= 50:
                break
            plane = plane_of(p, g, b, xl, xh)
            to_high = jnp.where(slot == s, pltpu.roll(plane, 16 * (s + 1) % 128, 1), to_high)
            to_low = jnp.where(slot == s, pltpu.roll(plane, 16 * s, 1) if s else plane, to_low)
        high[k] = to_high
        low[k] = to_low


INNER = 64
OUTER = list(range(1, 23)) + list(range(25, 49)) + list(range(50, 64))
LAST = list(range(29, 45))
OUTER_AT = 8 * INNER
LAST_AT = OUTER_AT + 4 * len(OUTER)
Y_ROWS = LAST_AT + len(LAST)


def pack_y_kernel(g, b, xl, xh, zl, zh, high, low):
    def plane(p):
        if p < 50:
            return plane_of(p, g, b, xl, xh)
        return zl[p - 50] if p < 57 else zh[p - 57]

    for p in range(INNER):
        here = plane(p)
        high[8 * p : 8 * p + 8, :] = here[24:32]
        low[8 * p : 8 * p + 8, :] = here[0:8]
    for i, p in enumerate(OUTER):
        here, at = plane(p), OUTER_AT + 4 * i
        high[at : at + 4, :] = here[20:24]
        low[at : at + 4, :] = here[8:12]
    for i, p in enumerate(LAST):
        here, at = plane(p), LAST_AT + i
        high[at : at + 1, :] = here[19:20]
        low[at : at + 1, :] = here[12:13]


def side_of(p, x_low, x_high):
    return x_low if p < 29 else x_high if p >= 45 else None


def times(factor, *values):
    return values if factor is None else tuple(factor * v for v in values)


def unpack(low, high, p, lanes):
    s = p % 8
    from_high = pltpu.roll(high, 128 - 16 * s, 1) if s else high
    from_low = pltpu.roll(low, 112 - 16 * s, 1) if s < 7 else low
    return jnp.where(lanes < 16, from_high, from_low)


def halved(pairs, count):
    near_mat = matrix((128, 128), lambda a, c: a // 2 == c, 0.125)
    far_mat = matrix((128, 128), lambda a, c: a // 2 + 64 == c, 0.125)
    sums = []
    for c in range(2):
        even = pairs[c, :, pl.ds(0, count, stride=2), :]
        odd = pairs[c, :, pl.ds(1, count, stride=2), :]
        sums.append((even + odd).reshape(8 * count, 128))
    total = product(sums[0], near_mat) + product(sums[1], far_mat)
    return total.reshape(8, count, 128)


def pack_x(out, planes):
    lanes = iota((24, 128), 1)
    for m in range(5):
        here = planes[2 * m]
        if m < 4:
            here = jnp.where(lanes < 64, here, pltpu.roll(planes[2 * m + 1], 64, 1))
        out[24 * m : 24 * m + 24, :] = here
    ends = jnp.zeros((24, 128), F32)
    for n in range(8):
        near = jnp.where(lanes % 16 < 8, turn(planes[n], 16 * n + 64), turn(planes[n], 16 * n + 16))
        ends = jnp.where(lanes // 16 == n, near, ends)
    out[120:144, :] = ends


def unpack_x(side, n):
    lanes = iota((24, 128), 1)
    at = 24 * (n // 2)
    own = turn(side[at : at + 24, :], 64 * (n % 2))
    far = jnp.zeros((24, 128), F32)
    if n < 8:
        ends = side[120:144, :]
        far = jnp.where(lanes < 72, turn(ends, 64 - 16 * n), far)
        far = jnp.where(lanes >= 120, turn(ends, 112 - 16 * n), far)
    return jnp.where(lanes < 64, own, far)


def middle_kernel(g, b, xl, xh, zl, zh, x4, rm, b1, VE, WE, GE, DE, G, B, W, GH, D2, VA, VB, DD, T):
    gx, gz = lax.axis_index("gx"), lax.axis_index("gz")
    lanes = iota((32, 128), 1)
    lane_in = jnp.where(lanes < 16, flag(gz < 7), jnp.where(lanes >= 112, flag(gz > 0), F32(0.0)))
    x_low, x_high = flag(gx > 0), flag(gx < 3)
    spare = jnp.zeros((2, 26, 8, 128), F32)
    B[:, :, 0:8, :] = spare
    B[:, :, 40:48, :] = spare
    for p in range(50):
        far = unpack(zl[p // 8], zh[p // 8], p, lanes)
        own = plane_of(p, g, b, xl, xh)
        if p < 24:
            G[0, p] = own
            G[1, p] = far
        else:
            own, far = times(side_of(p, x_low, x_high), own, far * lane_in)
            B[0, p - 24, 8:40, :] = own
            B[1, p - 24, 8:40, :] = far

    level = Level(32, BLOCK0, UNROLL0, 0, 1.0, smooth_low, SWEEPS, W, GH, DD, VA, VB, D2)
    level.clear([])
    level.prepare(0, 24, B, lambda c, i, r, n: G[c, i, pl.ds(r, n), :], 1)

    def keep(k, v):
        VE[k, :, :, 0:8, :] = v[:, :, 12:20, :]
        VE[k, :, :, 8:16, :] = v[:, :, 28:36, :]

    v = level.smooth(0, 24, 1, keep)
    x4[...] = v[0, 4:20, 12:36, :]

    def put(j, c, r, n, total):
        rm[c, j, pl.ds(r - 8, n), :] = total

    level.residual_pairs(v, 4, 20, [(8, 24)], put)
    for to, ref in ((WE, W), (GE, GH), (DE, D2)):
        to[..., 0:8, :] = ref[..., 4:20, 4:12, :]
        to[..., 8:16, :] = ref[..., 4:20, 20:28, :]
    for c in range(2):
        for j in range(8):
            T[c, j] = B[c, 5 + 2 * j, 8:40, :] + B[c, 6 + 2 * j, 8:40, :]
    b1[...] = halved(T, 16)


def ends_kernel(
    g, b, xl, xh, yl, yh, zl, zh, x4, rm, bm, VE, WE, GE, DE, x0, g1, b1, high, low,
    G, B, Z, W, GH, D2, VA, VB, DD, T,
):
    gx, gy, gz = lax.axis_index("gx"), lax.axis_index("gy"), lax.axis_index("gz")
    lanes = iota((48, 128), 1)
    rows = iota((48, 128), 0)
    y_low, y_high, x_low, x_high = flag(gy > 0), flag(gy < 7), flag(gx > 0), flag(gx < 3)
    lane_in = jnp.where(lanes < 16, flag(gz < 7), jnp.where(lanes >= 112, flag(gz > 0), F32(0.0)))
    lane_in = jnp.where(rows < 12, y_low, jnp.where(rows < 36, F32(1.0), y_high)) * lane_in
    blank4, blank8 = jnp.zeros((4, 128), F32), jnp.zeros((8, 128), F32)
    order = {p: i for i, p in enumerate(OUTER)}

    def outer(side, p):
        if p not in order:
            return blank4
        at = OUTER_AT + 4 * order[p]
        return side[at : at + 4, :]

    for side, source in ((0, zl), (1, zh)):
        for k in range(7):
            p = 50 + 7 * side + k
            Z[side, k, 0:4, :] = outer(yl, p)
            Z[side, k, 4:12, :] = yl[8 * p : 8 * p + 8, :]
            Z[side, k, 12:20, :] = source[k, 0:8]
            Z[side, k, 20:28, :] = blank8
            Z[side, k, 28:36, :] = source[k, 24:32]
            Z[side, k, 36:44, :] = yh[8 * p : 8 * p + 8, :]
            Z[side, k, 44:48, :] = outer(yh, p)
    for p in range(50):
        far = unpack(Z[0, p // 8], Z[1, p // 8], p, lanes)
        own = plane_of(p, g, b, xl, xh)
        first, last = own[0:8], own[24:32]
        below, above = yl[8 * p : 8 * p + 8, :], yh[8 * p : 8 * p + 8, :]
        below4, above4 = outer(yl, p), outer(yh, p)
        field, q = (G, p) if p < 24 else (B, p - 24)
        if p >= 24:
            side = side_of(p, x_low, x_high)
            first, last, far = times(side, first, last, far * lane_in)
            below, below4 = times(side, below * y_low, below4 * y_low)
            above, above4 = times(side, above * y_high, above4 * y_high)
            for c in range(2):
                field[c, q, 0:8, :] = blank8
                field[c, q, 56:64, :] = blank8
            if p in LAST:
                at = LAST_AT + LAST.index(p)
                field[0, q, 7:8, :] = yl[at : at + 1, :] * y_low
                field[0, q, 56:57, :] = yh[at : at + 1, :] * y_high
        field[0, q, 8:12, :] = below4
        field[0, q, 12:20, :] = below
        field[0, q, 20:28, :] = first
        field[0, q, 36:44, :] = last
        field[0, q, 44:52, :] = above
        field[0, q, 52:56, :] = above4
        field[1, q, 8:56, :] = far

    level = Level(48, BLOCK0, UNROLL0, 0, 1.0, smooth_low, SWEEPS, W, GH, DD, VA, VB, D2)
    level.spans = [(0, 16), (32, 48)]
    level.clear([])
    level.prepare(0, 24, B, lambda c, i, r, n: G[c, i, pl.ds(8 + r, n), :], 1)
    for to, ref in ((W, WE), (GH, GE), (D2, DE)):
        to[..., 4:20, 16:32, :] = ref[...]

    def join(k, v):
        v[:, :, 24:40, :] = VE[k]

    v = level.smooth(0, 24, 1, join)
    x0[:, 0:4, :] = v[0, 4:20, 20:24, :]
    x0[:, 4:28, :] = x4[...]
    x0[:, 28:32, :] = v[0, 4:20, 40:44, :]

    def put(j, c, r, n, total):
        T[c, j, pl.ds(r - 4 if r < 24 else r + 4, n), :] = total

    level.residual_pairs(v, 4, 20, [(4, 20), (28, 44)], put)
    T[:, :, 16:32, :] = rm[...]
    g1[...] = halved(T, 24)
    for c in range(2):
        for j in range(8):
            p, q = 5 + 2 * j, 6 + 2 * j
            T[c, j, 0:4, :] = blank4
            T[c, j, 4:16, :] = B[c, p, 8:20, :] + B[c, q, 8:20, :]
            T[c, j, 16:28, :] = B[c, p, 44:56, :] + B[c, q, 44:56, :]
            T[c, j, 28:32, :] = blank4
    both = halved(T, 16)
    b1[:, 0:8, :] = both[:, 0:8]
    b1[:, 8:24, :] = bm[...]
    b1[:, 24:32, :] = both[:, 8:16]
    pack_x(high, [g1[q] for q in range(4, 8)] + [b1[q, 4:28, :] for q in (4, 5, 6, 7, 3)])
    pack_x(low, [g1[q] for q in range(4)] + [b1[q, 4:28, :] for q in range(5)])


def level1_kernel(g, b, xl, xh, x1, chunk, G, B, W, GH, D2, VA, VB, DD, T):
    gx = lax.axis_index("gx")
    blank = jnp.zeros((8, 128), F32)
    for side, inside, at, planes in ((xl, gx > 0, 0, (1, 2, 3, 4, 0)), (xh, gx < 3, 4, range(13, 18))):
        for n in range(4):
            G[at + n] = unpack_x(side, n)
        for n, q in enumerate(planes):
            B[0, q, 0:8, :] = blank
            B[0, q, 8:32, :] = unpack_x(side, 4 + n) * flag(inside)
            B[0, q, 32:40, :] = blank
    for q in range(8):
        B[0, 5 + q, 4:36, :] = b[q]

    def source(c, i, r, n):
        if i < 4:
            return G[i, r : r + n, :]
        if i < 12:
            return g[i - 4, r : r + n, :]
        return G[i - 8, r : r + n, :]

    level = Level(24, 24, 16, 0, 0.25, smooth_low, SWEEPS, W, GH, DD, VA, VB, D2)
    level.clear([])
    level.prepare(0, 16, B, source, 1)
    v = level.smooth(0, 16, 1)
    x1[...] = v[0, 4:12, 12:28, :]

    def put(j, c, r, n, total):
        T[0, j, pl.ds(r, n), :] = total

    level.residual_pairs(v, 4, 12, None, put)
    for q in range(4):
        T[1, q] = B[0, 5 + 2 * q, 8:32, :] + B[0, 6 + 2 * q, 8:32, :]
    both = T[:, :, pl.ds(4, 8, stride=2), :] + T[:, :, pl.ds(5, 8, stride=2), :]
    mat = matrix((128, 128), lambda a, c: (a < 64) & (a // 2 == c), 0.125)
    total = product(both.reshape(64, 128), mat).reshape(2, 4, 8, 128)
    for a in range(2):
        out = total[a, 0]
        for q in range(1, 4):
            out = out + pltpu.roll(total[a, q], 32 * q, 1)
        chunk[a] = out


def pack_z_kernel(slab, high, low):
    lanes = iota((8, 128), 1)
    first = lanes % 32 < 16
    for j in range(32):
        g, b = slab[j, 0], slab[j, 1]
        high[j] = jnp.where(first, turn(g, -16), b)
        low[j] = jnp.where(first, g, turn(b, 16))
    gy = lax.axis_index("gy")
    for d in range(3):
        by = jnp.clip(gy + d - 1, 0, 7)
        to_high = jnp.zeros((8, 128), F32)
        to_low = jnp.zeros((8, 128), F32)
        for n in range(8):
            here = slab[8 * (n // 2) + by, n % 2]
            mine = lanes % 32 // 4 == n
            to_high = jnp.where(mine, turn(here, 4 * n - 12), to_high)
            to_low = jnp.where(mine, turn(here, 4 * n - 16), to_low)
        high[32 + d] = to_high
        low[32 + d] = to_low


def slab_kernel(slab, x0, x1, g, b, up, E0):
    lanes = iota((8, 128), 1)
    for j in range(32):
        row = 8 * (j % 8)
        for q in range(4):
            for a, field in ((0, g), (1, b)):
                own = jnp.where(lanes < 32, turn(slab[j, a], -32 * q), 0.0)
                field[4 * (j // 8) + q, row : row + 8, :] = own
    spread = matrix((128, 128), lambda a, c: a == c // 2, 1.0)
    wide = product(x1[...].reshape(128, 128), spread).reshape(8, 16, 128)
    for i in range(8):
        E0[i, pl.ds(0, 16, stride=2), :] = wide[i]
        E0[i, pl.ds(1, 16, stride=2), :] = wide[i]
        up[2 * i] = x0[2 * i] + E0[i]
        up[2 * i + 1] = x0[2 * i + 1] + E0[i]


def finish_kernel(
    own_g, own_b, zl, zh, x01, out, G, B, W, GH, D2, VA, VB, DD, T, B3, W3, VA3, VB3, DD3, GH3, X3, E0
):
    gx, gy, gz = lax.axis_index("gx"), lax.axis_index("gy"), lax.axis_index("gz")
    lanes = iota((8, 128), 1)
    zeros = jnp.zeros((8, 128), F32)
    lane_in = jnp.where(lanes < 32, F32(1.0), jnp.where(lanes < 64, flag(gz < 7), zeros))
    lane_in = jnp.where(lanes >= 96, flag(gz > 0), lane_in)

    for p in (0, 17):
        B[0, p] = jnp.zeros((80, 128), F32)
    B[0, :, 0:8, :] = jnp.zeros((18, 8, 128), F32)
    B[0, :, 72:80, :] = jnp.zeros((18, 8, 128), F32)
    for j in range(32):
        row = 8 * (j % 8)
        for q in range(4):
            plane = 4 * (j // 8) + q
            for a in range(2):
                left, right = zl[j], zh[j]
                far = jnp.where(lanes < 48, turn(right, 32 - 16 * a - 32 * q), 0.0)
                far = jnp.where(lanes >= 112, turn(left, 112 - 16 * a - 32 * q), far)
                own = (own_g, own_b)[a][plane, row : row + 8, :]
                if a == 0:
                    G[plane, row : row + 8, :] = jnp.where(lanes < 32, own, far)
                else:
                    far = jnp.where(lanes < 32, own, far * lane_in)
                    B[0, plane + 1, 8 + row : 16 + row, :] = far
    low4, high4 = (lanes >= 108) & (lanes < 112), (lanes >= 48) & (lanes < 52)
    for d in range(3):
        row = pl.multiple_of(8 * jnp.clip(gy + d - 1, 0, 7), 8)
        left, right = zl[32 + d], zh[32 + d]
        for n in range(8):
            for q in range(4):
                plane = 4 * (n // 2) + q
                far = jnp.where(low4, turn(left, 108 - 32 * q - 4 * n), 0.0)
                far = jnp.where(high4, turn(right, 48 - 32 * q - 4 * n), far)
                if n % 2 == 0:
                    here = G[plane, pl.ds(row, 8), :]
                    G[plane, pl.ds(row, 8), :] = jnp.where(low4 | high4, far, here)
                else:
                    here = B[0, plane + 1, pl.ds(8 + row, 8), :]
                    far = jnp.where(low4 | high4, far * lane_in, here)
                    B[0, plane + 1, pl.ds(8 + row, 8), :] = far

    level = Level(64, BLOCK2, UNROLL2, 1, 0.25**2, smooth_low, SWEEPS, W, GH, DD, VA, VB, D2)
    level.clear([0, 17])
    level.prepare(0, 16, B, lambda c, i, r, n: G[i, pl.ds(r, n), :], 1)
    v = level.smooth(0, 16, 0)

    def put(j, c, r, n, total):
        T[0, j, pl.ds(r, n), :] = total

    level.residual_pairs(v, 0, 16, None, put)
    for j in range(8):
        T[1, j] = B[0, 1 + 2 * j, 8:72, :] + B[0, 2 + 2 * j, 8:72, :]
    both = T[:, :, pl.ds(0, 32, stride=2), :] + T[:, :, pl.ds(1, 32, stride=2), :]
    mat = matrix((128, 128), lambda a, c: a // 2 == c % 64, 0.125)
    coarse = product(both.reshape(512, 128), mat).reshape(2, 8, 32, 128)
    for p in (0, 9):
        B3[0, p] = jnp.zeros((48, 128), F32)
    B3[0, :, 0:8, :] = jnp.zeros((10, 8, 128), F32)
    B3[0, :, 40:48, :] = jnp.zeros((10, 8, 128), F32)
    B3[0, 1:9, 8:40, :] = coarse[1]

    base = Level(32, 32, 8, 1, 0.25**3, bottom_low, BOTTOM, W3, GH3, DD3, VA3, VB3, None)
    base.clear([0, 9])
    base.prepare(0, 8, B3, lambda c, i, r, n: coarse[0, i, r : r + n, :], 1)
    e3 = base.smooth(0, 8, 0)

    spread = matrix((128, 128), lambda a, c: a == c // 2, 1.0)
    for i in range(2):
        own = e3[0, 1 + 2 * gx + i, 8:40, :]
        X3[i, pl.ds(0, 32, stride=2), :] = own
        X3[i, pl.ds(1, 32, stride=2), :] = own
    row = pl.multiple_of(8 * gy, 8)
    up = product(X3[:, pl.ds(row, 8), :].reshape(16, 128), spread).reshape(2, 8, 128)
    e2 = [v[0, 1 + 4 * gx + i, pl.ds(8 + row, 8), :] + up[i // 2] for i in range(4)]
    spread = matrix((128, 128), lambda a, c: a == c // 4, 1.0)
    up = product(jnp.concatenate(e2, axis=0), spread).reshape(4, 8, 128)
    for i in range(4):
        for r in range(4):
            E0[i, pl.ds(r, 8, stride=4), :] = up[i]
        for r in range(4):
            out[4 * i + r] = x01[4 * i + r] + E0[i]


BLOCK0, UNROLL0, BLOCK2, UNROLL2 = 16, 12, 64, 16


def call(kernel, outs, scratch, limit, us=1):
    many = len(outs) > 1
    shapes = [jax.ShapeDtypeStruct(s, F32) for s in outs]
    return pl.pallas_call(
        kernel,
        out_shape=shapes if many else shapes[0],
        scratch_shapes=[pltpu.VMEM(s, F32) for s in scratch],
        compiler_params=pltpu.CompilerParams(vmem_limit_bytes=limit << 20),
        cost_estimate=pl.CostEstimate(
            flops=us * 1000000, bytes_accessed=us * 3600000, transcendentals=0
        ),
    )


def stage0a(*args):
    wide, tall = (32, 128), (48, 128)
    outs = [(16, 24, 128), (2, 8, 16, 128), (8, 16, 128), (4, 2, 24, 16, 128)]
    outs += [(6, 2, 16, 16, 128), (2, 16, 16, 128), (2, 16, 16, 128)]
    scratch = [(2, 24) + wide, (2, 26) + tall, (6, 2, 24) + wide, (2, 24) + wide, (2, 24) + wide]
    scratch += [(2, 24) + tall, (2, 24) + tall, (2, 24) + wide, (2, 8) + wide]
    return call(middle_kernel, outs, scratch, 20, 4)(*args)


def stage0b(*args):
    wide, tall = (48, 128), (64, 128)
    scratch = [(2, 24) + tall, (2, 26) + tall, (2, 7) + wide, (6, 2, 24) + wide]
    scratch += [(2, 24) + wide, (2, 24) + wide]
    scratch += [(2, 24) + tall, (2, 24) + tall, (2, 24) + wide, (2, 8) + wide]
    outs = [(16, 32, 128), (8, 24, 128), (8, 32, 128), (144, 128), (144, 128)]
    return call(ends_kernel, outs, scratch, 28)(*args)


def stage1(*args):
    wide, tall = (24, 128), (40, 128)
    scratch = [(8,) + wide, (1, 18) + tall, (6, 1, 16) + wide, (1, 16) + wide, (1, 16) + wide]
    scratch += [(1, 16) + tall, (1, 16) + tall, (1, 16) + wide, (2, 4) + wide]
    return call(level1_kernel, [(8, 16, 128), (2, 8, 128)], scratch, 16)(*args)


def stage2(*args):
    wide, tall, wide3, tall3 = (64, 128), (80, 128), (32, 128), (48, 128)
    scratch = [(16,) + wide, (1, 18) + tall, (6, 1, 16) + wide, (1, 16) + wide, (1, 16) + wide]
    scratch += [(1, 18) + tall, (1, 18) + tall, (1, 16) + wide, (2, 8) + wide]
    scratch += [(1, 10) + tall3, (6, 1, 8) + wide3, (1, 10) + tall3, (1, 10) + tall3]
    scratch += [(1, 8) + wide3, (1, 8) + wide3, (2, 64, 128), (4, 32, 128)]
    return call(finish_kernel, [(16, 32, 128)], scratch, 24)(*args)


def load_kernel(g, b, gv, bv, high, low, sems):
    moves = [
        (g.at[12:16], high.at[0:4]),
        (b.at[11:16], high.at[4:9]),
        (g.at[0:4], low.at[0:4]),
        (b.at[0:5], low.at[4:9]),
    ]
    moves += [(g, gv), (b, bv)]
    copies = [pltpu.make_async_copy(a, c, sems.at[i]) for i, (a, c) in enumerate(moves)]
    for copy in copies:
        copy.start()
    for copy in copies:
        copy.wait()


def load(g, b):
    whole, ends = pltpu.VMEM((16, 32, 128), F32), pltpu.VMEM((9, 32, 128), F32)
    return pl.pallas_call(
        load_kernel,
        out_shape=[whole, whole, ends, ends],
        in_specs=[pl.BlockSpec(memory_space=pltpu.HBM)] * 2,
        scratch_shapes=[pltpu.SemaphoreType.DMA((6,))],
        compiler_params=pltpu.CompilerParams(vmem_limit_bytes=60 << 20),
    )(g, b)


def per_device(g, b):
    g, b, high, low = load(g, b)
    xl = ring(high, "gx", 1)
    xh = ring(low, "gx", -1)

    high, low = call(pack_kernel, [(7, 32, 128)] * 2, [], 16)(g, b, xl, xh)
    zl = ring(high, "gz", 1)
    zh = ring(low, "gz", -1)

    high, low = call(pack_y_kernel, [(Y_ROWS, 128)] * 2, [], 16)(g, b, xl, xh, zl, zh)
    yl = ring(high, "gy", 1)
    yh = ring(low, "gy", -1)
    middle = stage0a(g, b, xl, xh, zl, zh)
    x0, g1, b1, high, low = stage0b(g, b, xl, xh, yl, yh, zl, zh, *middle)

    xl = ring(high, "gx", 1)
    xh = ring(low, "gx", -1)
    x1, chunk = stage1(g1, b1, xl, xh)

    send = jnp.broadcast_to(chunk[None], (32, 2, 8, 128))
    slab = lax.all_to_all(send, ("gx", "gy"), 0, 0, tiled=False)
    high, low = call(pack_z_kernel, [(35, 8, 128)] * 2, [], 16)(slab)
    zl = ring(high, "gz", 1)
    zh = ring(low, "gz", -1)
    outs = [(16, 64, 128), (16, 64, 128), (16, 32, 128)]
    own_g, own_b, x01 = call(slab_kernel, outs, [(8, 32, 128)], 8, 2)(slab, x0, x1)
    return stage2(own_g, own_b, zl, zh, x01)


def solution(mesh):
    placed = (P("gx", "gy", "gz"), P("gx", "gy", "gz"))
    return jax.shard_map(
        per_device, mesh=mesh, in_specs=placed, out_specs=P("gx", "gy", "gz"), check_vma=False
    )
```

```python
import jax
import jax.numpy as jnp
from jax import lax
from jax.experimental import pallas as pl
from jax.experimental.pallas import tpu as pltpu
from jax.sharding import PartitionSpec as P

LEVELS = 3
SWEEPS = 4
BOTTOM = 8

cheby_top = 2.0
smooth_low = 0.25
bottom_low = 0.02

F32 = jnp.float32


def chebyshev_terms(lower_bound, sweeps):
    middle = (cheby_top + lower_bound) / 2.0
    radius = (cheby_top - lower_bound) / 2.0
    sigma_ratio = middle / radius
    rho_old = 1.0 / sigma_ratio
    term_list = []
    for sweep_index in range(1, sweeps):
        rho_new = 1.0 / (2.0 * sigma_ratio - rho_old)
        term_list.append((rho_new * rho_old, 2.0 * rho_new / radius))
        rho_old = rho_new
    return (1.0 / middle, term_list)


def ring(values, axis, step):
    count = lax.axis_size(axis)
    return lax.ppermute(values, axis, [(i, (i + step) % count) for i in range(count)])


def swap(values, axis, first):
    count = lax.axis_size(axis)
    pairs = [(i % count, (i + 1) % count) for i in range(first, first + count, 2)]
    return lax.ppermute(values, axis, pairs + [(j, i) for i, j in pairs])


def iota(shape, axis):
    return lax.broadcasted_iota(jnp.int32, shape, axis)


def matrix(shape, hit, value):
    return jnp.where(hit(iota(shape, 0), iota(shape, 1)), F32(value), F32(0.0))


def product(left, right):
    parts, rest = [], left
    for _ in range(3):
        part = rest.astype(jnp.bfloat16)
        parts.append(part)
        rest = rest - part.astype(F32)
    right = right.astype(jnp.bfloat16)
    high, middle, low = (jnp.dot(p, right, preferred_element_type=F32) for p in parts)
    return high + (middle + low)


def turn(v, shift):
    shift = shift % 128
    return pltpu.roll(v, shift, 1) if shift else v


def beside(cols):
    low = [pltpu.roll(c, 1, 1) for c in cols]
    high = [pltpu.roll(c, 127, 1) for c in cols]
    if len(cols) == 2:
        lanes = iota(cols[0].shape, 1)
        first, last = lanes == 0, lanes == 127
        low = [jnp.where(first, low[1], low[0]), jnp.where(first, low[0], low[1])]
        high = [jnp.where(last, high[1], high[0]), jnp.where(last, high[0], high[1])]
    return low, high


def around(field, first, planes, row, count):
    cols = range(field.shape[0])
    here = [
        [field[c, first + p, pl.ds(8 + row, count), :] for c in cols] for p in range(-1, planes + 1)
    ]
    out = []
    for p in range(planes):
        low, high = beside(here[p + 1])
        out.append(
            [
                (
                    here[p + 1][c],
                    here[p][c],
                    here[p + 2][c],
                    field[c, first + p, pl.ds(7 + row, count), :],
                    field[c, first + p, pl.ds(9 + row, count), :],
                    low[c],
                    high[c],
                )
                for c in cols
            ]
        )
    return out


def sweep_planes(low, high, body, unroll):
    steps = (high - low) // unroll
    if steps > 1:

        def several(j, _):
            body(low + j * unroll, unroll)
            return 0

        lax.fori_loop(0, steps, several, 0)
        low = low + steps * unroll
    if high > low:
        body(low, high - low)


class Level:
    def __init__(self, rows, block, unroll, at, scale, low, sweeps, w, gh, d, va, vb, double):
        self.rows, self.block, self.unroll, self.at, self.scale = rows, block, unroll, at, scale
        self.initial, self.terms = chebyshev_terms(low, sweeps)
        self.w, self.gh, self.d, self.va, self.vb, self.double = w, gh, d, va, vb, double
        self.spans = [(0, rows)]

    def blocks(self, spans=None):
        return [at for span in spans or self.spans for at in self.cut(*span)]

    def cut(self, first, last):
        return [(r, min(self.block, last - r)) for r in range(first, last, self.block)]

    def clear(self, planes):
        for ref in (self.va, self.vb):
            shape = ref.shape
            edge = jnp.zeros((shape[0], shape[1], 8, 128), F32)
            ref[:, :, 0:8, :] = edge
            ref[:, :, 8 + self.rows : 16 + self.rows, :] = edge
            for p in planes:
                ref[:, p] = jnp.zeros((shape[0],) + shape[2:], F32)

    def prepare(self, low, high, b, g, shift):
        def body(first, planes):
            for r, n in self.blocks():
                for p, fields in enumerate(around(b, first + shift, planes, r, n)):
                    i = first + p
                    for c, (bc, *near) in enumerate(fields):
                        double = 6.0 * bc + (
                            (near[0] + near[1]) + (near[2] + near[3]) + (near[4] + near[5])
                        )
                        inverse = jnp.where(bc > 0.0, 1.0 / double, 0.0)
                        for f in range(6):
                            self.w[f, c, i, pl.ds(r, n), :] = (bc + near[f]) * inverse
                        gh = g(c, i, r, n) * ((2.0 / self.scale) * inverse)
                        self.gh[c, i, pl.ds(r, n), :] = gh
                        self.va[c, i + self.at, pl.ds(8 + r, n), :] = gh * self.initial
                        if self.double is not None:
                            self.double[c, i, pl.ds(r, n), :] = (0.5 * self.scale) * double

        sweep_planes(low, high, body, self.unroll)

    def scaled_residual(self, v, first, planes, r, n):
        out = []
        for p, fields in enumerate(around(v, first + self.at, planes, r, n)):
            out.append([])
            for c, (vc, *near) in enumerate(fields):
                z = self.gh[c, first + p, pl.ds(r, n), :] - vc
                for f in range(6):
                    z = z + self.w[f, c, first + p, pl.ds(r, n), :] * near[f]
                out[-1].append((vc, z))
        return out

    def smooth(self, low, high, shrink, meet=None):
        src, dst = self.va, self.vb
        for k, (carry, push) in enumerate(self.terms):
            if meet is not None:
                meet(k, src)
            low, high = low + shrink, high - shrink

            def body(first, planes, src=src, dst=dst, k=k, carry=carry, push=push):
                for r, n in self.blocks():
                    for p, got in enumerate(self.scaled_residual(src, first, planes, r, n)):
                        i = first + p
                        for c, (vc, z) in enumerate(got):
                            old = vc if k == 0 else self.d[c, i, pl.ds(r, n), :]
                            step = carry * old + push * z
                            if k < len(self.terms) - 1:
                                self.d[c, i, pl.ds(r, n), :] = step
                            dst[c, i + self.at, pl.ds(8 + r, n), :] = vc + step

            sweep_planes(low, high, body, self.unroll)
            src, dst = dst, src
        if meet is not None:
            meet(len(self.terms), src)
        return src

    def residual_pairs(self, v, low, high, spans, put):
        def body(j, pairs):
            i = low + 2 * j
            for r, n in self.blocks(spans):
                got = self.scaled_residual(v, i, 2 * pairs, r, n)
                for p in range(pairs):
                    for c in range(len(got[0])):
                        total = None
                        for q in (2 * p, 2 * p + 1):
                            now = self.double[c, i + q, pl.ds(r, n), :] * got[q][c][1]
                            total = now if total is None else total + now
                        put(j + p, c, r, n, total)

        sweep_planes(0, (high - low) // 2, body, max(1, self.unroll // 2))


def flag(condition):
    return jnp.where(condition, F32(1.0), F32(0.0))


def plane_of(p, g, b, xl, xh):
    if p < 4:
        return xl[p]
    if p < 20:
        return g[p - 4]
    if p < 24:
        return xh[p - 20]
    if p < 29:
        return xl[p - 20]
    if p < 45:
        return b[p - 29]
    return xh[p - 41]


def pack_kernel(g, b, xl, xh, high, low):
    slot = iota((32, 128), 1) // 16
    for k in range(7):
        to_high = jnp.zeros((32, 128), F32)
        to_low = jnp.zeros((32, 128), F32)
        for s in range(8):
            p = 8 * k + s
            if p >= 50:
                break
            plane = plane_of(p, g, b, xl, xh)
            to_high = jnp.where(slot == s, pltpu.roll(plane, 16 * (s + 1) % 128, 1), to_high)
            to_low = jnp.where(slot == s, pltpu.roll(plane, 16 * s, 1) if s else plane, to_low)
        high[k] = to_high
        low[k] = to_low


INNER = 64
OUTER = list(range(1, 23)) + list(range(25, 49)) + list(range(50, 64))
LAST = list(range(29, 45))
OUTER_AT = 8 * INNER
LAST_AT = OUTER_AT + 4 * len(OUTER)
Y_ROWS = LAST_AT + len(LAST)


def pack_y_kernel(g, b, xl, xh, zl, zh, on, off):
    even = lax.rem(lax.axis_index("gy"), 2) == 0

    def put(at, count, upper, lower):
        on[at : at + count, :] = jnp.where(even, upper, lower)
        off[at : at + count, :] = jnp.where(even, lower, upper)

    def plane(p):
        if p < 50:
            return plane_of(p, g, b, xl, xh)
        return zl[p - 50] if p < 57 else zh[p - 57]

    for p in range(INNER):
        here = plane(p)
        put(8 * p, 8, here[24:32], here[0:8])
    for i, p in enumerate(OUTER):
        here, at = plane(p), OUTER_AT + 4 * i
        put(at, 4, here[20:24], here[8:12])
    for i, p in enumerate(LAST):
        here, at = plane(p), LAST_AT + i
        put(at, 1, here[19:20], here[12:13])


def side_of(p, x_low, x_high):
    return x_low if p < 29 else x_high if p >= 45 else None


def times(factor, *values):
    return values if factor is None else tuple(factor * v for v in values)


def unpack(low, high, p, lanes):
    s = p % 8
    from_high = pltpu.roll(high, 128 - 16 * s, 1) if s else high
    from_low = pltpu.roll(low, 112 - 16 * s, 1) if s < 7 else low
    return jnp.where(lanes < 16, from_high, from_low)


def halved(pairs, count):
    near_mat = matrix((128, 128), lambda a, c: a // 2 == c, 0.125)
    far_mat = matrix((128, 128), lambda a, c: a // 2 + 64 == c, 0.125)
    sums = []
    for c in range(2):
        even = pairs[c, :, pl.ds(0, count, stride=2), :]
        odd = pairs[c, :, pl.ds(1, count, stride=2), :]
        sums.append((even + odd).reshape(8 * count, 128))
    total = product(sums[0], near_mat) + product(sums[1], far_mat)
    return total.reshape(8, count, 128)


def pack_x(out, planes):
    lanes = iota((24, 128), 1)
    for m in range(5):
        here = planes[2 * m]
        if m < 4:
            here = jnp.where(lanes < 64, here, pltpu.roll(planes[2 * m + 1], 64, 1))
        out[24 * m : 24 * m + 24, :] = here
    ends = jnp.zeros((24, 128), F32)
    for n in range(8):
        near = jnp.where(lanes % 16 < 8, turn(planes[n], 16 * n + 64), turn(planes[n], 16 * n + 16))
        ends = jnp.where(lanes // 16 == n, near, ends)
    out[120:144, :] = ends


def unpack_x(side, n):
    lanes = iota((24, 128), 1)
    at = 24 * (n // 2)
    own = turn(side[at : at + 24, :], 64 * (n % 2))
    far = jnp.zeros((24, 128), F32)
    if n < 8:
        ends = side[120:144, :]
        far = jnp.where(lanes < 72, turn(ends, 64 - 16 * n), far)
        far = jnp.where(lanes >= 120, turn(ends, 112 - 16 * n), far)
    return jnp.where(lanes < 64, own, far)


def middle_kernel(g, b, xl, xh, zl, zh, x4, rm, b1, VE, WE, GE, DE, G, B, W, GH, D2, VA, VB, DD, T):
    gx, gz = lax.axis_index("gx"), lax.axis_index("gz")
    lanes = iota((32, 128), 1)
    lane_in = jnp.where(lanes < 16, flag(gz < 7), jnp.where(lanes >= 112, flag(gz > 0), F32(0.0)))
    x_low, x_high = flag(gx > 0), flag(gx < 3)
    spare = jnp.zeros((2, 26, 8, 128), F32)
    B[:, :, 0:8, :] = spare
    B[:, :, 40:48, :] = spare
    for p in range(50):
        far = unpack(zl[p // 8], zh[p // 8], p, lanes)
        own = plane_of(p, g, b, xl, xh)
        if p < 24:
            G[0, p] = own
            G[1, p] = far
        else:
            own, far = times(side_of(p, x_low, x_high), own, far * lane_in)
            B[0, p - 24, 8:40, :] = own
            B[1, p - 24, 8:40, :] = far

    level = Level(32, BLOCK0, UNROLL0, 0, 1.0, smooth_low, SWEEPS, W, GH, DD, VA, VB, D2)
    level.clear([])
    level.prepare(0, 24, B, lambda c, i, r, n: G[c, i, pl.ds(r, n), :], 1)

    def keep(k, v):
        VE[k, :, :, 0:8, :] = v[:, :, 12:20, :]
        VE[k, :, :, 8:16, :] = v[:, :, 28:36, :]

    v = level.smooth(0, 24, 1, keep)
    x4[...] = v[0, 4:20, 12:36, :]

    def put(j, c, r, n, total):
        rm[c, j, pl.ds(r - 8, n), :] = total

    level.residual_pairs(v, 4, 20, [(8, 24)], put)
    for to, ref in ((WE, W), (GE, GH), (DE, D2)):
        to[..., 0:8, :] = ref[..., 4:20, 4:12, :]
        to[..., 8:16, :] = ref[..., 4:20, 20:28, :]
    for c in range(2):
        for j in range(8):
            T[c, j] = B[c, 5 + 2 * j, 8:40, :] + B[c, 6 + 2 * j, 8:40, :]
    b1[...] = halved(T, 16)


class Either:
    def __init__(self, condition, first, second):
        self.condition, self.first, self.second = condition, first, second

    def __getitem__(self, at):
        return jnp.where(self.condition, self.first[at], self.second[at])


def ends_kernel(
    g, b, xl, xh, on, off, zl, zh, x4, rm, bm, VE, WE, GE, DE, x0, g1, b1, high, low,
    G, B, Z, W, GH, D2, VA, VB, DD, T,
):
    gx, gy, gz = lax.axis_index("gx"), lax.axis_index("gy"), lax.axis_index("gz")
    even = lax.rem(gy, 2) == 0
    yl, yh = Either(even, off, on), Either(even, on, off)
    lanes = iota((48, 128), 1)
    rows = iota((48, 128), 0)
    y_low, y_high, x_low, x_high = flag(gy > 0), flag(gy < 7), flag(gx > 0), flag(gx < 3)
    lane_in = jnp.where(lanes < 16, flag(gz < 7), jnp.where(lanes >= 112, flag(gz > 0), F32(0.0)))
    lane_in = jnp.where(rows < 12, y_low, jnp.where(rows < 36, F32(1.0), y_high)) * lane_in
    blank4, blank8 = jnp.zeros((4, 128), F32), jnp.zeros((8, 128), F32)
    order = {p: i for i, p in enumerate(OUTER)}

    def outer(side, p):
        if p not in order:
            return blank4
        at = OUTER_AT + 4 * order[p]
        return side[at : at + 4, :]

    for side, source in ((0, zl), (1, zh)):
        for k in range(7):
            p = 50 + 7 * side + k
            Z[side, k, 0:4, :] = outer(yl, p)
            Z[side, k, 4:12, :] = yl[8 * p : 8 * p + 8, :]
            Z[side, k, 12:20, :] = source[k, 0:8]
            Z[side, k, 20:28, :] = blank8
            Z[side, k, 28:36, :] = source[k, 24:32]
            Z[side, k, 36:44, :] = yh[8 * p : 8 * p + 8, :]
            Z[side, k, 44:48, :] = outer(yh, p)
    for p in range(50):
        far = unpack(Z[0, p // 8], Z[1, p // 8], p, lanes)
        own = plane_of(p, g, b, xl, xh)
        first, last = own[0:8], own[24:32]
        below, above = yl[8 * p : 8 * p + 8, :], yh[8 * p : 8 * p + 8, :]
        below4, above4 = outer(yl, p), outer(yh, p)
        field, q = (G, p) if p < 24 else (B, p - 24)
        if p >= 24:
            side = side_of(p, x_low, x_high)
            first, last, far = times(side, first, last, far * lane_in)
            below, below4 = times(side, below * y_low, below4 * y_low)
            above, above4 = times(side, above * y_high, above4 * y_high)
            for c in range(2):
                field[c, q, 0:8, :] = blank8
                field[c, q, 56:64, :] = blank8
            if p in LAST:
                at = LAST_AT + LAST.index(p)
                field[0, q, 7:8, :] = yl[at : at + 1, :] * y_low
                field[0, q, 56:57, :] = yh[at : at + 1, :] * y_high
        field[0, q, 8:12, :] = below4
        field[0, q, 12:20, :] = below
        field[0, q, 20:28, :] = first
        field[0, q, 36:44, :] = last
        field[0, q, 44:52, :] = above
        field[0, q, 52:56, :] = above4
        field[1, q, 8:56, :] = far

    level = Level(48, BLOCK0, UNROLL0, 0, 1.0, smooth_low, SWEEPS, W, GH, DD, VA, VB, D2)
    level.spans = [(0, 16), (32, 48)]
    level.clear([])
    level.prepare(0, 24, B, lambda c, i, r, n: G[c, i, pl.ds(8 + r, n), :], 1)
    for to, ref in ((W, WE), (GH, GE), (D2, DE)):
        to[..., 4:20, 16:32, :] = ref[...]

    def join(k, v):
        v[:, :, 24:40, :] = VE[k]

    v = level.smooth(0, 24, 1, join)
    x0[:, 0:4, :] = v[0, 4:20, 20:24, :]
    x0[:, 4:28, :] = x4[...]
    x0[:, 28:32, :] = v[0, 4:20, 40:44, :]

    def put(j, c, r, n, total):
        T[c, j, pl.ds(r - 4 if r < 24 else r + 4, n), :] = total

    level.residual_pairs(v, 4, 20, [(4, 20), (28, 44)], put)
    T[:, :, 16:32, :] = rm[...]
    g1[...] = halved(T, 24)
    for c in range(2):
        for j in range(8):
            p, q = 5 + 2 * j, 6 + 2 * j
            T[c, j, 0:4, :] = blank4
            T[c, j, 4:16, :] = B[c, p, 8:20, :] + B[c, q, 8:20, :]
            T[c, j, 16:28, :] = B[c, p, 44:56, :] + B[c, q, 44:56, :]
            T[c, j, 28:32, :] = blank4
    both = halved(T, 16)
    b1[:, 0:8, :] = both[:, 0:8]
    b1[:, 8:24, :] = bm[...]
    b1[:, 24:32, :] = both[:, 8:16]
    pack_x(high, [g1[q] for q in range(4, 8)] + [b1[q, 4:28, :] for q in (4, 5, 6, 7, 3)])
    pack_x(low, [g1[q] for q in range(4)] + [b1[q, 4:28, :] for q in range(5)])


def level1_kernel(g, b, xl, xh, x1, chunk, G, B, W, GH, D2, VA, VB, DD, T):
    gx = lax.axis_index("gx")
    blank = jnp.zeros((8, 128), F32)
    for side, inside, at, planes in ((xl, gx > 0, 0, (1, 2, 3, 4, 0)), (xh, gx < 3, 4, range(13, 18))):
        for n in range(4):
            G[at + n] = unpack_x(side, n)
        for n, q in enumerate(planes):
            B[0, q, 0:8, :] = blank
            B[0, q, 8:32, :] = unpack_x(side, 4 + n) * flag(inside)
            B[0, q, 32:40, :] = blank
    for q in range(8):
        B[0, 5 + q, 4:36, :] = b[q]

    def source(c, i, r, n):
        if i < 4:
            return G[i, r : r + n, :]
        if i < 12:
            return g[i - 4, r : r + n, :]
        return G[i - 8, r : r + n, :]

    level = Level(24, 24, 16, 0, 0.25, smooth_low, SWEEPS, W, GH, DD, VA, VB, D2)
    level.clear([])
    level.prepare(0, 16, B, source, 1)
    v = level.smooth(0, 16, 1)
    x1[...] = v[0, 4:12, 12:28, :]

    def put(j, c, r, n, total):
        T[0, j, pl.ds(r, n), :] = total

    level.residual_pairs(v, 4, 12, None, put)
    for q in range(4):
        T[1, q] = B[0, 5 + 2 * q, 8:32, :] + B[0, 6 + 2 * q, 8:32, :]
    both = T[:, :, pl.ds(4, 8, stride=2), :] + T[:, :, pl.ds(5, 8, stride=2), :]
    mat = matrix((128, 128), lambda a, c: (a < 64) & (a // 2 == c), 0.125)
    total = product(both.reshape(64, 128), mat).reshape(2, 4, 8, 128)
    for a in range(2):
        out = total[a, 0]
        for q in range(1, 4):
            out = out + pltpu.roll(total[a, q], 32 * q, 1)
        chunk[a] = out


def pack_z_kernel(slab, high, low):
    lanes = iota((8, 128), 1)
    first = lanes % 32 < 16
    for j in range(32):
        g, b = slab[j, 0], slab[j, 1]
        high[j] = jnp.where(first, turn(g, -16), b)
        low[j] = jnp.where(first, g, turn(b, 16))
    gy = lax.axis_index("gy")
    for d in range(3):
        by = jnp.clip(gy + d - 1, 0, 7)
        to_high = jnp.zeros((8, 128), F32)
        to_low = jnp.zeros((8, 128), F32)
        for n in range(8):
            here = slab[8 * (n // 2) + by, n % 2]
            mine = lanes % 32 // 4 == n
            to_high = jnp.where(mine, turn(here, 4 * n - 12), to_high)
            to_low = jnp.where(mine, turn(here, 4 * n - 16), to_low)
        high[32 + d] = to_high
        low[32 + d] = to_low


def slab_kernel(slab, x0, x1, g, b, up, E0):
    lanes = iota((8, 128), 1)
    for j in range(32):
        row = 8 * (j % 8)
        for q in range(4):
            for a, field in ((0, g), (1, b)):
                own = jnp.where(lanes < 32, turn(slab[j, a], -32 * q), 0.0)
                field[4 * (j // 8) + q, row : row + 8, :] = own
    spread = matrix((128, 128), lambda a, c: a == c // 2, 1.0)
    wide = product(x1[...].reshape(128, 128), spread).reshape(8, 16, 128)
    for i in range(8):
        E0[i, pl.ds(0, 16, stride=2), :] = wide[i]
        E0[i, pl.ds(1, 16, stride=2), :] = wide[i]
        up[2 * i] = x0[2 * i] + E0[i]
        up[2 * i + 1] = x0[2 * i + 1] + E0[i]


def finish_kernel(
    own_g, own_b, zl, zh, x01, out, G, B, W, GH, D2, VA, VB, DD, T, B3, W3, VA3, VB3, DD3, GH3, X3, E0
):
    gx, gy, gz = lax.axis_index("gx"), lax.axis_index("gy"), lax.axis_index("gz")
    lanes = iota((8, 128), 1)
    zeros = jnp.zeros((8, 128), F32)
    lane_in = jnp.where(lanes < 32, F32(1.0), jnp.where(lanes < 64, flag(gz < 7), zeros))
    lane_in = jnp.where(lanes >= 96, flag(gz > 0), lane_in)

    for p in (0, 17):
        B[0, p] = jnp.zeros((80, 128), F32)
    B[0, :, 0:8, :] = jnp.zeros((18, 8, 128), F32)
    B[0, :, 72:80, :] = jnp.zeros((18, 8, 128), F32)
    for j in range(32):
        row = 8 * (j % 8)
        for q in range(4):
            plane = 4 * (j // 8) + q
            for a in range(2):
                left, right = zl[j], zh[j]
                far = jnp.where(lanes < 48, turn(right, 32 - 16 * a - 32 * q), 0.0)
                far = jnp.where(lanes >= 112, turn(left, 112 - 16 * a - 32 * q), far)
                own = (own_g, own_b)[a][plane, row : row + 8, :]
                if a == 0:
                    G[plane, row : row + 8, :] = jnp.where(lanes < 32, own, far)
                else:
                    far = jnp.where(lanes < 32, own, far * lane_in)
                    B[0, plane + 1, 8 + row : 16 + row, :] = far
    low4, high4 = (lanes >= 108) & (lanes < 112), (lanes >= 48) & (lanes < 52)
    for d in range(3):
        row = pl.multiple_of(8 * jnp.clip(gy + d - 1, 0, 7), 8)
        left, right = zl[32 + d], zh[32 + d]
        for n in range(8):
            for q in range(4):
                plane = 4 * (n // 2) + q
                far = jnp.where(low4, turn(left, 108 - 32 * q - 4 * n), 0.0)
                far = jnp.where(high4, turn(right, 48 - 32 * q - 4 * n), far)
                if n % 2 == 0:
                    here = G[plane, pl.ds(row, 8), :]
                    G[plane, pl.ds(row, 8), :] = jnp.where(low4 | high4, far, here)
                else:
                    here = B[0, plane + 1, pl.ds(8 + row, 8), :]
                    far = jnp.where(low4 | high4, far * lane_in, here)
                    B[0, plane + 1, pl.ds(8 + row, 8), :] = far

    level = Level(64, BLOCK2, UNROLL2, 1, 0.25**2, smooth_low, SWEEPS, W, GH, DD, VA, VB, D2)
    level.clear([0, 17])
    level.prepare(0, 16, B, lambda c, i, r, n: G[i, pl.ds(r, n), :], 1)
    v = level.smooth(0, 16, 0)

    def put(j, c, r, n, total):
        T[0, j, pl.ds(r, n), :] = total

    level.residual_pairs(v, 0, 16, None, put)
    for j in range(8):
        T[1, j] = B[0, 1 + 2 * j, 8:72, :] + B[0, 2 + 2 * j, 8:72, :]
    both = T[:, :, pl.ds(0, 32, stride=2), :] + T[:, :, pl.ds(1, 32, stride=2), :]
    mat = matrix((128, 128), lambda a, c: a // 2 == c % 64, 0.125)
    coarse = product(both.reshape(512, 128), mat).reshape(2, 8, 32, 128)
    for p in (0, 9):
        B3[0, p] = jnp.zeros((48, 128), F32)
    B3[0, :, 0:8, :] = jnp.zeros((10, 8, 128), F32)
    B3[0, :, 40:48, :] = jnp.zeros((10, 8, 128), F32)
    B3[0, 1:9, 8:40, :] = coarse[1]

    base = Level(32, 32, 8, 1, 0.25**3, bottom_low, BOTTOM, W3, GH3, DD3, VA3, VB3, None)
    base.clear([0, 9])
    base.prepare(0, 8, B3, lambda c, i, r, n: coarse[0, i, r : r + n, :], 1)
    e3 = base.smooth(0, 8, 0)

    spread = matrix((128, 128), lambda a, c: a == c // 2, 1.0)
    for i in range(2):
        own = e3[0, 1 + 2 * gx + i, 8:40, :]
        X3[i, pl.ds(0, 32, stride=2), :] = own
        X3[i, pl.ds(1, 32, stride=2), :] = own
    row = pl.multiple_of(8 * gy, 8)
    up = product(X3[:, pl.ds(row, 8), :].reshape(16, 128), spread).reshape(2, 8, 128)
    e2 = [v[0, 1 + 4 * gx + i, pl.ds(8 + row, 8), :] + up[i // 2] for i in range(4)]
    spread = matrix((128, 128), lambda a, c: a == c // 4, 1.0)
    up = product(jnp.concatenate(e2, axis=0), spread).reshape(4, 8, 128)
    for i in range(4):
        for r in range(4):
            E0[i, pl.ds(r, 8, stride=4), :] = up[i]
        for r in range(4):
            out[4 * i + r] = x01[4 * i + r] + E0[i]


BLOCK0, UNROLL0, BLOCK2, UNROLL2 = 16, 12, 64, 16


def call(kernel, outs, scratch, limit, us=1):
    many = len(outs) > 1
    shapes = [jax.ShapeDtypeStruct(s, F32) for s in outs]
    return pl.pallas_call(
        kernel,
        out_shape=shapes if many else shapes[0],
        scratch_shapes=[pltpu.VMEM(s, F32) for s in scratch],
        compiler_params=pltpu.CompilerParams(vmem_limit_bytes=limit << 20),
        cost_estimate=pl.CostEstimate(
            flops=us * 1000000, bytes_accessed=us * 3600000, transcendentals=0
        ),
    )


def stage0a(*args):
    wide, tall = (32, 128), (48, 128)
    outs = [(16, 24, 128), (2, 8, 16, 128), (8, 16, 128), (4, 2, 24, 16, 128)]
    outs += [(6, 2, 16, 16, 128), (2, 16, 16, 128), (2, 16, 16, 128)]
    scratch = [(2, 24) + wide, (2, 26) + tall, (6, 2, 24) + wide, (2, 24) + wide, (2, 24) + wide]
    scratch += [(2, 24) + tall, (2, 24) + tall, (2, 24) + wide, (2, 8) + wide]
    return call(middle_kernel, outs, scratch, 20, 4)(*args)


def stage0b(*args):
    wide, tall = (48, 128), (64, 128)
    scratch = [(2, 24) + tall, (2, 26) + tall, (2, 7) + wide, (6, 2, 24) + wide]
    scratch += [(2, 24) + wide, (2, 24) + wide]
    scratch += [(2, 24) + tall, (2, 24) + tall, (2, 24) + wide, (2, 8) + wide]
    outs = [(16, 32, 128), (8, 24, 128), (8, 32, 128), (144, 128), (144, 128)]
    return call(ends_kernel, outs, scratch, 28)(*args)


def stage1(*args):
    wide, tall = (24, 128), (40, 128)
    scratch = [(8,) + wide, (1, 18) + tall, (6, 1, 16) + wide, (1, 16) + wide, (1, 16) + wide]
    scratch += [(1, 16) + tall, (1, 16) + tall, (1, 16) + wide, (2, 4) + wide]
    return call(level1_kernel, [(8, 16, 128), (2, 8, 128)], scratch, 16)(*args)


def stage2(*args):
    wide, tall, wide3, tall3 = (64, 128), (80, 128), (32, 128), (48, 128)
    scratch = [(16,) + wide, (1, 18) + tall, (6, 1, 16) + wide, (1, 16) + wide, (1, 16) + wide]
    scratch += [(1, 18) + tall, (1, 18) + tall, (1, 16) + wide, (2, 8) + wide]
    scratch += [(1, 10) + tall3, (6, 1, 8) + wide3, (1, 10) + tall3, (1, 10) + tall3]
    scratch += [(1, 8) + wide3, (1, 8) + wide3, (2, 64, 128), (4, 32, 128)]
    return call(finish_kernel, [(16, 32, 128)], scratch, 24)(*args)


def copy_all(moves, sems):
    copies = [pltpu.make_async_copy(a, c, sems.at[i]) for i, (a, c) in enumerate(moves)]
    for copy in copies:
        copy.start()
    for copy in copies:
        copy.wait()


def ends_load_kernel(g, b, high, low, sems):
    moves = [(g.at[12:16], high.at[0:4]), (b.at[11:16], high.at[4:9])]
    moves += [(g.at[0:4], low.at[0:4]), (b.at[0:5], low.at[4:9])]
    copy_all(moves, sems)


def load_kernel(g, b, gv, bv, sems):
    copy_all([(g, gv), (b, bv)], sems)


def load(kernel, shape, count, g, b):
    return pl.pallas_call(
        kernel,
        out_shape=[pltpu.VMEM(shape, F32)] * 2,
        in_specs=[pl.BlockSpec(memory_space=pltpu.HBM)] * 2,
        scratch_shapes=[pltpu.SemaphoreType.DMA((count,))],
        compiler_params=pltpu.CompilerParams(vmem_limit_bytes=60 << 20),
        cost_estimate=pl.CostEstimate(flops=0, bytes_accessed=3600000, transcendentals=0),
    )(g, b)


def per_device(g, b):
    high, low = load(ends_load_kernel, (9, 32, 128), 4, g, b)
    xl = ring(high, "gx", 1)
    xh = ring(low, "gx", -1)
    g, b = load(load_kernel, (16, 32, 128), 2, g, b)

    high, low = call(pack_kernel, [(7, 32, 128)] * 2, [], 16)(g, b, xl, xh)
    zl = ring(high, "gz", 1)
    zh = ring(low, "gz", -1)

    on, off = call(pack_y_kernel, [(Y_ROWS, 128)] * 2, [], 16)(g, b, xl, xh, zl, zh)
    off = swap(off, "gy", 1)
    on = swap(on, "gy", 0)
    middle = stage0a(g, b, xl, xh, zl, zh)
    x0, g1, b1, high, low = stage0b(g, b, xl, xh, on, off, zl, zh, *middle)

    xl = ring(high, "gx", 1)
    xh = ring(low, "gx", -1)
    x1, chunk = stage1(g1, b1, xl, xh)

    send = jnp.broadcast_to(chunk[None], (32, 2, 8, 128))
    slab = lax.all_to_all(send, ("gx", "gy"), 0, 0, tiled=False)
    high, low = call(pack_z_kernel, [(35, 8, 128)] * 2, [], 16)(slab)
    zl = ring(high, "gz", 1)
    zh = ring(low, "gz", -1)
    outs = [(16, 64, 128), (16, 64, 128), (16, 32, 128)]
    own_g, own_b, x01 = call(slab_kernel, outs, [(8, 32, 128)], 8, 2)(slab, x0, x1)
    return stage2(own_g, own_b, zl, zh, x01)


def solution(mesh):
    placed = (P("gx", "gy", "gz"), P("gx", "gy", "gz"))
    return jax.shard_map(
        per_device, mesh=mesh, in_specs=placed, out_specs=P("gx", "gy", "gz"), check_vma=False
    )
```

```python
import jax
import jax.numpy as jnp
from jax import lax
from jax.experimental import pallas as pl
from jax.experimental.pallas import tpu as pltpu
from jax.sharding import PartitionSpec as P

LEVELS = 3
SWEEPS = 4
BOTTOM = 8

cheby_top = 2.0
smooth_low = 0.25
bottom_low = 0.02

F32 = jnp.float32


def chebyshev_terms(lower_bound, sweeps):
    middle = (cheby_top + lower_bound) / 2.0
    radius = (cheby_top - lower_bound) / 2.0
    sigma_ratio = middle / radius
    rho_old = 1.0 / sigma_ratio
    term_list = []
    for sweep_index in range(1, sweeps):
        rho_new = 1.0 / (2.0 * sigma_ratio - rho_old)
        term_list.append((rho_new * rho_old, 2.0 * rho_new / radius))
        rho_old = rho_new
    return (1.0 / middle, term_list)


def ring(values, axis, step):
    count = lax.axis_size(axis)
    return lax.ppermute(values, axis, [(i, (i + step) % count) for i in range(count)])


def swap(values, axis, first):
    count = lax.axis_size(axis)
    pairs = [(i % count, (i + 1) % count) for i in range(first, first + count, 2)]
    return lax.ppermute(values, axis, pairs + [(j, i) for i, j in pairs])


def iota(shape, axis):
    return lax.broadcasted_iota(jnp.int32, shape, axis)


def matrix(shape, hit, value):
    return jnp.where(hit(iota(shape, 0), iota(shape, 1)), F32(value), F32(0.0))


def product(left, right):
    parts, rest = [], left
    for _ in range(3):
        part = rest.astype(jnp.bfloat16)
        parts.append(part)
        rest = rest - part.astype(F32)
    right = right.astype(jnp.bfloat16)
    high, middle, low = (jnp.dot(p, right, preferred_element_type=F32) for p in parts)
    return high + (middle + low)


def turn(v, shift):
    shift = shift % 128
    return pltpu.roll(v, shift, 1) if shift else v


def beside(cols):
    low = [pltpu.roll(c, 1, 1) for c in cols]
    high = [pltpu.roll(c, 127, 1) for c in cols]
    if len(cols) == 2:
        lanes = iota(cols[0].shape, 1)
        first, last = lanes == 0, lanes == 127
        low = [jnp.where(first, low[1], low[0]), jnp.where(first, low[0], low[1])]
        high = [jnp.where(last, high[1], high[0]), jnp.where(last, high[0], high[1])]
    return low, high


def around(field, first, planes, row, count):
    cols = range(field.shape[0])
    here = [
        [field[c, first + p, pl.ds(8 + row, count), :] for c in cols] for p in range(-1, planes + 1)
    ]
    out = []
    for p in range(planes):
        low, high = beside(here[p + 1])
        out.append(
            [
                (
                    here[p + 1][c],
                    here[p][c],
                    here[p + 2][c],
                    field[c, first + p, pl.ds(7 + row, count), :],
                    field[c, first + p, pl.ds(9 + row, count), :],
                    low[c],
                    high[c],
                )
                for c in cols
            ]
        )
    return out


def sweep_planes(low, high, body, unroll):
    steps = (high - low) // unroll
    if steps > 1:

        def several(j, _):
            body(low + j * unroll, unroll)
            return 0

        lax.fori_loop(0, steps, several, 0)
        low = low + steps * unroll
    if high > low:
        body(low, high - low)


class Level:
    def __init__(self, rows, block, unroll, at, scale, low, sweeps, w, gh, d, va, vb, double):
        self.rows, self.block, self.unroll, self.at, self.scale = rows, block, unroll, at, scale
        self.initial, self.terms = chebyshev_terms(low, sweeps)
        self.w, self.gh, self.d, self.va, self.vb, self.double = w, gh, d, va, vb, double
        self.spans = [(0, rows)]

    def blocks(self, spans=None):
        return [at for span in spans or self.spans for at in self.cut(*span)]

    def cut(self, first, last):
        return [(r, min(self.block, last - r)) for r in range(first, last, self.block)]

    def clear(self, planes):
        for ref in (self.va, self.vb):
            shape = ref.shape
            edge = jnp.zeros((shape[0], shape[1], 8, 128), F32)
            ref[:, :, 0:8, :] = edge
            ref[:, :, 8 + self.rows : 16 + self.rows, :] = edge
            for p in planes:
                ref[:, p] = jnp.zeros((shape[0],) + shape[2:], F32)

    def prepare(self, low, high, b, g, shift):
        def body(first, planes):
            for r, n in self.blocks():
                for p, fields in enumerate(around(b, first + shift, planes, r, n)):
                    i = first + p
                    for c, (bc, *near) in enumerate(fields):
                        double = 6.0 * bc + (
                            (near[0] + near[1]) + (near[2] + near[3]) + (near[4] + near[5])
                        )
                        inverse = jnp.where(bc > 0.0, 1.0 / double, 0.0)
                        for f in range(6):
                            self.w[f, c, i, pl.ds(r, n), :] = (bc + near[f]) * inverse
                        gh = g(c, i, r, n) * ((2.0 / self.scale) * inverse)
                        self.gh[c, i, pl.ds(r, n), :] = gh
                        self.va[c, i + self.at, pl.ds(8 + r, n), :] = gh * self.initial
                        if self.double is not None:
                            self.double[c, i, pl.ds(r, n), :] = (0.5 * self.scale) * double

        sweep_planes(low, high, body, self.unroll)

    def scaled_residual(self, v, first, planes, r, n):
        out = []
        for p, fields in enumerate(around(v, first + self.at, planes, r, n)):
            out.append([])
            for c, (vc, *near) in enumerate(fields):
                z = self.gh[c, first + p, pl.ds(r, n), :] - vc
                for f in range(6):
                    z = z + self.w[f, c, first + p, pl.ds(r, n), :] * near[f]
                out[-1].append((vc, z))
        return out

    def smooth(self, low, high, shrink, meet=None):
        src, dst = self.va, self.vb
        for k, (carry, push) in enumerate(self.terms):
            if meet is not None:
                meet(k, src)
            low, high = low + shrink, high - shrink

            def body(first, planes, src=src, dst=dst, k=k, carry=carry, push=push):
                for r, n in self.blocks():
                    for p, got in enumerate(self.scaled_residual(src, first, planes, r, n)):
                        i = first + p
                        for c, (vc, z) in enumerate(got):
                            old = vc if k == 0 else self.d[c, i, pl.ds(r, n), :]
                            step = carry * old + push * z
                            if k < len(self.terms) - 1:
                                self.d[c, i, pl.ds(r, n), :] = step
                            dst[c, i + self.at, pl.ds(8 + r, n), :] = vc + step

            sweep_planes(low, high, body, self.unroll)
            src, dst = dst, src
        if meet is not None:
            meet(len(self.terms), src)
        return src

    def residual_pairs(self, v, low, high, spans, put):
        def body(j, pairs):
            i = low + 2 * j
            for r, n in self.blocks(spans):
                got = self.scaled_residual(v, i, 2 * pairs, r, n)
                for p in range(pairs):
                    for c in range(len(got[0])):
                        total = None
                        for q in (2 * p, 2 * p + 1):
                            now = self.double[c, i + q, pl.ds(r, n), :] * got[q][c][1]
                            total = now if total is None else total + now
                        put(j + p, c, r, n, total)

        sweep_planes(0, (high - low) // 2, body, max(1, self.unroll // 2))


def flag(condition):
    return jnp.where(condition, F32(1.0), F32(0.0))


def plane_of(p, g, b, xl, xh):
    if p < 4:
        return xl[p]
    if p < 20:
        return g[p - 4]
    if p < 24:
        return xh[p - 20]
    if p < 29:
        return xl[p - 20]
    if p < 45:
        return b[p - 29]
    return xh[p - 41]


def pack_planes(planes, high, low, plane, start):
    slot = iota((32, 128), 1) // 16
    for k in range(7):
        to_high, to_low = start(k)
        for s in range(8):
            if 8 * k + s in planes:
                here = plane(8 * k + s)
                to_high = jnp.where(slot == s, turn(here, 16 * (s + 1)), to_high)
                to_low = jnp.where(slot == s, turn(here, 16 * s), to_low)
        high[k] = to_high
        low[k] = to_low


OWN = list(range(4, 20)) + list(range(29, 45))


def pack_own_kernel(g, b, high, low):
    blank = jnp.zeros((32, 128), F32)
    pack_planes(OWN, high, low, lambda p: plane_of(p, g, b, None, None), lambda k: (blank, blank))


def pack_kernel(xl, xh, own_high, own_low, high, low):
    halo = [p for p in range(50) if p not in OWN]
    start = lambda k: (own_high[k], own_low[k])
    pack_planes(halo, high, low, lambda p: plane_of(p, None, None, xl, xh), start)


INNER = 64
OUTER = list(range(1, 23)) + list(range(25, 49)) + list(range(50, 64))
LAST = list(range(29, 45))
OUTER_AT = 8 * INNER
LAST_AT = OUTER_AT + 4 * len(OUTER)
Y_ROWS = LAST_AT + len(LAST)


def pack_y_kernel(g, b, xl, xh, zl, zh, on, off):
    even = lax.rem(lax.axis_index("gy"), 2) == 0

    def put(at, count, upper, lower):
        on[at : at + count, :] = jnp.where(even, upper, lower)
        off[at : at + count, :] = jnp.where(even, lower, upper)

    def plane(p):
        if p < 50:
            return plane_of(p, g, b, xl, xh)
        return zl[p - 50] if p < 57 else zh[p - 57]

    for p in range(INNER):
        here = plane(p)
        put(8 * p, 8, here[24:32], here[0:8])
    for i, p in enumerate(OUTER):
        here, at = plane(p), OUTER_AT + 4 * i
        put(at, 4, here[20:24], here[8:12])
    for i, p in enumerate(LAST):
        here, at = plane(p), LAST_AT + i
        put(at, 1, here[19:20], here[12:13])


def side_of(p, x_low, x_high):
    return x_low if p < 29 else x_high if p >= 45 else None


def times(factor, *values):
    return values if factor is None else tuple(factor * v for v in values)


def unpack(low, high, p, lanes):
    s = p % 8
    from_high = pltpu.roll(high, 128 - 16 * s, 1) if s else high
    from_low = pltpu.roll(low, 112 - 16 * s, 1) if s < 7 else low
    return jnp.where(lanes < 16, from_high, from_low)


def halved(pairs, count):
    near_mat = matrix((128, 128), lambda a, c: a // 2 == c, 0.125)
    far_mat = matrix((128, 128), lambda a, c: a // 2 + 64 == c, 0.125)
    sums = []
    for c in range(2):
        even = pairs[c, :, pl.ds(0, count, stride=2), :]
        odd = pairs[c, :, pl.ds(1, count, stride=2), :]
        sums.append((even + odd).reshape(8 * count, 128))
    total = product(sums[0], near_mat) + product(sums[1], far_mat)
    return total.reshape(8, count, 128)


def pack_x(out, planes):
    lanes = iota((24, 128), 1)
    for m in range(5):
        here = planes[2 * m]
        if m < 4:
            here = jnp.where(lanes < 64, here, pltpu.roll(planes[2 * m + 1], 64, 1))
        out[24 * m : 24 * m + 24, :] = here
    ends = jnp.zeros((24, 128), F32)
    for n in range(8):
        near = jnp.where(lanes % 16 < 8, turn(planes[n], 16 * n + 64), turn(planes[n], 16 * n + 16))
        ends = jnp.where(lanes // 16 == n, near, ends)
    out[120:144, :] = ends


def unpack_x(side, n):
    lanes = iota((24, 128), 1)
    at = 24 * (n // 2)
    own = turn(side[at : at + 24, :], 64 * (n % 2))
    far = jnp.zeros((24, 128), F32)
    if n < 8:
        ends = side[120:144, :]
        far = jnp.where(lanes < 72, turn(ends, 64 - 16 * n), far)
        far = jnp.where(lanes >= 120, turn(ends, 112 - 16 * n), far)
    return jnp.where(lanes < 64, own, far)


def middle_kernel(g, b, xl, xh, zl, zh, x4, rm, b1, VE, WE, GE, DE, G, B, W, GH, D2, VA, VB, DD, T):
    gx, gz = lax.axis_index("gx"), lax.axis_index("gz")
    lanes = iota((32, 128), 1)
    lane_in = jnp.where(lanes < 16, flag(gz < 7), jnp.where(lanes >= 112, flag(gz > 0), F32(0.0)))
    x_low, x_high = flag(gx > 0), flag(gx < 3)
    spare = jnp.zeros((2, 26, 8, 128), F32)
    B[:, :, 0:8, :] = spare
    B[:, :, 40:48, :] = spare
    for p in range(50):
        far = unpack(zl[p // 8], zh[p // 8], p, lanes)
        own = plane_of(p, g, b, xl, xh)
        if p < 24:
            G[0, p] = own
            G[1, p] = far
        else:
            own, far = times(side_of(p, x_low, x_high), own, far * lane_in)
            B[0, p - 24, 8:40, :] = own
            B[1, p - 24, 8:40, :] = far

    level = Level(32, BLOCK0, UNROLL0, 0, 1.0, smooth_low, SWEEPS, W, GH, DD, VA, VB, D2)
    level.clear([])
    level.prepare(0, 24, B, lambda c, i, r, n: G[c, i, pl.ds(r, n), :], 1)

    def keep(k, v):
        VE[k, :, :, 0:8, :] = v[:, :, 12:20, :]
        VE[k, :, :, 8:16, :] = v[:, :, 28:36, :]

    v = level.smooth(0, 24, 1, keep)
    x4[...] = v[0, 4:20, 12:36, :]

    def put(j, c, r, n, total):
        rm[c, j, pl.ds(r - 8, n), :] = total

    level.residual_pairs(v, 4, 20, [(8, 24)], put)
    for to, ref in ((WE, W), (GE, GH), (DE, D2)):
        to[..., 0:8, :] = ref[..., 4:20, 4:12, :]
        to[..., 8:16, :] = ref[..., 4:20, 20:28, :]
    for c in range(2):
        for j in range(8):
            T[c, j] = B[c, 5 + 2 * j, 8:40, :] + B[c, 6 + 2 * j, 8:40, :]
    b1[...] = halved(T, 16)


class Either:
    def __init__(self, condition, first, second):
        self.condition, self.first, self.second = condition, first, second

    def __getitem__(self, at):
        return jnp.where(self.condition, self.first[at], self.second[at])


def ends_kernel(
    g, b, xl, xh, on, off, zl, zh, x4, rm, bm, VE, WE, GE, DE, x0, g1, b1, high, low,
    G, B, Z, W, GH, D2, VA, VB, DD, T,
):
    gx, gy, gz = lax.axis_index("gx"), lax.axis_index("gy"), lax.axis_index("gz")
    even = lax.rem(gy, 2) == 0
    yl, yh = Either(even, off, on), Either(even, on, off)
    lanes = iota((48, 128), 1)
    rows = iota((48, 128), 0)
    y_low, y_high, x_low, x_high = flag(gy > 0), flag(gy < 7), flag(gx > 0), flag(gx < 3)
    lane_in = jnp.where(lanes < 16, flag(gz < 7), jnp.where(lanes >= 112, flag(gz > 0), F32(0.0)))
    lane_in = jnp.where(rows < 12, y_low, jnp.where(rows < 36, F32(1.0), y_high)) * lane_in
    blank4, blank8 = jnp.zeros((4, 128), F32), jnp.zeros((8, 128), F32)
    order = {p: i for i, p in enumerate(OUTER)}

    def outer(side, p):
        if p not in order:
            return blank4
        at = OUTER_AT + 4 * order[p]
        return side[at : at + 4, :]

    for side, source in ((0, zl), (1, zh)):
        for k in range(7):
            p = 50 + 7 * side + k
            Z[side, k, 0:4, :] = outer(yl, p)
            Z[side, k, 4:12, :] = yl[8 * p : 8 * p + 8, :]
            Z[side, k, 12:20, :] = source[k, 0:8]
            Z[side, k, 20:28, :] = blank8
            Z[side, k, 28:36, :] = source[k, 24:32]
            Z[side, k, 36:44, :] = yh[8 * p : 8 * p + 8, :]
            Z[side, k, 44:48, :] = outer(yh, p)
    for p in range(50):
        far = unpack(Z[0, p // 8], Z[1, p // 8], p, lanes)
        own = plane_of(p, g, b, xl, xh)
        first, last = own[0:8], own[24:32]
        below, above = yl[8 * p : 8 * p + 8, :], yh[8 * p : 8 * p + 8, :]
        below4, above4 = outer(yl, p), outer(yh, p)
        field, q = (G, p) if p < 24 else (B, p - 24)
        if p >= 24:
            side = side_of(p, x_low, x_high)
            first, last, far = times(side, first, last, far * lane_in)
            below, below4 = times(side, below * y_low, below4 * y_low)
            above, above4 = times(side, above * y_high, above4 * y_high)
            for c in range(2):
                field[c, q, 0:8, :] = blank8
                field[c, q, 56:64, :] = blank8
            if p in LAST:
                at = LAST_AT + LAST.index(p)
                field[0, q, 7:8, :] = yl[at : at + 1, :] * y_low
                field[0, q, 56:57, :] = yh[at : at + 1, :] * y_high
        field[0, q, 8:12, :] = below4
        field[0, q, 12:20, :] = below
        field[0, q, 20:28, :] = first
        field[0, q, 36:44, :] = last
        field[0, q, 44:52, :] = above
        field[0, q, 52:56, :] = above4
        field[1, q, 8:56, :] = far

    level = Level(48, BLOCK0, UNROLL0, 0, 1.0, smooth_low, SWEEPS, W, GH, DD, VA, VB, D2)
    level.spans = [(0, 16), (32, 48)]
    level.clear([])
    level.prepare(0, 24, B, lambda c, i, r, n: G[c, i, pl.ds(8 + r, n), :], 1)
    for to, ref in ((W, WE), (GH, GE), (D2, DE)):
        to[..., 4:20, 16:32, :] = ref[...]

    def join(k, v):
        v[:, :, 24:40, :] = VE[k]

    v = level.smooth(0, 24, 1, join)
    x0[:, 0:4, :] = v[0, 4:20, 20:24, :]
    x0[:, 4:28, :] = x4[...]
    x0[:, 28:32, :] = v[0, 4:20, 40:44, :]

    def put(j, c, r, n, total):
        T[c, j, pl.ds(r - 4 if r < 24 else r + 4, n), :] = total

    level.residual_pairs(v, 4, 20, [(4, 20), (28, 44)], put)
    T[:, :, 16:32, :] = rm[...]
    g1[...] = halved(T, 24)
    for c in range(2):
        for j in range(8):
            p, q = 5 + 2 * j, 6 + 2 * j
            T[c, j, 0:4, :] = blank4
            T[c, j, 4:16, :] = B[c, p, 8:20, :] + B[c, q, 8:20, :]
            T[c, j, 16:28, :] = B[c, p, 44:56, :] + B[c, q, 44:56, :]
            T[c, j, 28:32, :] = blank4
    both = halved(T, 16)
    b1[:, 0:8, :] = both[:, 0:8]
    b1[:, 8:24, :] = bm[...]
    b1[:, 24:32, :] = both[:, 8:16]
    pack_x(high, [g1[q] for q in range(4, 8)] + [b1[q, 4:28, :] for q in (4, 5, 6, 7, 3)])
    pack_x(low, [g1[q] for q in range(4)] + [b1[q, 4:28, :] for q in range(5)])


def level1_kernel(g, b, xl, xh, x1, chunk, G, B, W, GH, D2, VA, VB, DD, T):
    gx = lax.axis_index("gx")
    blank = jnp.zeros((8, 128), F32)
    for side, inside, at, planes in ((xl, gx > 0, 0, (1, 2, 3, 4, 0)), (xh, gx < 3, 4, range(13, 18))):
        for n in range(4):
            G[at + n] = unpack_x(side, n)
        for n, q in enumerate(planes):
            B[0, q, 0:8, :] = blank
            B[0, q, 8:32, :] = unpack_x(side, 4 + n) * flag(inside)
            B[0, q, 32:40, :] = blank
    for q in range(8):
        B[0, 5 + q, 4:36, :] = b[q]

    def source(c, i, r, n):
        if i < 4:
            return G[i, r : r + n, :]
        if i < 12:
            return g[i - 4, r : r + n, :]
        return G[i - 8, r : r + n, :]

    level = Level(24, 24, 16, 0, 0.25, smooth_low, SWEEPS, W, GH, DD, VA, VB, D2)
    level.clear([])
    level.prepare(0, 16, B, source, 1)
    v = level.smooth(0, 16, 1)
    x1[...] = v[0, 4:12, 12:28, :]

    def put(j, c, r, n, total):
        T[0, j, pl.ds(r, n), :] = total

    level.residual_pairs(v, 4, 12, None, put)
    for q in range(4):
        T[1, q] = B[0, 5 + 2 * q, 8:32, :] + B[0, 6 + 2 * q, 8:32, :]
    both = T[:, :, pl.ds(4, 8, stride=2), :] + T[:, :, pl.ds(5, 8, stride=2), :]
    mat = matrix((128, 128), lambda a, c: (a < 64) & (a // 2 == c), 0.125)
    total = product(both.reshape(64, 128), mat).reshape(2, 4, 8, 128)
    for a in range(2):
        out = total[a, 0]
        for q in range(1, 4):
            out = out + pltpu.roll(total[a, q], 32 * q, 1)
        chunk[a] = out


def pack_z_kernel(slab, high, low):
    lanes = iota((8, 128), 1)
    first = lanes % 32 < 16
    for j in range(32):
        g, b = slab[j, 0], slab[j, 1]
        high[j] = jnp.where(first, turn(g, -16), b)
        low[j] = jnp.where(first, g, turn(b, 16))
    gy = lax.axis_index("gy")
    for d in range(3):
        by = jnp.clip(gy + d - 1, 0, 7)
        to_high = jnp.zeros((8, 128), F32)
        to_low = jnp.zeros((8, 128), F32)
        for n in range(8):
            here = slab[8 * (n // 2) + by, n % 2]
            mine = lanes % 32 // 4 == n
            to_high = jnp.where(mine, turn(here, 4 * n - 12), to_high)
            to_low = jnp.where(mine, turn(here, 4 * n - 16), to_low)
        high[32 + d] = to_high
        low[32 + d] = to_low


def slab_kernel(slab, x0, x1, g, b, up, E0):
    lanes = iota((8, 128), 1)
    for j in range(32):
        row = 8 * (j % 8)
        for q in range(4):
            for a, field in ((0, g), (1, b)):
                own = jnp.where(lanes < 32, turn(slab[j, a], -32 * q), 0.0)
                field[4 * (j // 8) + q, row : row + 8, :] = own
    spread = matrix((128, 128), lambda a, c: a == c // 2, 1.0)
    wide = product(x1[...].reshape(128, 128), spread).reshape(8, 16, 128)
    for i in range(8):
        E0[i, pl.ds(0, 16, stride=2), :] = wide[i]
        E0[i, pl.ds(1, 16, stride=2), :] = wide[i]
        up[2 * i] = x0[2 * i] + E0[i]
        up[2 * i + 1] = x0[2 * i + 1] + E0[i]


def finish_kernel(
    own_g, own_b, zl, zh, x01, out, G, B, W, GH, D2, VA, VB, DD, T, B3, W3, VA3, VB3, DD3, GH3, X3, E0
):
    gx, gy, gz = lax.axis_index("gx"), lax.axis_index("gy"), lax.axis_index("gz")
    lanes = iota((8, 128), 1)
    zeros = jnp.zeros((8, 128), F32)
    lane_in = jnp.where(lanes < 32, F32(1.0), jnp.where(lanes < 64, flag(gz < 7), zeros))
    lane_in = jnp.where(lanes >= 96, flag(gz > 0), lane_in)

    for p in (0, 17):
        B[0, p] = jnp.zeros((80, 128), F32)
    B[0, :, 0:8, :] = jnp.zeros((18, 8, 128), F32)
    B[0, :, 72:80, :] = jnp.zeros((18, 8, 128), F32)
    for j in range(32):
        row = 8 * (j % 8)
        for q in range(4):
            plane = 4 * (j // 8) + q
            for a in range(2):
                left, right = zl[j], zh[j]
                far = jnp.where(lanes < 48, turn(right, 32 - 16 * a - 32 * q), 0.0)
                far = jnp.where(lanes >= 112, turn(left, 112 - 16 * a - 32 * q), far)
                own = (own_g, own_b)[a][plane, row : row + 8, :]
                if a == 0:
                    G[plane, row : row + 8, :] = jnp.where(lanes < 32, own, far)
                else:
                    far = jnp.where(lanes < 32, own, far * lane_in)
                    B[0, plane + 1, 8 + row : 16 + row, :] = far
    low4, high4 = (lanes >= 108) & (lanes < 112), (lanes >= 48) & (lanes < 52)
    for d in range(3):
        row = pl.multiple_of(8 * jnp.clip(gy + d - 1, 0, 7), 8)
        left, right = zl[32 + d], zh[32 + d]
        for n in range(8):
            for q in range(4):
                plane = 4 * (n // 2) + q
                far = jnp.where(low4, turn(left, 108 - 32 * q - 4 * n), 0.0)
                far = jnp.where(high4, turn(right, 48 - 32 * q - 4 * n), far)
                if n % 2 == 0:
                    here = G[plane, pl.ds(row, 8), :]
                    G[plane, pl.ds(row, 8), :] = jnp.where(low4 | high4, far, here)
                else:
                    here = B[0, plane + 1, pl.ds(8 + row, 8), :]
                    far = jnp.where(low4 | high4, far * lane_in, here)
                    B[0, plane + 1, pl.ds(8 + row, 8), :] = far

    level = Level(64, BLOCK2, UNROLL2, 1, 0.25**2, smooth_low, SWEEPS, W, GH, DD, VA, VB, D2)
    level.clear([0, 17])
    level.prepare(0, 16, B, lambda c, i, r, n: G[i, pl.ds(r, n), :], 1)
    v = level.smooth(0, 16, 0)

    def put(j, c, r, n, total):
        T[0, j, pl.ds(r, n), :] = total

    level.residual_pairs(v, 0, 16, None, put)
    for j in range(8):
        T[1, j] = B[0, 1 + 2 * j, 8:72, :] + B[0, 2 + 2 * j, 8:72, :]
    both = T[:, :, pl.ds(0, 32, stride=2), :] + T[:, :, pl.ds(1, 32, stride=2), :]
    mat = matrix((128, 128), lambda a, c: a // 2 == c % 64, 0.125)
    coarse = product(both.reshape(512, 128), mat).reshape(2, 8, 32, 128)
    for p in (0, 9):
        B3[0, p] = jnp.zeros((48, 128), F32)
    B3[0, :, 0:8, :] = jnp.zeros((10, 8, 128), F32)
    B3[0, :, 40:48, :] = jnp.zeros((10, 8, 128), F32)
    B3[0, 1:9, 8:40, :] = coarse[1]

    base = Level(32, 32, 8, 1, 0.25**3, bottom_low, BOTTOM, W3, GH3, DD3, VA3, VB3, None)
    base.clear([0, 9])
    base.prepare(0, 8, B3, lambda c, i, r, n: coarse[0, i, r : r + n, :], 1)
    e3 = base.smooth(0, 8, 0)

    spread = matrix((128, 128), lambda a, c: a == c // 2, 1.0)
    for i in range(2):
        own = e3[0, 1 + 2 * gx + i, 8:40, :]
        X3[i, pl.ds(0, 32, stride=2), :] = own
        X3[i, pl.ds(1, 32, stride=2), :] = own
    row = pl.multiple_of(8 * gy, 8)
    up = product(X3[:, pl.ds(row, 8), :].reshape(16, 128), spread).reshape(2, 8, 128)
    e2 = [v[0, 1 + 4 * gx + i, pl.ds(8 + row, 8), :] + up[i // 2] for i in range(4)]
    spread = matrix((128, 128), lambda a, c: a == c // 4, 1.0)
    up = product(jnp.concatenate(e2, axis=0), spread).reshape(4, 8, 128)
    for i in range(4):
        for r in range(4):
            E0[i, pl.ds(r, 8, stride=4), :] = up[i]
        for r in range(4):
            out[4 * i + r] = x01[4 * i + r] + E0[i]


BLOCK0, UNROLL0, BLOCK2, UNROLL2 = 16, 12, 64, 16


def call(kernel, outs, scratch, limit, us=1):
    many = len(outs) > 1
    shapes = [jax.ShapeDtypeStruct(s, F32) for s in outs]
    return pl.pallas_call(
        kernel,
        out_shape=shapes if many else shapes[0],
        scratch_shapes=[pltpu.VMEM(s, F32) for s in scratch],
        compiler_params=pltpu.CompilerParams(vmem_limit_bytes=limit << 20),
        cost_estimate=pl.CostEstimate(
            flops=us * 1000000, bytes_accessed=us * 3600000, transcendentals=0
        ),
    )


def stage0a(*args):
    wide, tall = (32, 128), (48, 128)
    outs = [(16, 24, 128), (2, 8, 16, 128), (8, 16, 128), (4, 2, 24, 16, 128)]
    outs += [(6, 2, 16, 16, 128), (2, 16, 16, 128), (2, 16, 16, 128)]
    scratch = [(2, 24) + wide, (2, 26) + tall, (6, 2, 24) + wide, (2, 24) + wide, (2, 24) + wide]
    scratch += [(2, 24) + tall, (2, 24) + tall, (2, 24) + wide, (2, 8) + wide]
    return call(middle_kernel, outs, scratch, 20, 4)(*args)


def stage0b(*args):
    wide, tall = (48, 128), (64, 128)
    scratch = [(2, 24) + tall, (2, 26) + tall, (2, 7) + wide, (6, 2, 24) + wide]
    scratch += [(2, 24) + wide, (2, 24) + wide]
    scratch += [(2, 24) + tall, (2, 24) + tall, (2, 24) + wide, (2, 8) + wide]
    outs = [(16, 32, 128), (8, 24, 128), (8, 32, 128), (144, 128), (144, 128)]
    return call(ends_kernel, outs, scratch, 28)(*args)


def stage1(*args):
    wide, tall = (24, 128), (40, 128)
    scratch = [(8,) + wide, (1, 18) + tall, (6, 1, 16) + wide, (1, 16) + wide, (1, 16) + wide]
    scratch += [(1, 16) + tall, (1, 16) + tall, (1, 16) + wide, (2, 4) + wide]
    return call(level1_kernel, [(8, 16, 128), (2, 8, 128)], scratch, 16)(*args)


def stage2(*args):
    wide, tall, wide3, tall3 = (64, 128), (80, 128), (32, 128), (48, 128)
    scratch = [(16,) + wide, (1, 18) + tall, (6, 1, 16) + wide, (1, 16) + wide, (1, 16) + wide]
    scratch += [(1, 18) + tall, (1, 18) + tall, (1, 16) + wide, (2, 8) + wide]
    scratch += [(1, 10) + tall3, (6, 1, 8) + wide3, (1, 10) + tall3, (1, 10) + tall3]
    scratch += [(1, 8) + wide3, (1, 8) + wide3, (2, 64, 128), (4, 32, 128)]
    return call(finish_kernel, [(16, 32, 128)], scratch, 24)(*args)


def copy_all(moves, sems):
    copies = [pltpu.make_async_copy(a, c, sems.at[i]) for i, (a, c) in enumerate(moves)]
    for copy in copies:
        copy.start()
    for copy in copies:
        copy.wait()


def ends_load_kernel(g, b, high, low, sems):
    moves = [(g.at[12:16], high.at[0:4]), (b.at[11:16], high.at[4:9])]
    moves += [(g.at[0:4], low.at[0:4]), (b.at[0:5], low.at[4:9])]
    copy_all(moves, sems)


def load_kernel(g, b, gv, bv, sems):
    copy_all([(g, gv), (b, bv)], sems)


def load(kernel, shape, count, g, b):
    return pl.pallas_call(
        kernel,
        out_shape=[pltpu.VMEM(shape, F32)] * 2,
        in_specs=[pl.BlockSpec(memory_space=pltpu.HBM)] * 2,
        scratch_shapes=[pltpu.SemaphoreType.DMA((count,))],
        compiler_params=pltpu.CompilerParams(vmem_limit_bytes=60 << 20),
        cost_estimate=pl.CostEstimate(flops=0, bytes_accessed=3600000, transcendentals=0),
    )(g, b)


def per_device(g, b):
    high, low = load(ends_load_kernel, (9, 32, 128), 4, g, b)
    xl = ring(high, "gx", 1)
    xh = ring(low, "gx", -1)
    g, b = load(load_kernel, (16, 32, 128), 2, g, b)

    own = call(pack_own_kernel, [(7, 32, 128)] * 2, [], 8)(g, b)
    high, low = call(pack_kernel, [(7, 32, 128)] * 2, [], 8)(xl, xh, *own)
    zl = ring(high, "gz", 1)
    zh = ring(low, "gz", -1)

    on, off = call(pack_y_kernel, [(Y_ROWS, 128)] * 2, [], 16)(g, b, xl, xh, zl, zh)
    off = swap(off, "gy", 1)
    on = swap(on, "gy", 0)
    middle = stage0a(g, b, xl, xh, zl, zh)
    x0, g1, b1, high, low = stage0b(g, b, xl, xh, on, off, zl, zh, *middle)

    xl = ring(high, "gx", 1)
    xh = ring(low, "gx", -1)
    x1, chunk = stage1(g1, b1, xl, xh)

    send = jnp.broadcast_to(chunk[None], (32, 2, 8, 128))
    slab = lax.all_to_all(send, ("gx", "gy"), 0, 0, tiled=False)
    high, low = call(pack_z_kernel, [(35, 8, 128)] * 2, [], 16)(slab)
    zl = ring(high, "gz", 1)
    zh = ring(low, "gz", -1)
    outs = [(16, 64, 128), (16, 64, 128), (16, 32, 128)]
    own_g, own_b, x01 = call(slab_kernel, outs, [(8, 32, 128)], 8, 2)(slab, x0, x1)
    return stage2(own_g, own_b, zl, zh, x01)


def solution(mesh):
    placed = (P("gx", "gy", "gz"), P("gx", "gy", "gz"))
    return jax.shard_map(
        per_device, mesh=mesh, in_specs=placed, out_specs=P("gx", "gy", "gz"), check_vma=False
    )
```
